32 devices in a mesh: seq: 8 (over z, x), head: 4 (over y, core).
Axes of the slice: x: 2, y: 2, z: 4, core: 2. Of those that a mesh axis runs over, the one named last changes fastest.
Arguments:
- frames: bfloat16 [2048, 1024], P('seq'), may hold values from -6 to 6
- norm_gain: float32 [1024], replicated, may hold values from 0.5 to 1.5
- w_qkv: bfloat16 [3, 1024, 1024], P(None, None, 'head'), may hold values from -2 to 2
- w_out: bfloat16 [1024, 1024], P('head'), may hold values from -0.1875 to 0.1875
- w_proj: bfloat16 [1024, 512], replicated, may hold values from -0.1875 to 0.1875
- text_table: bfloat16 [32768, 512], P(('seq', 'head')), may hold values from -6 to 6
- token_ids: int32 [64, 16], replicated, may hold values from 0 to 32767
- span_bounds: int32 [64, 2], P(('seq', 'head')), may hold values from 0 to 2048, as said below
- contrast_divisor: float32 [1], replicated, may hold values from 10 to 30
Outputs:
- interval_embedding_derivative: float32 [64, 512], P(('seq', 'head'))
- loss_terms: float32 [64], P(('seq', 'head'))
The draws below stay inside these ranges and needn't reach their ends.
Inputs may be any that keep to these rules, and one draw needn't show every extreme that they name: `span_bounds`: both entries are multiples of 128 and the first is smaller than the second.
All inputs are finite; a program needn't handle non-finite values.
Results may differ from the reference program's by a relative error of at most 0.006.
Values may be sent and summed in bfloat16 or wider, within the bound.
No kernel may reach another device: no remote copies, remote signals or barrier semaphores. Data moves between devices by JAX's collectives and lax.ppermute only.
A program may use at most 64 MiB of HBM per device.

```python
import math
import jax
import jax.numpy as jnp
import numpy as np
from jax import lax

D = 1024
HEADS = 16
HDIM = 64
E = 512
VOCAB = 32768
CL = 16
BLK = 128
FR_DEV = 256
FRAMES = 2048
NBLK = 16
NCAP = 64


def draw_span_bounds(key, part):
    first_key, second_key, third_key = jax.random.split(jax.random.fold_in(key, 7), 3)
    starts = jax.random.randint(first_key, (NCAP,), 0, NBLK, dtype=jnp.int32)
    largest = (8 * (FR_DEV // BLK)).bit_length() - 1
    expo = jax.random.randint(second_key, (NCAP,), 0, largest + 1, dtype=jnp.int32)
    longest = jnp.left_shift(jnp.ones_like(expo), expo)
    lengths = 1 + jax.random.randint(third_key, (NCAP,), 0, longest, dtype=jnp.int32)
    starts = starts.at[0].set(0)
    ends = jnp.minimum(starts + lengths, NBLK)
    ends = ends.at[NCAP - 1].set(NBLK)
    return (jnp.stack([starts, ends], axis=1) * BLK).astype(jnp.int32)


def draw_w_qkv(key, part):
    base_key = jax.random.fold_in(jax.random.fold_in(key, 11), 0)
    entries = jnp.clip(jax.random.normal(base_key, (3, D, D), jnp.float32), -6.0, 6.0) * D ** (-0.5)
    return entries.astype(jnp.bfloat16)


def place_ends(drawn, rng, least, top_value):
    longest = drawn.shape.index(max(drawn.shape))
    spots = []
    for shift in (0, 1):
        where = [jax.random.randint(jax.random.fold_in(rng, axis), (), 0, length) for axis, length in enumerate(drawn.shape)]
        where[longest] = (where[longest] + shift) % drawn.shape[longest]
        spots.append(tuple(where))
    return drawn.at[spots[0]].set(least).at[spots[1]].set(top_value)


def steps_of(rng, extent, shards, smallest, high):
    level, own = 1.0, jax.random.fold_in(rng, 6)
    for axis_at, blocks in shards:
        steps = jnp.exp(jax.random.uniform(jax.random.fold_in(own, axis_at), (blocks,), jnp.float32, smallest / len(shards), high / len(shards)))
        level = level * jnp.repeat(steps, extent[axis_at] // blocks).reshape([-1 if axis == axis_at else 1 for axis in range(len(extent))])
    return level


def cumulative_ranks(amount, lean):
    loads = [(1 << 20) // math.isqrt(grade ** lean) + 1 for grade in range(1, amount + 1)]
    width = 1 + sum(loads) // (1 << 30)
    return np.cumsum(np.array([max(1, weight // width) for weight in loads]))


def ranked(key, shape, number_of, slope):
    listing = cumulative_ranks(number_of, slope)
    pick = jax.random.randint(jax.random.fold_in(key, 1), shape, 0, int(listing[number_of - 1]))
    grade = jnp.searchsorted(jnp.asarray(listing, jnp.int32), pick, side="right")
    return jax.random.permutation(jax.random.fold_in(key, 2), number_of)[grade].astype(jnp.int32)


def normal_values(own_key, shape, scale, bound, shards=(), held_as=jnp.bfloat16):
    level = steps_of(own_key, shape, shards, -0.22, 0.18) if shards else 1.0
    array = jax.random.normal(own_key, shape, jnp.float32) * scale * level
    return jnp.minimum(jnp.maximum(array, -bound), bound).astype(held_as)


def setup_inputs(seed: int = 0) -> dict:
    streams_of = jax.random.split(jax.random.key(seed), 10)
    return {
        "frames": normal_values(streams_of[0], (FRAMES, D), 1.0, 6.0, ((0, 8),)),
        "norm_gain": jnp.clip(1.0 + 0.1 * jax.random.normal(streams_of[1], (D,), jnp.float32), 0.5, 1.5),
        "w_qkv": draw_w_qkv(jax.random.fold_in(streams_of[9], 71), 0),
        "w_out": normal_values(streams_of[3], (D, D), D ** -0.5, 0.1875, ((0, 4),)),
        "w_proj": normal_values(streams_of[4], (D, E), D ** -0.5, 0.1875),
        "text_table": normal_values(streams_of[5], (VOCAB, E), 1.0, 6.0, ((0, 32),)),
        "token_ids": place_ends(ranked(streams_of[6], (NCAP, CL), VOCAB, 2), jax.random.fold_in(streams_of[6], 3), 0, VOCAB - 1).astype(jnp.int32),
        "span_bounds": draw_span_bounds(jax.random.fold_in(streams_of[9], 71), 0),
        "contrast_divisor": jnp.clip(jnp.exp(jax.random.uniform(streams_of[8], (1,), jnp.float32, math.log(10.0), math.log(30.0))), 10.0, 30.0),
    }


def log_total(values, axis):
    return jnp.log(lax.optimization_barrier(jnp.sum(jnp.exp(values), axis=axis)))

def unit_rows(values):
    return values * lax.rsqrt(lax.optimization_barrier(jnp.mean(values * values, axis=-1, keepdims=True)) + 1e-06) * E ** (-0.5)

def reference(frames, norm_gain, w_qkv, w_out, w_proj, text_table, token_ids, span_bounds, contrast_divisor):
    as32 = frames.astype(jnp.float32)
    normed = (as32 * lax.rsqrt(lax.optimization_barrier(jnp.mean(as32 * as32, axis=-1, keepdims=True)) + 1e-05) * norm_gain).astype(jnp.bfloat16)
    queries = jnp.dot(normed, w_qkv[0], preferred_element_type=jnp.float32).astype(jnp.bfloat16)
    keys_all = jnp.dot(normed, w_qkv[1], preferred_element_type=jnp.float32).astype(jnp.bfloat16)
    values_all = jnp.dot(normed, w_qkv[2], preferred_element_type=jnp.float32).astype(jnp.bfloat16)
    query_block = min(512, FR_DEV)
    span_width = 2 * FR_DEV + query_block
    keys_pad = jnp.pad(keys_all, ((FR_DEV, FR_DEV), (0, 0)))
    values_pad = jnp.pad(values_all, ((FR_DEV, FR_DEV), (0, 0)))

    def attend(block):
        begin = (block * query_block).astype(jnp.int32)
        query_part = lax.dynamic_slice_in_dim(queries, begin, query_block, 0).astype(jnp.float32).reshape(query_block, HEADS, HDIM)
        key_part = lax.dynamic_slice_in_dim(keys_pad, begin, span_width, 0).astype(jnp.float32).reshape(span_width, HEADS, HDIM)
        value_part = lax.dynamic_slice_in_dim(values_pad, begin, span_width, 0).astype(jnp.float32).reshape(span_width, HEADS, HDIM)
        scores = jnp.einsum('qhd,khd->hqk', query_part, key_part) * HDIM ** (-0.5)
        query_pos = begin + jnp.arange(query_block, dtype=jnp.int32)
        key_pos = begin - FR_DEV + jnp.arange(span_width, dtype=jnp.int32)
        allowed = (jnp.abs(query_pos[:, None] - key_pos[None, :]) <= FR_DEV) & (key_pos >= 0)[None, :] & (key_pos < FRAMES)[None, :]
        scores = jnp.where(allowed[None], scores, -1e+30)
        top = lax.optimization_barrier(jnp.max(scores, axis=2, keepdims=True))
        probs = jnp.exp(scores - top)
        denom = lax.optimization_barrier(jnp.sum(probs, axis=2))
        weights = probs.astype(jnp.bfloat16).astype(jnp.float32)
        mixed = jnp.einsum('hqk,khd->qhd', weights, value_part)
        return (mixed / denom.T[:, :, None]).astype(jnp.bfloat16).reshape(query_block, D)
    attended = lax.map(attend, jnp.arange(FRAMES // query_block, dtype=jnp.int32)).reshape(FRAMES, D)
    residual = as32 + jnp.dot(attended, w_out, preferred_element_type=jnp.float32)
    block_sums = residual.reshape(NBLK, BLK, D).sum(axis=1)
    block_table = jnp.dot(block_sums, w_proj.astype(jnp.float32), precision=lax.Precision.HIGHEST)
    block_ids = jnp.arange(NBLK, dtype=jnp.int32)
    lower = span_bounds[:, 0] // BLK
    upper = span_bounds[:, 1] // BLK
    span_mask = ((block_ids[None, :] >= lower[:, None]) & (block_ids[None, :] < upper[:, None])).astype(jnp.float32)
    pooled = jnp.dot(span_mask, block_table, precision=lax.Precision.HIGHEST)
    interval_embedding_rows = unit_rows(pooled).astype(jnp.bfloat16)
    raw = lax.optimization_barrier(jnp.sum(jnp.take(text_table, token_ids, axis=0).astype(jnp.float32), axis=1))
    text_embedding_rows = unit_rows(raw).astype(jnp.bfloat16)
    normalizer_divisor = contrast_divisor[0]
    pairwise_affinity_logits = jnp.dot(text_embedding_rows, interval_embedding_rows.T, preferred_element_type=jnp.float32) * normalizer_divisor
    row_lse = log_total(pairwise_affinity_logits, 1)
    col_lse = log_total(pairwise_affinity_logits, 0)
    loss_terms = 0.5 * (row_lse + col_lse) - jnp.diagonal(pairwise_affinity_logits)
    marker = jnp.eye(NCAP, dtype=jnp.float32)
    derivative_multipliers = (0.5 * jnp.exp(pairwise_affinity_logits - row_lse[:, None]) + 0.5 * jnp.exp(pairwise_affinity_logits - col_lse[None, :]) - marker).astype(jnp.bfloat16)
    interval_embedding_derivative = jnp.dot(derivative_multipliers.T, text_embedding_rows, preferred_element_type=jnp.float32) * normalizer_divisor
    return (interval_embedding_derivative, loss_terms)
```

```python
import jax
import jax.numpy as jnp
from jax import lax
from jax.sharding import PartitionSpec as P

HDIM = 64
E = 512
BLK = 128
EVERY = ("seq", "head")
LANES = 128


def unit_rows(values):
    return (
        values * lax.rsqrt(jnp.mean(values * values, axis=-1, keepdims=True) + 1e-06) * E ** (-0.5)
    )


def to_everyone(piece, devices):
    return lax.all_to_all(jnp.broadcast_to(piece[None], (devices,) + piece.shape), EVERY, 0, 0)


def local(
    frames, norm_gain, w_qkv, w_out, w_proj, text_table, token_ids, span_bounds, contrast_divisor
):
    frame_rows = frames.shape[0]
    head_cols = w_qkv.shape[2]
    local_heads = head_cols // HDIM
    seq_count = lax.axis_size("seq")
    head_count = lax.axis_size("head")
    devices = seq_count * head_count
    own_caps = span_bounds.shape[0]
    all_caps = token_ids.shape[0]
    slot = lax.axis_index(EVERY)
    head_slot = lax.axis_index("head")
    total_frames = frame_rows * seq_count
    first_frame = lax.axis_index("seq") * frame_rows

    as32 = frames.astype(jnp.float32)
    normed = (
        as32 * lax.rsqrt(jnp.mean(as32 * as32, axis=-1, keepdims=True) + 1e-05) * norm_gain
    ).astype(jnp.bfloat16)
    keys_now = jnp.dot(normed, w_qkv[1], preferred_element_type=jnp.float32).astype(jnp.bfloat16)
    values_now = jnp.dot(normed, w_qkv[2], preferred_element_type=jnp.float32).astype(jnp.bfloat16)
    pairs = jnp.concatenate([keys_now, values_now], axis=1)
    ends = seq_count - 1
    before = lax.ppermute(pairs, "seq", [(i, i + 1) for i in range(ends)])
    after = lax.ppermute(pairs, "seq", [(i + 1, i) for i in range(ends)])
    queries = jnp.dot(normed, w_qkv[0], preferred_element_type=jnp.float32).astype(jnp.bfloat16)

    vocab = text_table.shape[0]
    words = slot * vocab + jnp.arange(vocab, dtype=jnp.int32)
    counts = (token_ids[:, :, None] == words[None, None, :]).astype(jnp.float32).sum(axis=1)
    part = jnp.dot(counts.astype(jnp.bfloat16), text_table, preferred_element_type=jnp.float32)
    bounds = jnp.pad((span_bounds // BLK).astype(jnp.float32), ((0, 0), (0, LANES - 2)))
    sent = jnp.concatenate(
        [
            part.reshape(devices, own_caps, E),
            jnp.broadcast_to(bounds[None], (devices,) + bounds.shape),
        ],
        axis=2,
    )
    got = lax.all_to_all(sent, EVERY, 0, 0)
    caption_own = unit_rows(got[:, :, :E].sum(axis=0)).astype(jnp.bfloat16)
    lower = got[:, :, E].reshape(all_caps, 1)
    upper = got[:, :, E + 1].reshape(all_caps, 1)

    padded = jnp.concatenate([before, pairs, after], axis=0)
    span_width = 3 * frame_rows
    query_part = queries.reshape(frame_rows, local_heads, HDIM)
    key_part = padded[:, :head_cols].reshape(span_width, local_heads, HDIM)
    value_part = padded[:, head_cols:].reshape(span_width, local_heads, HDIM)
    scores = jnp.einsum(
        "qhd,khd->hqk", query_part, key_part, preferred_element_type=jnp.float32
    ) * HDIM ** (-0.5)
    query_pos = first_frame + jnp.arange(frame_rows, dtype=jnp.int32)
    key_pos = first_frame - frame_rows + jnp.arange(span_width, dtype=jnp.int32)
    allowed = (
        (jnp.abs(query_pos[:, None] - key_pos[None, :]) <= frame_rows)
        & (key_pos >= 0)[None, :]
        & (key_pos < total_frames)[None, :]
    )
    scores = jnp.where(allowed[None], scores, -1e30)
    top = jnp.max(scores, axis=2, keepdims=True)
    probs = jnp.exp(scores - top)
    denom = jnp.sum(probs, axis=2)
    mixed = jnp.einsum(
        "hqk,khd->qhd", probs.astype(jnp.bfloat16), value_part, preferred_element_type=jnp.float32
    )
    attended = (mixed / denom.T[:, :, None]).astype(jnp.bfloat16).reshape(frame_rows, head_cols)

    block_count = frame_rows // BLK
    out_sums = attended.astype(jnp.float32).reshape(block_count, BLK, head_cols).sum(axis=1)
    own_features = lax.dynamic_slice_in_dim(as32, head_slot * head_cols, head_cols, 1)
    feature_sums = own_features.reshape(block_count, BLK, head_cols).sum(axis=1)
    proj_rows = lax.dynamic_slice_in_dim(w_proj, head_slot * head_cols, head_cols, 0)
    through_out = jnp.dot(out_sums, w_out.astype(jnp.float32), precision=lax.Precision.HIGHEST)
    partial_value = jnp.dot(
        through_out, w_proj.astype(jnp.float32), precision=lax.Precision.HIGHEST
    ) + jnp.dot(feature_sums, proj_rows.astype(jnp.float32), precision=lax.Precision.HIGHEST)

    everyone = to_everyone(
        jnp.concatenate([partial_value, caption_own.astype(jnp.float32)], axis=0), devices
    )
    block_table = (
        everyone[:, :block_count]
        .reshape(seq_count, head_count, block_count, E)
        .sum(axis=1)
        .reshape(seq_count * block_count, E)
    )
    captions = everyone[:, block_count:].reshape(all_caps, E).astype(jnp.bfloat16)
    block_ids = jnp.arange(seq_count * block_count, dtype=jnp.int32).astype(jnp.float32)
    span_mask = ((block_ids[None, :] >= lower) & (block_ids[None, :] < upper)).astype(jnp.float32)
    pooled = jnp.dot(span_mask, block_table, precision=lax.Precision.HIGHEST)
    spans = unit_rows(pooled).astype(jnp.bfloat16)

    divisor = contrast_divisor[0]
    logits = jnp.einsum("je,ie->ji", captions, spans, preferred_element_type=jnp.float32) * divisor
    grown = jnp.exp(logits)
    row_total = jnp.log(jnp.sum(grown, axis=1))
    first = slot * own_caps
    own_logits = lax.dynamic_slice_in_dim(logits, first, own_caps, 1)
    col_total = jnp.log(jnp.sum(jnp.exp(own_logits), axis=0))
    marker = (
        jnp.arange(all_caps, dtype=jnp.int32)[:, None]
        == first + jnp.arange(own_caps, dtype=jnp.int32)[None, :]
    ).astype(jnp.float32)
    own_square = jnp.sum(own_logits * marker, axis=0)
    own_row_total = lax.dynamic_slice_in_dim(row_total, first, own_caps, 0)
    loss_terms = 0.5 * (own_row_total + col_total) - own_square
    weights = (
        0.5 * jnp.exp(own_logits - row_total[:, None])
        + 0.5 * jnp.exp(own_logits - col_total[None, :])
        - marker
    ).astype(jnp.bfloat16)
    derivative = (
        jnp.einsum("ji,je->ie", weights, captions, preferred_element_type=jnp.float32) * divisor
    )
    return (derivative, loss_terms)


def solution(mesh):
    placed = (
        P("seq", None),
        P(),
        P(None, None, "head"),
        P("head", None),
        P(),
        P(EVERY, None),
        P(),
        P(EVERY, None),
        P(),
    )
    return jax.shard_map(
        local,
        mesh=mesh,
        in_specs=placed,
        out_specs=(P(EVERY, None), P(EVERY)),
        check_vma=False,
    )
```

```python
import functools

import jax
import jax.numpy as jnp
from jax import lax
from jax.experimental import pallas as pl
from jax.experimental.pallas import tpu as pltpu
from jax.sharding import PartitionSpec as P

HDIM = 64
E = 512
BLK = 128
EVERY = ("seq", "head")
LANES = 128
SUB = 8
NEVER = -1e30
PIECE = jnp.bfloat16
VMEM = pl.BlockSpec(memory_space=pltpu.VMEM)
SMEM = pl.BlockSpec(memory_space=pltpu.SMEM)
ANY = pl.BlockSpec(memory_space=pl.ANY)
HIGHEST = lax.Precision.HIGHEST


def call(body, outs, ins, scratch=(), cost=(0, 0, 0), mib=40):
    return pl.pallas_call(
        body,
        out_shape=outs,
        in_specs=ins,
        out_specs=jax.tree.map(lambda _: VMEM, outs),
        scratch_shapes=scratch,
        compiler_params=pltpu.CompilerParams(vmem_limit_bytes=mib << 20),
        cost_estimate=pl.CostEstimate(
            flops=cost[0], bytes_accessed=cost[1], transcendentals=cost[2]
        ),
    )


def transposed_dot(left, right):
    return lax.dot_general(
        left, right, (((1,), (1,)), ((), ())), preferred_element_type=jnp.float32
    )


def qkv_kernel(
    frames_hbm, gain_ref, w_hbm, own_ref, p1_ref, p2_ref, p3_ref, frames, w, normed, sems
):
    rows = frames.shape[0]
    half = own_ref.shape[1]
    copies = [pltpu.make_async_copy(frames_hbm, frames, sems.at[0])] + [
        pltpu.make_async_copy(w_hbm.at[k], w.at[k], sems.at[1 + k]) for k in range(3)
    ]
    for k in (0, 2, 3, 1):
        copies[k].start()
    odd = lax.axis_index("seq") % 2 == 1
    copies[0].wait()
    step = min(64, rows)
    for r in range(0, rows, step):
        part = frames[r : r + step].astype(jnp.float32)
        scale = lax.rsqrt(jnp.mean(part * part, axis=-1, keepdims=True) + 1e-05)
        normed[r : r + step] = (part * scale * gain_ref[...]).astype(jnp.bfloat16)
    for k in (1, 2, 0):
        copies[1 + k].wait()
        both = jnp.dot(normed[...], w[k], preferred_element_type=jnp.float32).astype(jnp.bfloat16)
        if k == 0:
            both = both * jnp.bfloat16(HDIM ** (-0.5))
        mine = jnp.where(odd, both[:, half:], both[:, :half])
        other = jnp.where(odd, both[:, :half], both[:, half:])
        own_ref[k * rows : (k + 1) * rows] = mine
        p1_ref[k * rows : (k + 1) * rows] = other
        if k > 0:
            p2_ref[(k - 1) * rows : k * rows] = mine
            p3_ref[(k - 1) * rows : k * rows] = other


def text_kernel(ids_ref, table_ref, bounds_ref, t32_ref, t16_ref):
    caps, tokens = ids_ref.shape
    vocab = table_ref.shape[0]
    own_caps = bounds_ref.shape[0]
    slot = lax.axis_index("seq") * lax.axis_size("head") + lax.axis_index("head")
    ids = ids_ref[...] - slot * vocab
    words = lax.broadcasted_iota(jnp.int32, (caps, vocab), 1)
    counts = jnp.zeros((caps, vocab), jnp.float32)
    for t in range(tokens):
        counts = counts + jnp.where(ids[:, t : t + 1] == words, 1.0, 0.0)
    part = jnp.dot(counts.astype(jnp.bfloat16), table_ref[...], preferred_element_type=jnp.float32)
    chunks = [part[:, c : c + LANES] for c in range(0, E, LANES)]
    row = lax.broadcasted_iota(jnp.int32, (caps, LANES), 0)
    lane = lax.broadcasted_iota(jnp.int32, (caps, LANES), 1)
    bounds = jnp.zeros((caps, LANES), jnp.float32)
    for c in range(own_caps):
        for side in range(2):
            block = (bounds_ref[c, side] // BLK).astype(jnp.float32)
            bounds = jnp.where((row == slot * own_caps + c) & (lane == side), block, bounds)
    chunks.append(bounds)
    for c, chunk in enumerate(chunks):
        t32_ref[c * caps : (c + 1) * caps] = chunk
        t16_ref[c * caps : (c + 1) * caps] = chunk.astype(jnp.bfloat16)


def weights_kernel(frames_ref, w_out_ref, w_proj_ref, wc_ref, fp_ref):
    half = wc_ref.shape[0]
    cols = w_out_ref.shape[0]
    blocks = fp_ref.shape[0]
    odd = lax.axis_index("seq") % 2
    start = pl.multiple_of(lax.axis_index("head") * cols, LANES)
    wc_ref[...] = jnp.dot(
        w_out_ref[pl.ds(pl.multiple_of(odd * half, half), half), :],
        w_proj_ref[...],
        preferred_element_type=jnp.float32,
    )
    features = frames_ref[:, pl.ds(start, cols)].astype(jnp.float32)
    sums = jnp.sum(features.reshape(blocks, BLK, cols), axis=1)
    padded = jnp.concatenate([sums, jnp.zeros((SUB - blocks, cols), jnp.float32)], axis=0)
    fp_ref[...] = jnp.dot(
        padded, w_proj_ref[pl.ds(start, cols), :].astype(jnp.float32), precision=HIGHEST
    )[:blocks]


def attend_kernel(own_ref, r1_ref, r2_ref, r3_ref, wc_ref, fp_ref, out_ref):
    rows = own_ref.shape[0] // 3
    half = own_ref.shape[1]
    blocks = rows // BLK
    seq, last = lax.axis_index("seq"), lax.axis_size("seq") - 1
    odd = seq % 2
    apart = lax.broadcasted_iota(jnp.int32, (rows, rows), 0) - lax.broadcasted_iota(
        jnp.int32, (rows, rows), 1
    )
    lane = lax.broadcasted_iota(jnp.int32, (rows, half), 1)

    def block_sums(me, other, halo, parity, exists):
        side = jnp.where(parity == 0, apart, -apart)
        near = side >= 0
        far = side <= jnp.where(exists, 0, -2 * rows)
        query = me[0:rows]
        attended = jnp.zeros((rows, half), jnp.float32)
        for head in range(half // HDIM):
            mine = lane // HDIM == head
            q = jnp.where(mine, query, jnp.zeros_like(query))
            scores = [
                transposed_dot(q, me[rows : 2 * rows]),
                jnp.where(near, transposed_dot(q, other[rows : 2 * rows]), NEVER),
                jnp.where(far, transposed_dot(q, halo[0:rows]), NEVER),
            ]
            top = functools.reduce(jnp.maximum, [jnp.max(s, axis=1, keepdims=True) for s in scores])
            probs = [jnp.exp(s - top) for s in scores]
            denom = sum(jnp.sum(p, axis=1, keepdims=True) for p in probs)
            values = (me[2 * rows : 3 * rows], other[2 * rows : 3 * rows], halo[rows : 2 * rows])
            mixed = sum(
                jnp.dot(p.astype(jnp.bfloat16), v, preferred_element_type=jnp.float32)
                for p, v in zip(probs, values)
            )
            attended = jnp.where(mine, mixed / denom, attended)
        attended = attended.astype(jnp.bfloat16).astype(jnp.float32)
        return jnp.sum(attended.reshape(blocks, BLK, half), axis=1)

    here = block_sums(own_ref, r1_ref, r3_ref, odd, jnp.where(odd == 0, seq > 0, seq < last))
    there = block_sums(
        r1_ref, own_ref, r2_ref, 1 - odd, jnp.where(odd == 0, seq + 1 < last, seq > 1)
    )
    first = jnp.where(odd == 0, here, there)
    second = jnp.where(odd == 0, there, here)
    blank = jnp.zeros((SUB - 2 * blocks, half), jnp.float32)
    table = jnp.dot(jnp.concatenate([first, second, blank], axis=0), wc_ref[...], precision=HIGHEST)
    feature = fp_ref[...]
    none = jnp.zeros_like(feature)
    table = table[: 2 * blocks] + jnp.concatenate(
        [jnp.where(odd == 0, feature, none), jnp.where(odd == 0, none, feature)], axis=0
    )
    piece = jnp.concatenate([table[:, : E // 2], table[:, E // 2 :]], axis=0).astype(out_ref.dtype)
    out_ref[...] = jnp.broadcast_to(piece[None], out_ref.shape)


def tail_kernel(everyone_ref, mine_ref, last_ref, divisor_ref, derivative_ref, loss_ref):
    own_caps = derivative_ref.shape[0]
    devices, width, half = everyone_ref.shape
    caps = mine_ref.shape[0] // (E // LANES + 1)
    group = 2 * lax.axis_size("head")
    pairs = devices // group
    blocks = width // 2
    slot = lax.axis_index("seq") * lax.axis_size("head") + lax.axis_index("head")
    divisor = divisor_ref[0]

    total = mine_ref[...] + last_ref[...].astype(jnp.float32)
    raw = jnp.concatenate(
        [total[c * caps : (c + 1) * caps] for c in range(E // LANES)], axis=1
    )
    bounds = total[E // LANES * caps :]
    lower, upper = bounds[:, 0:1], bounds[:, 1:2]

    def unit(parts):
        mean = sum(jnp.sum(p * p, axis=-1, keepdims=True) for p in parts) * (1.0 / E)
        scale = lax.rsqrt(mean + 1e-06)
        parts = [(p * scale * E ** (-0.5)).astype(jnp.bfloat16) for p in parts]
        return parts[0] if len(parts) == 1 else jnp.concatenate(parts, axis=1)

    captions = unit([raw])
    sums = jnp.sum(
        everyone_ref[...].astype(jnp.float32).reshape(pairs, group, width, half), axis=1
    ).reshape(pairs * width, half)
    place = lax.broadcasted_iota(jnp.int32, (caps, pairs * width), 1)
    inner = place % width
    block = (place // width * blocks + inner % blocks).astype(jnp.float32)
    inside = (block >= lower) & (block < upper)
    pooled = [
        jnp.dot(
            jnp.where(inside & (inner // blocks == side), 1.0, 0.0), sums, precision=HIGHEST
        )
        for side in range(2)
    ]
    spans = unit(pooled)

    logits = transposed_dot(spans, captions) * divisor
    row_total = jnp.log(jnp.sum(jnp.exp(logits), axis=0, keepdims=True))
    tall = -(-own_caps // SUB) * SUB
    row = lax.broadcasted_iota(jnp.int32, (tall, caps), 0)
    marker = jnp.where(
        (row < own_caps) & (lax.broadcasted_iota(jnp.int32, (tall, caps), 1) == slot * own_caps + row),
        1.0,
        0.0,
    )
    own_spans = jnp.dot(
        marker.astype(jnp.bfloat16), spans, preferred_element_type=jnp.float32
    ).astype(jnp.bfloat16)
    own = transposed_dot(own_spans, captions) * divisor
    col_total = jnp.log(jnp.sum(jnp.exp(own), axis=1, keepdims=True))
    loss = 0.5 * (jnp.sum(marker * row_total, axis=1, keepdims=True) + col_total) - jnp.sum(
        marker * own, axis=1, keepdims=True
    )
    flip = lax.broadcasted_iota(jnp.int32, (tall, tall), 0) == lax.broadcasted_iota(
        jnp.int32, (tall, tall), 1
    )
    loss_ref[...] = jnp.sum(jnp.where(flip, loss, 0.0), axis=0, keepdims=True)[:, :own_caps]
    weights = (
        0.5 * jnp.exp(own - row_total) + 0.5 * jnp.exp(own - col_total) - marker
    ).astype(jnp.bfloat16)
    derivative = jnp.dot(weights, captions, preferred_element_type=jnp.float32) * divisor
    derivative_ref[...] = derivative[:own_caps]


def local(
    frames, norm_gain, w_qkv, w_out, w_proj, text_table, token_ids, span_bounds, contrast_divisor
):
    rows, width = frames.shape
    cols = w_qkv.shape[2]
    half = cols // 2
    seq_count, head_count = lax.axis_size("seq"), lax.axis_size("head")
    devices = seq_count * head_count
    own_caps = span_bounds.shape[0]
    blocks = rows // BLK
    shape = jax.ShapeDtypeStruct
    bf16, f32 = jnp.bfloat16, jnp.float32

    own, p1, p2, p3 = call(
        qkv_kernel,
        [shape((n * rows, half), bf16) for n in (3, 3, 2, 2)],
        [ANY, VMEM, ANY],
        [
            pltpu.VMEM(frames.shape, bf16),
            pltpu.VMEM(w_qkv.shape, bf16),
            pltpu.VMEM(frames.shape, bf16),
            pltpu.SemaphoreType.DMA((4,)),
        ],
        (6 * rows * width * cols, 2 * w_qkv.size, 0),
    )(frames, norm_gain[None], w_qkv)
    ends = seq_count - 1
    r1 = lax.ppermute(p1, "seq", [(s, s ^ 1) for s in range(seq_count)])
    r3 = lax.ppermute(
        p3,
        "seq",
        [(s, s + 1) for s in range(1, ends, 2)] + [(s, s - 1) for s in range(2, seq_count, 2)],
    )
    r2 = lax.ppermute(
        p2,
        "seq",
        [(s, s + 2) for s in range(1, ends - 1, 2)] + [(s, s - 2) for s in range(2, seq_count, 2)],
    )

    ids, _ = lax.optimization_barrier((token_ids, own))
    tall = (E // LANES + 1) * token_ids.shape[0]
    mine, sent = call(
        text_kernel,
        [shape((tall, LANES), f32), shape((tall, LANES), bf16)],
        [VMEM, VMEM, SMEM],
        cost=(2 * token_ids.shape[0] * text_table.size, 2 * text_table.size, 0),
    )(ids, text_table, span_bounds)

    def swap(mine, sent, axis, step):
        count = lax.axis_size(axis)
        return lax.ppermute(sent, axis, [(i, i ^ step) for i in range(count)])

    def add(mine, got):
        mine = mine + got.astype(f32)
        return mine, mine.astype(bf16)

    step = 1
    while step < head_count:
        mine, sent = add(mine, swap(mine, sent, "head", step))
        step *= 2

    wc, fp = call(
        weights_kernel,
        [shape((half, E), f32), shape((blocks, E), f32)],
        [VMEM] * 3,
        cost=(2 * half * w_proj.size, 2 * (w_proj.size + w_out.size + frames.size), 0),
    )(frames, w_out, w_proj)

    piece = call(
        attend_kernel,
        shape((devices, 4 * blocks, E // 2), PIECE),
        [VMEM] * 6,
        cost=(24 * rows * rows * cols, 10 * rows * cols, 6 * rows * rows * cols // HDIM),
    )(own, r1, r2, r3, wc, fp)

    got = swap(mine, sent, "seq", 1)
    everyone = lax.all_to_all(piece, EVERY, 0, 0)
    step = 2
    while step < seq_count:
        mine, sent = add(mine, got)
        got = swap(mine, sent, "seq", step)
        step *= 2

    derivative, loss = call(
        tail_kernel,
        [shape((own_caps, E), f32), shape((1, own_caps), f32)],
        [VMEM, VMEM, VMEM, SMEM],
        cost=(4 * E * token_ids.shape[0] ** 2, 2 * piece.size, 0),
    )(everyone, mine, got, contrast_divisor)
    return derivative, loss.reshape(own_caps)


def solution(mesh):
    placed = (
        P("seq", None),
        P(),
        P(None, None, "head"),
        P("head", None),
        P(),
        P(EVERY, None),
        P(),
        P(EVERY, None),
        P(),
    )
    return jax.shard_map(
        local,
        mesh=mesh,
        in_specs=placed,
        out_specs=(P(EVERY, None), P(EVERY)),
        check_vma=False,
    )
```

```python
import functools

import jax
import jax.numpy as jnp
from jax import lax
from jax.experimental import pallas as pl
from jax.experimental.pallas import tpu as pltpu
from jax.sharding import PartitionSpec as P

HDIM = 64
E = 512
BLK = 128
EVERY = ("seq", "head")
LANES = 128
SUB = 8
NEVER = -1e30
BOUND_ROWS = 16
PIECE = jnp.bfloat16
VMEM = pl.BlockSpec(memory_space=pltpu.VMEM)
SMEM = pl.BlockSpec(memory_space=pltpu.SMEM)
HBM = pl.BlockSpec(memory_space=pltpu.HBM)
HIGHEST = lax.Precision.HIGHEST


def call(body, outs, ins, scratch=(), cost=(0, 0, 0), mib=16):
    return pl.pallas_call(
        body,
        out_shape=outs,
        in_specs=ins,
        out_specs=jax.tree.map(lambda _: VMEM, outs),
        scratch_shapes=scratch,
        compiler_params=pltpu.CompilerParams(vmem_limit_bytes=mib << 20),
        cost_estimate=pl.CostEstimate(
            flops=cost[0], bytes_accessed=cost[1], transcendentals=cost[2]
        ),
    )


def transposed_dot(left, right):
    return lax.dot_general(
        left, right, (((1,), (1,)), ((), ())), preferred_element_type=jnp.float32
    )


def first_kernel(
    frames_hbm,
    gain_ref,
    w_hbm,
    ids_ref,
    table_hbm,
    bounds_ref,
    own_ref,
    p1_ref,
    p2_ref,
    p3_ref,
    t32_ref,
    t16_ref,
    frames,
    w,
    table,
    normed,
    sems,
):
    rows = frames.shape[0]
    half = own_ref.shape[1]
    copies = [
        pltpu.make_async_copy(frames_hbm, frames, sems.at[0]),
        *[pltpu.make_async_copy(w_hbm.at[k], w.at[k], sems.at[1 + k]) for k in range(3)],
        pltpu.make_async_copy(table_hbm, table, sems.at[4]),
    ]
    for k in (0, 2, 3, 1, 4):
        copies[k].start()
    odd = lax.axis_index("seq") % 2 == 1

    caps, tokens = ids_ref.shape
    vocab = table.shape[0]
    own_caps = bounds_ref.shape[0]
    slot = lax.axis_index("seq") * lax.axis_size("head") + lax.axis_index("head")
    ids = ids_ref[...] - slot * vocab
    words = lax.broadcasted_iota(jnp.int32, (caps, vocab), 1)
    counts = jnp.zeros((caps, vocab), jnp.float32)
    for t in range(tokens):
        counts = counts + jnp.where(ids[:, t : t + 1] == words, 1.0, 0.0)
    counts = counts.astype(jnp.bfloat16)

    copies[0].wait()
    step = min(64, rows)
    for r in range(0, rows, step):
        part = frames[r : r + step].astype(jnp.float32)
        scale = lax.rsqrt(jnp.mean(part * part, axis=-1, keepdims=True) + 1e-05)
        normed[r : r + step] = (part * scale * gain_ref[...]).astype(jnp.bfloat16)
    for k in (1, 2, 0):
        copies[1 + k].wait()
        both = jnp.dot(normed[...], w[k], preferred_element_type=jnp.float32).astype(jnp.bfloat16)
        if k == 0:
            both = both * jnp.bfloat16(HDIM ** (-0.5))
        mine = jnp.where(odd, both[:, half:], both[:, :half])
        other = jnp.where(odd, both[:, :half], both[:, half:])
        own_ref[k * rows : (k + 1) * rows] = mine
        p1_ref[k * rows : (k + 1) * rows] = other
        if k > 0:
            p2_ref[(k - 1) * rows : k * rows] = mine
            p3_ref[(k - 1) * rows : k * rows] = other

    copies[4].wait()
    part = jnp.dot(counts, table[...], preferred_element_type=jnp.float32)
    row = lax.broadcasted_iota(jnp.int32, (BOUND_ROWS, LANES), 0)
    place = row * LANES + lax.broadcasted_iota(jnp.int32, (BOUND_ROWS, LANES), 1)
    bounds = jnp.zeros((BOUND_ROWS, LANES), jnp.float32)
    for c in range(own_caps):
        for side in range(2):
            block = (bounds_ref[c, side] // BLK).astype(jnp.float32)
            bounds = jnp.where(place == side * caps + slot * own_caps + c, block, bounds)
    late = lax.axis_index("head") % 2 == 1
    few = caps // 2
    for c in range(E // LANES):
        early_half = part[:few, c * LANES : (c + 1) * LANES]
        late_half = part[few:, c * LANES : (c + 1) * LANES]
        t32_ref[c * few : (c + 1) * few] = jnp.where(late, late_half, early_half)
        t16_ref[c * few : (c + 1) * few] = jnp.where(late, early_half, late_half).astype(
            jnp.bfloat16
        )
    t32_ref[E // LANES * few :] = bounds
    t16_ref[E // LANES * few :] = bounds.astype(jnp.bfloat16)


def weights_kernel(frames_ref, w_out_ref, w_proj_ref, wc_ref, fp_ref):
    half = wc_ref.shape[0]
    cols = w_out_ref.shape[0]
    blocks = fp_ref.shape[0]
    odd = lax.axis_index("seq") % 2
    start = pl.multiple_of(lax.axis_index("head") * cols, LANES)
    wc_ref[...] = jnp.dot(
        w_out_ref[pl.ds(pl.multiple_of(odd * half, half), half), :],
        w_proj_ref[...],
        preferred_element_type=jnp.float32,
    )
    features = frames_ref[:, pl.ds(start, cols)].astype(jnp.float32)
    sums = jnp.sum(features.reshape(blocks, BLK, cols), axis=1)
    padded = jnp.concatenate([sums, jnp.zeros((SUB - blocks, cols), jnp.float32)], axis=0)
    fp_ref[...] = jnp.dot(
        padded, w_proj_ref[pl.ds(start, cols), :].astype(jnp.float32), precision=HIGHEST
    )[:blocks]


def attend_kernel(own_ref, r1_ref, r2_ref, r3_ref, wc_ref, fp_ref, out_ref):
    rows = own_ref.shape[0] // 3
    half = own_ref.shape[1]
    blocks = rows // BLK
    seq, last = lax.axis_index("seq"), lax.axis_size("seq") - 1
    odd = seq % 2
    apart = lax.broadcasted_iota(jnp.int32, (rows, rows), 0) - lax.broadcasted_iota(
        jnp.int32, (rows, rows), 1
    )
    lane = lax.broadcasted_iota(jnp.int32, (rows, half), 1)

    def block_sums(me, other, halo, parity, exists):
        side = jnp.where(parity == 0, apart, -apart)
        near = side >= 0
        far = side <= jnp.where(exists, 0, -2 * rows)
        query = me[0:rows]
        attended = jnp.zeros((rows, half), jnp.float32)
        for head in range(half // HDIM):
            mine = lane // HDIM == head
            q = jnp.where(mine, query, jnp.zeros_like(query))
            scores = [
                transposed_dot(q, me[rows : 2 * rows]),
                jnp.where(near, transposed_dot(q, other[rows : 2 * rows]), NEVER),
                jnp.where(far, transposed_dot(q, halo[0:rows]), NEVER),
            ]
            top = functools.reduce(jnp.maximum, [jnp.max(s, axis=1, keepdims=True) for s in scores])
            probs = [jnp.exp(s - top) for s in scores]
            denom = sum(jnp.sum(p, axis=1, keepdims=True) for p in probs)
            values = (me[2 * rows : 3 * rows], other[2 * rows : 3 * rows], halo[rows : 2 * rows])
            mixed = sum(
                jnp.dot(p.astype(jnp.bfloat16), v, preferred_element_type=jnp.float32)
                for p, v in zip(probs, values)
            )
            attended = jnp.where(mine, mixed / denom, attended)
        attended = attended.astype(jnp.bfloat16).astype(jnp.float32)
        return jnp.sum(attended.reshape(blocks, BLK, half), axis=1)

    here = block_sums(own_ref, r1_ref, r3_ref, odd, jnp.where(odd == 0, seq > 0, seq < last))
    there = block_sums(
        r1_ref, own_ref, r2_ref, 1 - odd, jnp.where(odd == 0, seq + 1 < last, seq > 1)
    )
    first = jnp.where(odd == 0, here, there)
    second = jnp.where(odd == 0, there, here)
    blank = jnp.zeros((SUB - 2 * blocks, half), jnp.float32)
    table = jnp.dot(jnp.concatenate([first, second, blank], axis=0), wc_ref[...], precision=HIGHEST)
    feature = fp_ref[...]
    none = jnp.zeros_like(feature)
    table = table[: 2 * blocks] + jnp.concatenate(
        [jnp.where(odd == 0, feature, none), jnp.where(odd == 0, none, feature)], axis=0
    )
    piece = jnp.concatenate([table[:, : E // 2], table[:, E // 2 :]], axis=0).astype(out_ref.dtype)
    out_ref[...] = jnp.broadcast_to(piece[None], out_ref.shape)


def tail_kernel(everyone_ref, mine_ref, last_ref, divisor_ref, derivative_ref, loss_ref):
    own_caps = derivative_ref.shape[0]
    devices, width, half = everyone_ref.shape
    few = (mine_ref.shape[0] - BOUND_ROWS) // (E // LANES)
    caps = 2 * few
    group = 2 * lax.axis_size("head")
    pairs = devices // group
    blocks = width // 2
    head = lax.axis_index("head")
    slot = lax.axis_index("seq") * lax.axis_size("head") + head
    divisor = divisor_ref[0]

    def rows_of(ref):
        chunks = [ref[c * few : (c + 1) * few] for c in range(E // LANES)]
        return jnp.concatenate(chunks, axis=1).astype(jnp.float32)

    mine, other = rows_of(mine_ref), rows_of(last_ref)
    late = head % 2 == 1
    raw = jnp.concatenate([jnp.where(late, other, mine), jnp.where(late, mine, other)], axis=0)

    def column(side):
        found = jnp.zeros((caps, LANES), jnp.float32)
        at = lax.broadcasted_iota(jnp.int32, (caps, LANES), 0) + side * caps
        lane = lax.broadcasted_iota(jnp.int32, (caps, LANES), 1)
        for r in range(-(-2 * caps // LANES)):
            line = mine_ref[E // LANES * few + r : E // LANES * few + r + 1]
            found = found + jnp.where(at == lane + r * LANES, line, 0.0)
        return jnp.sum(found, axis=1, keepdims=True)

    lower, upper = column(0), column(1)

    def unit(parts):
        mean = sum(jnp.sum(p * p, axis=-1, keepdims=True) for p in parts) * (1.0 / E)
        scale = lax.rsqrt(mean + 1e-06)
        parts = [(p * scale * E ** (-0.5)).astype(jnp.bfloat16) for p in parts]
        return parts[0] if len(parts) == 1 else jnp.concatenate(parts, axis=1)

    captions = unit([raw])
    sums = jnp.sum(
        everyone_ref[...].astype(jnp.float32).reshape(pairs, group, width, half), axis=1
    ).reshape(pairs * width, half)
    place = lax.broadcasted_iota(jnp.int32, (caps, pairs * width), 1)
    inner = place % width
    block = (place // width * blocks + inner % blocks).astype(jnp.float32)
    inside = (block >= lower) & (block < upper)
    pooled = [
        jnp.dot(
            jnp.where(inside & (inner // blocks == side), 1.0, 0.0), sums, precision=HIGHEST
        )
        for side in range(2)
    ]
    spans = unit(pooled)

    logits = transposed_dot(spans, captions) * divisor
    row_total = jnp.log(jnp.sum(jnp.exp(logits), axis=0, keepdims=True))
    tall = -(-own_caps // SUB) * SUB
    row = lax.broadcasted_iota(jnp.int32, (tall, caps), 0)
    marker = jnp.where(
        (row < own_caps) & (lax.broadcasted_iota(jnp.int32, (tall, caps), 1) == slot * own_caps + row),
        1.0,
        0.0,
    )
    own_spans = jnp.dot(
        marker.astype(jnp.bfloat16), spans, preferred_element_type=jnp.float32
    ).astype(jnp.bfloat16)
    own = transposed_dot(own_spans, captions) * divisor
    col_total = jnp.log(jnp.sum(jnp.exp(own), axis=1, keepdims=True))
    loss = 0.5 * (jnp.sum(marker * row_total, axis=1, keepdims=True) + col_total) - jnp.sum(
        marker * own, axis=1, keepdims=True
    )
    flip = lax.broadcasted_iota(jnp.int32, (tall, tall), 0) == lax.broadcasted_iota(
        jnp.int32, (tall, tall), 1
    )
    loss_ref[...] = jnp.sum(jnp.where(flip, loss, 0.0), axis=0, keepdims=True)[:, :own_caps]
    weights = (
        0.5 * jnp.exp(own - row_total) + 0.5 * jnp.exp(own - col_total) - marker
    ).astype(jnp.bfloat16)
    derivative = jnp.dot(weights, captions, preferred_element_type=jnp.float32) * divisor
    derivative_ref[...] = derivative[:own_caps]


def local(
    frames, norm_gain, w_qkv, w_out, w_proj, text_table, token_ids, span_bounds, contrast_divisor
):
    rows, width = frames.shape
    cols = w_qkv.shape[2]
    half = cols // 2
    seq_count, head_count = lax.axis_size("seq"), lax.axis_size("head")
    devices = seq_count * head_count
    own_caps = span_bounds.shape[0]
    blocks = rows // BLK
    shape = jax.ShapeDtypeStruct
    bf16, f32 = jnp.bfloat16, jnp.float32

    tall = E // LANES * token_ids.shape[0] // 2 + BOUND_ROWS
    own, p1, p2, p3, mine, sent = call(
        first_kernel,
        [shape((n * rows, half), bf16) for n in (3, 3, 2, 2)]
        + [shape((tall, LANES), f32), shape((tall, LANES), bf16)],
        [HBM, VMEM, HBM, VMEM, HBM, SMEM],
        [
            pltpu.VMEM(frames.shape, bf16),
            pltpu.VMEM(w_qkv.shape, bf16),
            pltpu.VMEM(text_table.shape, bf16),
            pltpu.VMEM(frames.shape, bf16),
            pltpu.SemaphoreType.DMA((5,)),
        ],
        (6 * rows * width * cols, 2 * w_qkv.size, 0),
        60,
    )(frames, norm_gain[None], w_qkv, token_ids, text_table, span_bounds)
    ends = seq_count - 1
    r1 = lax.ppermute(p1, "seq", [(s, s ^ 1) for s in range(seq_count)])
    r3 = lax.ppermute(
        p3,
        "seq",
        [(s, s + 1) for s in range(1, ends, 2)] + [(s, s - 1) for s in range(2, seq_count, 2)],
    )
    r2 = lax.ppermute(
        p2,
        "seq",
        [(s, s + 2) for s in range(1, ends - 1, 2)] + [(s, s - 2) for s in range(2, seq_count, 2)],
    )

    def swap(sent, seq_step, head_step):
        to = [
            (s ^ seq_step) * head_count + (h ^ head_step)
            for s in range(seq_count)
            for h in range(head_count)
        ]
        return lax.ppermute(sent, EVERY, list(enumerate(to)))

    def add(mine, *got):
        for g in got:
            mine = mine + g.astype(f32)
        return mine, mine.astype(bf16)

    mine, sent = add(mine, swap(sent, 0, 1))
    mine, sent = add(mine, swap(sent, 0, 2), swap(sent, 1, 0), swap(sent, 1, 2))

    wc, fp = call(
        weights_kernel,
        [shape((half, E), f32), shape((blocks, E), f32)],
        [VMEM] * 3,
        cost=(2 * half * w_proj.size, 2 * (w_proj.size + w_out.size + frames.size), 0),
    )(frames, w_out, w_proj)

    piece = call(
        attend_kernel,
        shape((devices, 4 * blocks, E // 2), PIECE),
        [VMEM] * 6,
        cost=(24 * rows * rows * cols, 10 * rows * cols, 6 * rows * rows * cols // HDIM),
    )(own, r1, r2, r3, wc, fp)

    step = 2
    while step < seq_count:
        if 4 * step <= seq_count:
            mine, sent = add(mine, *[swap(sent, k * step, 0) for k in (1, 2, 3)])
            step *= 4
        else:
            mine, sent = add(mine, swap(sent, step, 0))
            step *= 2
    everyone = lax.all_to_all(piece, EVERY, 0, 0)
    got = swap(sent, 0, 1)

    derivative, loss = call(
        tail_kernel,
        [shape((own_caps, E), f32), shape((1, own_caps), f32)],
        [VMEM, VMEM, VMEM, SMEM],
        cost=(4 * E * token_ids.shape[0] ** 2, 2 * piece.size, 0),
    )(everyone, mine, got, contrast_divisor)
    return derivative, loss.reshape(own_caps)


def solution(mesh):
    placed = (
        P("seq", None),
        P(),
        P(None, None, "head"),
        P("head", None),
        P(),
        P(EVERY, None),
        P(),
        P(EVERY, None),
        P(),
    )
    return jax.shard_map(
        local,
        mesh=mesh,
        in_specs=placed,
        out_specs=(P(EVERY, None), P(EVERY)),
        check_vma=False,
    )
```

```python
import functools

import jax
import jax.numpy as jnp
from jax import lax
from jax.experimental import pallas as pl
from jax.experimental.pallas import tpu as pltpu
from jax.sharding import PartitionSpec as P

HDIM = 64
E = 512
BLK = 128
EVERY = ("seq", "head")
LANES = 128
SUB = 8
NEVER = -1e30
BOUND_ROWS = 16
PIECE = jnp.bfloat16
VMEM = pl.BlockSpec(memory_space=pltpu.VMEM)
SMEM = pl.BlockSpec(memory_space=pltpu.SMEM)
HBM = pl.BlockSpec(memory_space=pltpu.HBM)
HIGHEST = lax.Precision.HIGHEST


def call(body, outs, ins, scratch=(), cost=(0, 0, 0), mib=16):
    return pl.pallas_call(
        body,
        out_shape=outs,
        in_specs=ins,
        out_specs=jax.tree.map(lambda _: VMEM, outs),
        scratch_shapes=scratch,
        compiler_params=pltpu.CompilerParams(vmem_limit_bytes=mib << 20),
        cost_estimate=pl.CostEstimate(
            flops=cost[0], bytes_accessed=cost[1], transcendentals=cost[2]
        ),
    )


def transposed_dot(left, right):
    return lax.dot_general(
        left, right, (((1,), (1,)), ((), ())), preferred_element_type=jnp.float32
    )


def first_kernel(
    frames_hbm,
    gain_ref,
    w_hbm,
    ids_ref,
    table_hbm,
    bounds_ref,
    own_ref,
    p1_ref,
    p2_ref,
    p3_ref,
    t32_ref,
    t16_ref,
    frames,
    w,
    table,
    normed,
    sems,
):
    rows = frames.shape[0]
    half = own_ref.shape[1]
    copies = [
        pltpu.make_async_copy(frames_hbm, frames, sems.at[0]),
        *[pltpu.make_async_copy(w_hbm.at[k], w.at[k], sems.at[1 + k]) for k in range(3)],
        pltpu.make_async_copy(table_hbm, table, sems.at[4]),
    ]
    for k in (0, 2, 3, 1, 4):
        copies[k].start()
    odd = lax.axis_index("seq") % 2 == 1

    tokens, caps = ids_ref.shape
    vocab = table.shape[0]
    own_caps = bounds_ref.shape[0]
    slot = lax.axis_index("seq") * lax.axis_size("head") + lax.axis_index("head")
    ids = (ids_ref[...] - slot * vocab).T
    words = lax.broadcasted_iota(jnp.int32, (caps, vocab), 1)
    counts = jnp.zeros((caps, vocab), jnp.float32)
    for t in range(tokens):
        counts = counts + jnp.where(ids[:, t : t + 1] == words, 1.0, 0.0)
    counts = counts.astype(jnp.bfloat16)

    copies[0].wait()
    step = min(64, rows)
    for r in range(0, rows, step):
        part = frames[r : r + step].astype(jnp.float32)
        scale = lax.rsqrt(jnp.mean(part * part, axis=-1, keepdims=True) + 1e-05)
        normed[r : r + step] = (part * scale * gain_ref[...]).astype(jnp.bfloat16)
    for k in (1, 2, 0):
        copies[1 + k].wait()
        both = jnp.dot(normed[...], w[k], preferred_element_type=jnp.float32).astype(jnp.bfloat16)
        if k == 0:
            both = both * jnp.bfloat16(HDIM ** (-0.5))
        mine = jnp.where(odd, both[:, half:], both[:, :half])
        other = jnp.where(odd, both[:, :half], both[:, half:])
        own_ref[k * rows : (k + 1) * rows] = mine
        p1_ref[k * rows : (k + 1) * rows] = other
        if k > 0:
            p2_ref[(k - 1) * rows : k * rows] = mine
            p3_ref[(k - 1) * rows : k * rows] = other

    copies[4].wait()
    part = jnp.dot(counts, table[...], preferred_element_type=jnp.float32)
    row = lax.broadcasted_iota(jnp.int32, (BOUND_ROWS, LANES), 0)
    place = row * LANES + lax.broadcasted_iota(jnp.int32, (BOUND_ROWS, LANES), 1)
    bounds = jnp.zeros((BOUND_ROWS, LANES), jnp.float32)
    for c in range(own_caps):
        for side in range(2):
            block = (bounds_ref[c, side] // BLK).astype(jnp.float32)
            bounds = jnp.where(place == side * caps + slot * own_caps + c, block, bounds)
    late = lax.axis_index("head") % 2 == 1
    few = caps // 2
    for c in range(E // LANES):
        early_half = part[:few, c * LANES : (c + 1) * LANES]
        late_half = part[few:, c * LANES : (c + 1) * LANES]
        t32_ref[c * few : (c + 1) * few] = jnp.where(late, late_half, early_half)
        t16_ref[c * few : (c + 1) * few] = jnp.where(late, early_half, late_half).astype(
            jnp.bfloat16
        )
    t32_ref[E // LANES * few :] = bounds
    t16_ref[E // LANES * few :] = bounds.astype(jnp.bfloat16)


def weights_kernel(frames_ref, w_out_ref, w_proj_ref, wc_ref, fp_ref):
    half = wc_ref.shape[0]
    cols = w_out_ref.shape[0]
    blocks = fp_ref.shape[0]
    odd = lax.axis_index("seq") % 2
    start = pl.multiple_of(lax.axis_index("head") * cols, LANES)
    wc_ref[...] = jnp.dot(
        w_out_ref[pl.ds(pl.multiple_of(odd * half, half), half), :],
        w_proj_ref[...],
        preferred_element_type=jnp.float32,
    )
    features = frames_ref[:, pl.ds(start, cols)].astype(jnp.float32)
    sums = jnp.sum(features.reshape(blocks, BLK, cols), axis=1)
    padded = jnp.concatenate([sums, jnp.zeros((SUB - blocks, cols), jnp.float32)], axis=0)
    fp_ref[...] = jnp.dot(
        padded, w_proj_ref[pl.ds(start, cols), :].astype(jnp.float32), precision=HIGHEST
    )[:blocks]


def attend_kernel(own_ref, r1_ref, r2_ref, r3_ref, wc_ref, fp_ref, out_ref):
    rows = own_ref.shape[0] // 3
    half = own_ref.shape[1]
    blocks = rows // BLK
    seq, last = lax.axis_index("seq"), lax.axis_size("seq") - 1
    odd = seq % 2
    apart = lax.broadcasted_iota(jnp.int32, (rows, rows), 0) - lax.broadcasted_iota(
        jnp.int32, (rows, rows), 1
    )
    lane = lax.broadcasted_iota(jnp.int32, (rows, half), 1)

    def block_sums(me, other, halo, parity, exists):
        side = jnp.where(parity == 0, apart, -apart)
        near = side >= 0
        far = side <= jnp.where(exists, 0, -2 * rows)
        query = me[0:rows]
        attended = jnp.zeros((rows, half), jnp.float32)
        for head in range(half // HDIM):
            mine = lane // HDIM == head
            q = jnp.where(mine, query, jnp.zeros_like(query))
            scores = [
                transposed_dot(q, me[rows : 2 * rows]),
                jnp.where(near, transposed_dot(q, other[rows : 2 * rows]), NEVER),
                jnp.where(far, transposed_dot(q, halo[0:rows]), NEVER),
            ]
            top = functools.reduce(jnp.maximum, [jnp.max(s, axis=1, keepdims=True) for s in scores])
            probs = [jnp.exp(s - top) for s in scores]
            denom = sum(jnp.sum(p, axis=1, keepdims=True) for p in probs)
            values = (me[2 * rows : 3 * rows], other[2 * rows : 3 * rows], halo[rows : 2 * rows])
            mixed = sum(
                jnp.dot(p.astype(jnp.bfloat16), v, preferred_element_type=jnp.float32)
                for p, v in zip(probs, values)
            )
            attended = jnp.where(mine, mixed / denom, attended)
        attended = attended.astype(jnp.bfloat16).astype(jnp.float32)
        return jnp.sum(attended.reshape(blocks, BLK, half), axis=1)

    here = block_sums(own_ref, r1_ref, r3_ref, odd, jnp.where(odd == 0, seq > 0, seq < last))
    there = block_sums(
        r1_ref, own_ref, r2_ref, 1 - odd, jnp.where(odd == 0, seq + 1 < last, seq > 1)
    )
    first = jnp.where(odd == 0, here, there)
    second = jnp.where(odd == 0, there, here)
    blank = jnp.zeros((SUB - 2 * blocks, half), jnp.float32)
    table = jnp.dot(jnp.concatenate([first, second, blank], axis=0), wc_ref[...], precision=HIGHEST)
    feature = fp_ref[...]
    none = jnp.zeros_like(feature)
    table = table[: 2 * blocks] + jnp.concatenate(
        [jnp.where(odd == 0, feature, none), jnp.where(odd == 0, none, feature)], axis=0
    )
    piece = jnp.concatenate([table[:, : E // 2], table[:, E // 2 :]], axis=0).astype(out_ref.dtype)
    out_ref[...] = jnp.broadcast_to(piece[None], out_ref.shape)


def tail_kernel(everyone_ref, mine_ref, last_ref, divisor_ref, derivative_ref, loss_ref):
    own_caps = derivative_ref.shape[0]
    devices, width, half = everyone_ref.shape
    few = (mine_ref.shape[0] - BOUND_ROWS) // (E // LANES)
    caps = 2 * few
    group = 2 * lax.axis_size("head")
    pairs = devices // group
    blocks = width // 2
    head = lax.axis_index("head")
    slot = lax.axis_index("seq") * lax.axis_size("head") + head
    divisor = divisor_ref[0]

    def rows_of(ref):
        chunks = [ref[c * few : (c + 1) * few] for c in range(E // LANES)]
        return jnp.concatenate(chunks, axis=1).astype(jnp.float32)

    mine, other = rows_of(mine_ref), rows_of(last_ref)
    late = head % 2 == 1
    raw = jnp.concatenate([jnp.where(late, other, mine), jnp.where(late, mine, other)], axis=0)

    def column(side):
        found = jnp.zeros((caps, LANES), jnp.float32)
        at = lax.broadcasted_iota(jnp.int32, (caps, LANES), 0) + side * caps
        lane = lax.broadcasted_iota(jnp.int32, (caps, LANES), 1)
        for r in range(-(-2 * caps // LANES)):
            line = mine_ref[E // LANES * few + r : E // LANES * few + r + 1]
            found = found + jnp.where(at == lane + r * LANES, line, 0.0)
        return jnp.sum(found, axis=1, keepdims=True)

    lower, upper = column(0), column(1)

    def unit(parts):
        mean = sum(jnp.sum(p * p, axis=-1, keepdims=True) for p in parts) * (1.0 / E)
        scale = lax.rsqrt(mean + 1e-06)
        parts = [(p * scale * E ** (-0.5)).astype(jnp.bfloat16) for p in parts]
        return parts[0] if len(parts) == 1 else jnp.concatenate(parts, axis=1)

    captions = unit([raw])
    sums = jnp.sum(
        everyone_ref[...].astype(jnp.float32).reshape(pairs, group, width, half), axis=1
    ).reshape(pairs * width, half)
    place = lax.broadcasted_iota(jnp.int32, (caps, pairs * width), 1)
    inner = place % width
    block = (place // width * blocks + inner % blocks).astype(jnp.float32)
    inside = (block >= lower) & (block < upper)
    pooled = [
        jnp.dot(
            jnp.where(inside & (inner // blocks == side), 1.0, 0.0), sums, precision=HIGHEST
        )
        for side in range(2)
    ]
    spans = unit(pooled)

    logits = transposed_dot(spans, captions) * divisor
    row_total = jnp.log(jnp.sum(jnp.exp(logits), axis=0, keepdims=True))
    tall = -(-own_caps // SUB) * SUB
    row = lax.broadcasted_iota(jnp.int32, (tall, caps), 0)
    marker = jnp.where(
        (row < own_caps) & (lax.broadcasted_iota(jnp.int32, (tall, caps), 1) == slot * own_caps + row),
        1.0,
        0.0,
    )
    own_spans = jnp.dot(
        marker.astype(jnp.bfloat16), spans, preferred_element_type=jnp.float32
    ).astype(jnp.bfloat16)
    own = transposed_dot(own_spans, captions) * divisor
    col_total = jnp.log(jnp.sum(jnp.exp(own), axis=1, keepdims=True))
    loss = 0.5 * (jnp.sum(marker * row_total, axis=1, keepdims=True) + col_total) - jnp.sum(
        marker * own, axis=1, keepdims=True
    )
    flip = lax.broadcasted_iota(jnp.int32, (tall, tall), 0) == lax.broadcasted_iota(
        jnp.int32, (tall, tall), 1
    )
    loss_ref[...] = jnp.sum(jnp.where(flip, loss, 0.0), axis=0, keepdims=True)[:, :own_caps]
    weights = (
        0.5 * jnp.exp(own - row_total) + 0.5 * jnp.exp(own - col_total) - marker
    ).astype(jnp.bfloat16)
    derivative = jnp.dot(weights, captions, preferred_element_type=jnp.float32) * divisor
    derivative_ref[...] = derivative[:own_caps]


def local(
    frames, norm_gain, w_qkv, w_out, w_proj, text_table, token_ids, span_bounds, contrast_divisor
):
    rows, width = frames.shape
    cols = w_qkv.shape[2]
    half = cols // 2
    seq_count, head_count = lax.axis_size("seq"), lax.axis_size("head")
    devices = seq_count * head_count
    own_caps = span_bounds.shape[0]
    blocks = rows // BLK
    shape = jax.ShapeDtypeStruct
    bf16, f32 = jnp.bfloat16, jnp.float32

    tall = E // LANES * token_ids.shape[0] // 2 + BOUND_ROWS
    own, p1, p2, p3, mine, sent = call(
        first_kernel,
        [shape((n * rows, half), bf16) for n in (3, 3, 2, 2)]
        + [shape((tall, LANES), f32), shape((tall, LANES), bf16)],
        [HBM, VMEM, HBM, VMEM, HBM, SMEM],
        [
            pltpu.VMEM(frames.shape, bf16),
            pltpu.VMEM(w_qkv.shape, bf16),
            pltpu.VMEM(text_table.shape, bf16),
            pltpu.VMEM(frames.shape, bf16),
            pltpu.SemaphoreType.DMA((5,)),
        ],
        (6 * rows * width * cols, 2 * w_qkv.size, 0),
        60,
    )(frames, norm_gain[None], w_qkv, token_ids.T, text_table, span_bounds)
    ends = seq_count - 1
    r1 = lax.ppermute(p1, "seq", [(s, s ^ 1) for s in range(seq_count)])
    r3 = lax.ppermute(
        p3,
        "seq",
        [(s, s + 1) for s in range(1, ends, 2)] + [(s, s - 1) for s in range(2, seq_count, 2)],
    )
    r2 = lax.ppermute(
        p2,
        "seq",
        [(s, s + 2) for s in range(1, ends - 1, 2)] + [(s, s - 2) for s in range(2, seq_count, 2)],
    )

    def swap(sent, seq_step, head_step):
        to = [
            (s ^ seq_step) * head_count + (h ^ head_step)
            for s in range(seq_count)
            for h in range(head_count)
        ]
        return lax.ppermute(sent, EVERY, list(enumerate(to)))

    def add(mine, *got):
        for g in got:
            mine = mine + g.astype(f32)
        return mine, mine.astype(bf16)

    mine, sent = add(mine, swap(sent, 0, 1))
    gots = [swap(sent, 0, 2), swap(sent, 1, 0), swap(sent, 1, 2)]

    wc, fp = call(
        weights_kernel,
        [shape((half, E), f32), shape((blocks, E), f32)],
        [VMEM] * 3,
        cost=(10**10, 2 * (w_proj.size + w_out.size + frames.size), 0),
    )(frames, w_out, w_proj)

    piece = call(
        attend_kernel,
        shape((devices, 4 * blocks, E // 2), PIECE),
        [VMEM] * 6,
        cost=(10**10, 10 * rows * cols, 6 * rows * rows * cols // HDIM),
    )(own, r1, r2, r3, wc, fp)

    gots, piece = lax.optimization_barrier((gots, piece))
    mine, sent = add(mine, *gots)
    step = 2
    while step < seq_count:
        if 4 * step <= seq_count:
            mine, sent = add(mine, *[swap(sent, k * step, 0) for k in (1, 2, 3)])
            step *= 4
        else:
            mine, sent = add(mine, swap(sent, step, 0))
            step *= 2
    everyone = lax.all_to_all(piece, EVERY, 0, 0)
    got = swap(sent, 0, 1)

    derivative, loss = call(
        tail_kernel,
        [shape((own_caps, E), f32), shape((1, own_caps), f32)],
        [VMEM, VMEM, VMEM, SMEM],
        cost=(4 * E * token_ids.shape[0] ** 2, 2 * piece.size, 0),
    )(everyone, mine, got, contrast_divisor)
    return derivative, loss.reshape(own_caps)


def solution(mesh):
    placed = (
        P("seq", None),
        P(),
        P(None, None, "head"),
        P("head", None),
        P(),
        P(EVERY, None),
        P(),
        P(EVERY, None),
        P(),
    )
    return jax.shard_map(
        local,
        mesh=mesh,
        in_specs=placed,
        out_specs=(P(EVERY, None), P(EVERY)),
        check_vma=False,
    )
```

```python
import functools

import jax
import jax.numpy as jnp
from jax import lax
from jax.experimental import pallas as pl
from jax.experimental.pallas import tpu as pltpu
from jax.sharding import PartitionSpec as P

HDIM = 64
E = 512
BLK = 128
EVERY = ("seq", "head")
LANES = 128
SUB = 8
NEVER = -1e30
BOUND_ROWS = 16
PIECE = jnp.bfloat16
VMEM = pl.BlockSpec(memory_space=pltpu.VMEM)
SMEM = pl.BlockSpec(memory_space=pltpu.SMEM)
HBM = pl.BlockSpec(memory_space=pltpu.HBM)
HIGHEST = lax.Precision.HIGHEST


def call(body, outs, ins, scratch=(), cost=(0, 0, 0), mib=16):
    return pl.pallas_call(
        body,
        out_shape=outs,
        in_specs=ins,
        out_specs=jax.tree.map(lambda _: VMEM, outs),
        scratch_shapes=scratch,
        compiler_params=pltpu.CompilerParams(vmem_limit_bytes=mib << 20),
        cost_estimate=pl.CostEstimate(
            flops=cost[0], bytes_accessed=cost[1], transcendentals=cost[2]
        ),
    )


def transposed_dot(left, right):
    return lax.dot_general(
        left, right, (((1,), (1,)), ((), ())), preferred_element_type=jnp.float32
    )


def first_kernel(
    frames_hbm,
    gain_ref,
    w_hbm,
    ids_ref,
    table_hbm,
    bounds_ref,
    own_ref,
    p1_ref,
    p2_ref,
    p3_ref,
    t32_ref,
    t16_ref,
    frames,
    w,
    table,
    normed,
    sems,
):
    rows = frames.shape[0]
    half = own_ref.shape[1]
    copies = [
        pltpu.make_async_copy(frames_hbm, frames, sems.at[0]),
        *[pltpu.make_async_copy(w_hbm.at[k], w.at[k], sems.at[1 + k]) for k in range(3)],
        pltpu.make_async_copy(table_hbm, table, sems.at[4]),
    ]
    for k in (0, 2, 3, 1, 4):
        copies[k].start()
    odd = lax.axis_index("seq") % 2 == 1

    tokens, caps = ids_ref.shape
    vocab = table.shape[0]
    own_caps = bounds_ref.shape[0]
    slot = lax.axis_index("seq") * lax.axis_size("head") + lax.axis_index("head")
    ids = (ids_ref[...] - slot * vocab).T
    words = lax.broadcasted_iota(jnp.int32, (caps, vocab), 1)
    counts = jnp.zeros((caps, vocab), jnp.float32)
    for t in range(tokens):
        counts = counts + jnp.where(ids[:, t : t + 1] == words, 1.0, 0.0)
    counts = counts.astype(jnp.bfloat16)

    copies[0].wait()
    step = min(64, rows)
    for r in range(0, rows, step):
        part = frames[r : r + step].astype(jnp.float32)
        scale = lax.rsqrt(jnp.mean(part * part, axis=-1, keepdims=True) + 1e-05)
        normed[r : r + step] = (part * scale * gain_ref[...]).astype(jnp.bfloat16)
    for k in (1, 2, 0):
        copies[1 + k].wait()
        both = jnp.dot(normed[...], w[k], preferred_element_type=jnp.float32).astype(jnp.bfloat16)
        if k == 0:
            both = both * jnp.bfloat16(HDIM ** (-0.5))
        mine = jnp.where(odd, both[:, half:], both[:, :half])
        other = jnp.where(odd, both[:, :half], both[:, half:])
        own_ref[k * rows : (k + 1) * rows] = mine
        p1_ref[k * rows : (k + 1) * rows] = other
        if k > 0:
            p2_ref[(k - 1) * rows : k * rows] = mine
            p3_ref[(k - 1) * rows : k * rows] = other

    copies[4].wait()
    part = jnp.dot(counts, table[...], preferred_element_type=jnp.float32)
    row = lax.broadcasted_iota(jnp.int32, (BOUND_ROWS, LANES), 0)
    place = row * LANES + lax.broadcasted_iota(jnp.int32, (BOUND_ROWS, LANES), 1)
    bounds = jnp.zeros((BOUND_ROWS, LANES), jnp.float32)
    for c in range(own_caps):
        for side in range(2):
            block = (bounds_ref[c, side] // BLK).astype(jnp.float32)
            bounds = jnp.where(place == side * caps + slot * own_caps + c, block, bounds)
    late = lax.axis_index("head") % 2 == 1
    few = caps // 2
    for c in range(E // LANES):
        early_half = part[:few, c * LANES : (c + 1) * LANES]
        late_half = part[few:, c * LANES : (c + 1) * LANES]
        t32_ref[c * few : (c + 1) * few] = jnp.where(late, late_half, early_half)
        t16_ref[c * few : (c + 1) * few] = jnp.where(late, early_half, late_half).astype(
            jnp.bfloat16
        )
    t32_ref[E // LANES * few :] = bounds
    t16_ref[E // LANES * few :] = bounds.astype(jnp.bfloat16)


def weights_kernel(frames_ref, w_out_ref, w_proj_ref, wc_ref, fp_ref):
    half = wc_ref.shape[0]
    cols = w_out_ref.shape[0]
    blocks = fp_ref.shape[0]
    odd = lax.axis_index("seq") % 2
    start = pl.multiple_of(lax.axis_index("head") * cols, LANES)
    wc_ref[...] = jnp.dot(
        w_out_ref[pl.ds(pl.multiple_of(odd * half, half), half), :],
        w_proj_ref[...],
        preferred_element_type=jnp.float32,
    )
    features = frames_ref[:, pl.ds(start, cols)].astype(jnp.float32)
    sums = jnp.sum(features.reshape(blocks, BLK, cols), axis=1)
    padded = jnp.concatenate([sums, jnp.zeros((SUB - blocks, cols), jnp.float32)], axis=0)
    fp_ref[...] = jnp.dot(
        padded, w_proj_ref[pl.ds(start, cols), :].astype(jnp.float32), precision=HIGHEST
    )[:blocks]


def attend_kernel(own_ref, r1_ref, r2_ref, r3_ref, wc_ref, fp_ref, out_ref):
    rows = own_ref.shape[0] // 3
    half = own_ref.shape[1]
    blocks = rows // BLK
    seq, last = lax.axis_index("seq"), lax.axis_size("seq") - 1
    odd = seq % 2
    apart = lax.broadcasted_iota(jnp.int32, (rows, rows), 0) - lax.broadcasted_iota(
        jnp.int32, (rows, rows), 1
    )
    lane = lax.broadcasted_iota(jnp.int32, (rows, half), 1)

    def block_sums(me, other, halo, parity, exists):
        side = jnp.where(parity == 0, apart, -apart)
        near = side >= 0
        far = side <= jnp.where(exists, 0, -2 * rows)
        query = me[0:rows]
        attended = jnp.zeros((rows, half), jnp.float32)
        for head in range(half // HDIM):
            mine = lane // HDIM == head
            q = jnp.where(mine, query, jnp.zeros_like(query))
            scores = [
                transposed_dot(q, me[rows : 2 * rows]),
                jnp.where(near, transposed_dot(q, other[rows : 2 * rows]), NEVER),
                jnp.where(far, transposed_dot(q, halo[0:rows]), NEVER),
            ]
            top = functools.reduce(jnp.maximum, [jnp.max(s, axis=1, keepdims=True) for s in scores])
            probs = [jnp.exp(s - top) for s in scores]
            denom = sum(jnp.sum(p, axis=1, keepdims=True) for p in probs)
            values = (me[2 * rows : 3 * rows], other[2 * rows : 3 * rows], halo[rows : 2 * rows])
            mixed = sum(
                jnp.dot(p.astype(jnp.bfloat16), v, preferred_element_type=jnp.float32)
                for p, v in zip(probs, values)
            )
            attended = jnp.where(mine, mixed / denom, attended)
        attended = attended.astype(jnp.bfloat16).astype(jnp.float32)
        return jnp.sum(attended.reshape(blocks, BLK, half), axis=1)

    here = block_sums(own_ref, r1_ref, r3_ref, odd, jnp.where(odd == 0, seq > 0, seq < last))
    there = block_sums(
        r1_ref, own_ref, r2_ref, 1 - odd, jnp.where(odd == 0, seq + 1 < last, seq > 1)
    )
    first = jnp.where(odd == 0, here, there)
    second = jnp.where(odd == 0, there, here)
    blank = jnp.zeros((SUB - 2 * blocks, half), jnp.float32)
    table = jnp.dot(jnp.concatenate([first, second, blank], axis=0), wc_ref[...], precision=HIGHEST)
    feature = fp_ref[...]
    none = jnp.zeros_like(feature)
    table = table[: 2 * blocks] + jnp.concatenate(
        [jnp.where(odd == 0, feature, none), jnp.where(odd == 0, none, feature)], axis=0
    )
    piece = jnp.concatenate([table[:, : E // 2], table[:, E // 2 :]], axis=0).astype(out_ref.dtype)
    out_ref[...] = jnp.broadcast_to(piece[None], out_ref.shape)


def tail_kernel(everyone_ref, mine_ref, last_ref, divisor_ref, derivative_ref, loss_ref):
    own_caps = derivative_ref.shape[0]
    devices, width, half = everyone_ref.shape
    few = (mine_ref.shape[0] - BOUND_ROWS) // (E // LANES)
    caps = 2 * few
    group = 2 * lax.axis_size("head")
    pairs = devices // group
    blocks = width // 2
    head = lax.axis_index("head")
    slot = lax.axis_index("seq") * lax.axis_size("head") + head
    divisor = divisor_ref[0]

    def rows_of(ref):
        chunks = [ref[c * few : (c + 1) * few] for c in range(E // LANES)]
        return jnp.concatenate(chunks, axis=1).astype(jnp.float32)

    mine, other = rows_of(mine_ref), rows_of(last_ref)
    late = head % 2 == 1
    raw = jnp.concatenate([jnp.where(late, other, mine), jnp.where(late, mine, other)], axis=0)

    def column(side):
        found = jnp.zeros((caps, LANES), jnp.float32)
        at = lax.broadcasted_iota(jnp.int32, (caps, LANES), 0) + side * caps
        lane = lax.broadcasted_iota(jnp.int32, (caps, LANES), 1)
        for r in range(-(-2 * caps // LANES)):
            line = mine_ref[E // LANES * few + r : E // LANES * few + r + 1]
            found = found + jnp.where(at == lane + r * LANES, line, 0.0)
        return jnp.sum(found, axis=1, keepdims=True)

    lower, upper = column(0), column(1)

    def unit(parts):
        mean = sum(jnp.sum(p * p, axis=-1, keepdims=True) for p in parts) * (1.0 / E)
        scale = lax.rsqrt(mean + 1e-06)
        parts = [(p * scale * E ** (-0.5)).astype(jnp.bfloat16) for p in parts]
        return parts[0] if len(parts) == 1 else jnp.concatenate(parts, axis=1)

    captions = unit([raw])
    sums = jnp.sum(
        everyone_ref[...].astype(jnp.float32).reshape(pairs, group, width, half), axis=1
    ).reshape(pairs * width, half)
    place = lax.broadcasted_iota(jnp.int32, (caps, pairs * width), 1)
    inner = place % width
    block = (place // width * blocks + inner % blocks).astype(jnp.float32)
    inside = (block >= lower) & (block < upper)
    pooled = [
        jnp.dot(
            jnp.where(inside & (inner // blocks == side), 1.0, 0.0), sums, precision=HIGHEST
        )
        for side in range(2)
    ]
    spans = unit(pooled)

    logits = transposed_dot(spans, captions) * divisor
    row_total = jnp.log(jnp.sum(jnp.exp(logits), axis=0, keepdims=True))
    tall = -(-own_caps // SUB) * SUB
    row = lax.broadcasted_iota(jnp.int32, (tall, caps), 0)
    marker = jnp.where(
        (row < own_caps) & (lax.broadcasted_iota(jnp.int32, (tall, caps), 1) == slot * own_caps + row),
        1.0,
        0.0,
    )
    own_spans = jnp.dot(
        marker.astype(jnp.bfloat16), spans, preferred_element_type=jnp.float32
    ).astype(jnp.bfloat16)
    own = transposed_dot(own_spans, captions) * divisor
    col_total = jnp.log(jnp.sum(jnp.exp(own), axis=1, keepdims=True))
    loss = 0.5 * (jnp.sum(marker * row_total, axis=1, keepdims=True) + col_total) - jnp.sum(
        marker * own, axis=1, keepdims=True
    )
    flip = lax.broadcasted_iota(jnp.int32, (tall, tall), 0) == lax.broadcasted_iota(
        jnp.int32, (tall, tall), 1
    )
    loss_ref[...] = jnp.sum(jnp.where(flip, loss, 0.0), axis=0, keepdims=True)[:, :own_caps]
    weights = (
        0.5 * jnp.exp(own - row_total) + 0.5 * jnp.exp(own - col_total) - marker
    ).astype(jnp.bfloat16)
    derivative = jnp.dot(weights, captions, preferred_element_type=jnp.float32) * divisor
    derivative_ref[...] = derivative[:own_caps]


def local(
    frames, norm_gain, w_qkv, w_out, w_proj, text_table, token_ids, span_bounds, contrast_divisor
):
    rows, width = frames.shape
    cols = w_qkv.shape[2]
    half = cols // 2
    seq_count, head_count = lax.axis_size("seq"), lax.axis_size("head")
    devices = seq_count * head_count
    own_caps = span_bounds.shape[0]
    blocks = rows // BLK
    shape = jax.ShapeDtypeStruct
    bf16, f32 = jnp.bfloat16, jnp.float32

    tall = E // LANES * token_ids.shape[0] // 2 + BOUND_ROWS
    own, p1, p2, p3, mine, sent = call(
        first_kernel,
        [shape((n * rows, half), bf16) for n in (3, 3, 2, 2)]
        + [shape((tall, LANES), f32), shape((tall, LANES), bf16)],
        [HBM, VMEM, HBM, VMEM, HBM, SMEM],
        [
            pltpu.VMEM(frames.shape, bf16),
            pltpu.VMEM(w_qkv.shape, bf16),
            pltpu.VMEM(text_table.shape, bf16),
            pltpu.VMEM(frames.shape, bf16),
            pltpu.SemaphoreType.DMA((5,)),
        ],
        (6 * rows * width * cols, 2 * w_qkv.size, 0),
        60,
    )(frames, norm_gain[None], w_qkv, token_ids.T, text_table, span_bounds)
    ends = seq_count - 1
    r1 = lax.ppermute(p1, "seq", [(s, s ^ 1) for s in range(seq_count)])
    r3 = lax.ppermute(
        p3,
        "seq",
        [(s, s + 1) for s in range(1, ends, 2)] + [(s, s - 1) for s in range(2, seq_count, 2)],
    )
    r2 = lax.ppermute(
        p2,
        "seq",
        [(s, s + 2) for s in range(1, ends - 1, 2)] + [(s, s - 2) for s in range(2, seq_count, 2)],
    )

    def swap(sent, seq_step, head_step):
        to = [
            (s ^ seq_step) * head_count + (h ^ head_step)
            for s in range(seq_count)
            for h in range(head_count)
        ]
        return lax.ppermute(sent, EVERY, list(enumerate(to)))

    def add(mine, *got):
        for g in got:
            mine = mine + g.astype(f32)
        return mine, mine.astype(bf16)

    mine, sent = add(mine, swap(sent, 0, 1))
    got, r1 = lax.optimization_barrier((swap(sent, 0, 2), r1))
    mine, sent = add(mine, got)
    got = swap(sent, 1, 0)

    wc, fp = call(
        weights_kernel,
        [shape((half, E), f32), shape((blocks, E), f32)],
        [VMEM] * 3,
        cost=(10**10, 2 * (w_proj.size + w_out.size + frames.size), 0),
    )(frames, w_out, w_proj)

    piece = call(
        attend_kernel,
        shape((devices, 4 * blocks, E // 2), PIECE),
        [VMEM] * 6,
        cost=(10**10, 10 * rows * cols, 6 * rows * rows * cols // HDIM),
    )(own, r1, r2, r3, wc, fp)

    got, piece = lax.optimization_barrier((got, piece))
    mine, sent = add(mine, got)
    step = 2
    while step < seq_count:
        if 4 * step <= seq_count:
            mine, sent = add(mine, *[swap(sent, k * step, 0) for k in (1, 2, 3)])
            step *= 4
        else:
            mine, sent = add(mine, swap(sent, step, 0))
            step *= 2
    everyone = lax.all_to_all(piece, EVERY, 0, 0)
    got = swap(sent, 0, 1)

    derivative, loss = call(
        tail_kernel,
        [shape((own_caps, E), f32), shape((1, own_caps), f32)],
        [VMEM, VMEM, VMEM, SMEM],
        cost=(4 * E * token_ids.shape[0] ** 2, 2 * piece.size, 0),
    )(everyone, mine, got, contrast_divisor)
    return derivative, loss.reshape(own_caps)


def solution(mesh):
    placed = (
        P("seq", None),
        P(),
        P(None, None, "head"),
        P("head", None),
        P(),
        P(EVERY, None),
        P(),
        P(EVERY, None),
        P(),
    )
    return jax.shard_map(
        local,
        mesh=mesh,
        in_specs=placed,
        out_specs=(P(EVERY, None), P(EVERY)),
        check_vma=False,
    )
```

```python
import functools

import jax
import jax.numpy as jnp
from jax import lax
from jax.experimental import pallas as pl
from jax.experimental.pallas import tpu as pltpu
from jax.sharding import PartitionSpec as P

HDIM = 64
E = 512
BLK = 128
EVERY = ("seq", "head")
LANES = 128
SUB = 8
NEVER = -1e30
BOUND_ROWS = 16
PIECE = jnp.bfloat16
VMEM = pl.BlockSpec(memory_space=pltpu.VMEM)
SMEM = pl.BlockSpec(memory_space=pltpu.SMEM)
HBM = pl.BlockSpec(memory_space=pltpu.HBM)
HIGHEST = lax.Precision.HIGHEST


def call(body, outs, ins, scratch=(), cost=(0, 0, 0), mib=24):
    return pl.pallas_call(
        body,
        out_shape=outs,
        in_specs=ins,
        out_specs=jax.tree.map(lambda _: VMEM, outs),
        scratch_shapes=scratch,
        compiler_params=pltpu.CompilerParams(vmem_limit_bytes=mib << 20),
        cost_estimate=pl.CostEstimate(
            flops=cost[0], bytes_accessed=cost[1], transcendentals=cost[2]
        ),
    )


def transposed_dot(left, right):
    return lax.dot_general(
        left, right, (((1,), (1,)), ((), ())), preferred_element_type=jnp.float32
    )


def first_kernel(
    frames_hbm,
    gain_hbm,
    w_hbm,
    ids_hbm,
    table_hbm,
    bounds_hbm,
    own_ref,
    p1_ref,
    p2_ref,
    p3_ref,
    t32_ref,
    t16_ref,
    frames,
    gain,
    w,
    id_rows,
    table,
    bound,
    normed,
    sems,
):
    rows = frames.shape[0]
    half = own_ref.shape[1]
    parts = [(ids_hbm, id_rows), (frames_hbm, frames), (gain_hbm, gain)]
    parts += [(w_hbm.at[k], w.at[k]) for k in (1, 2, 0)]
    parts += [(table_hbm, table), (bounds_hbm, bound)]
    copies = [pltpu.make_async_copy(*part, sems.at[n]) for n, part in enumerate(parts)]
    for copy in copies:
        copy.start()
    odd = lax.axis_index("seq") % 2 == 1

    tokens, caps = id_rows.shape
    vocab = table.shape[0]
    own_caps = bound.shape[0]
    slot = lax.axis_index("seq") * lax.axis_size("head") + lax.axis_index("head")
    copies[0].wait()
    ids = (id_rows[...] - slot * vocab).T
    words = lax.broadcasted_iota(jnp.int32, (caps, vocab), 1)
    counts = jnp.zeros((caps, vocab), jnp.float32)
    for t in range(tokens):
        counts = counts + jnp.where(ids[:, t : t + 1] == words, 1.0, 0.0)
    counts = counts.astype(jnp.bfloat16)

    copies[1].wait()
    copies[2].wait()
    step = min(64, rows)
    for r in range(0, rows, step):
        part = frames[r : r + step].astype(jnp.float32)
        scale = lax.rsqrt(jnp.mean(part * part, axis=-1, keepdims=True) + 1e-05)
        normed[r : r + step] = (part * scale * gain[...]).astype(jnp.bfloat16)
    for n, k in enumerate((1, 2, 0)):
        copies[3 + n].wait()
        both = jnp.dot(normed[...], w[k], preferred_element_type=jnp.float32).astype(jnp.bfloat16)
        if k == 0:
            both = both * jnp.bfloat16(HDIM ** (-0.5))
        mine = jnp.where(odd, both[:, half:], both[:, :half])
        other = jnp.where(odd, both[:, :half], both[:, half:])
        own_ref[k * rows : (k + 1) * rows] = mine
        p1_ref[k * rows : (k + 1) * rows] = other
        if k > 0:
            p2_ref[(k - 1) * rows : k * rows] = mine
            p3_ref[(k - 1) * rows : k * rows] = other

    copies[6].wait()
    copies[7].wait()
    part = jnp.dot(counts, table[...], preferred_element_type=jnp.float32)
    row = lax.broadcasted_iota(jnp.int32, (BOUND_ROWS, LANES), 0)
    place = row * LANES + lax.broadcasted_iota(jnp.int32, (BOUND_ROWS, LANES), 1)
    bounds = jnp.zeros((BOUND_ROWS, LANES), jnp.float32)
    for c in range(own_caps):
        for side in range(2):
            block = (bound[c, side] // BLK).astype(jnp.float32)
            bounds = jnp.where(place == side * caps + slot * own_caps + c, block, bounds)
    sums = E // LANES * caps
    for c in range(E // LANES):
        chunk = part[:, c * LANES : (c + 1) * LANES]
        t32_ref[c * caps : (c + 1) * caps] = chunk
        t16_ref[c * caps : (c + 1) * caps] = chunk.astype(jnp.bfloat16)
    t32_ref[sums:] = bounds
    t16_ref[sums:] = bounds.astype(jnp.bfloat16)


def weights_kernel(frames_ref, w_out_ref, w_proj_ref, wc_ref, fp_ref):
    half = wc_ref.shape[0]
    cols = w_out_ref.shape[0]
    blocks = fp_ref.shape[0]
    odd = lax.axis_index("seq") % 2
    start = pl.multiple_of(lax.axis_index("head") * cols, LANES)
    wc_ref[...] = jnp.dot(
        w_out_ref[pl.ds(pl.multiple_of(odd * half, half), half), :],
        w_proj_ref[...],
        preferred_element_type=jnp.float32,
    )
    features = frames_ref[:, pl.ds(start, cols)].astype(jnp.float32)
    sums = jnp.sum(features.reshape(blocks, BLK, cols), axis=1)
    padded = jnp.concatenate([sums, jnp.zeros((SUB - blocks, cols), jnp.float32)], axis=0)
    fp_ref[...] = jnp.dot(
        padded, w_proj_ref[pl.ds(start, cols), :].astype(jnp.float32), precision=HIGHEST
    )[:blocks]


def attend_kernel(own_ref, r1_ref, r2_ref, r3_ref, wc_ref, fp_ref, out_ref):
    rows = own_ref.shape[0] // 3
    half = own_ref.shape[1]
    blocks = rows // BLK
    seq, last = lax.axis_index("seq"), lax.axis_size("seq") - 1
    odd = seq % 2
    apart = lax.broadcasted_iota(jnp.int32, (rows, rows), 0) - lax.broadcasted_iota(
        jnp.int32, (rows, rows), 1
    )
    lane = lax.broadcasted_iota(jnp.int32, (rows, half), 1)

    def block_sums(me, other, halo, parity, exists):
        side = jnp.where(parity == 0, apart, -apart)
        near = side >= 0
        far = side <= jnp.where(exists, 0, -2 * rows)
        query = me[0:rows]
        attended = jnp.zeros((rows, half), jnp.float32)
        for head in range(half // HDIM):
            mine = lane // HDIM == head
            q = jnp.where(mine, query, jnp.zeros_like(query))
            scores = [
                transposed_dot(q, me[rows : 2 * rows]),
                jnp.where(near, transposed_dot(q, other[rows : 2 * rows]), NEVER),
                jnp.where(far, transposed_dot(q, halo[0:rows]), NEVER),
            ]
            top = functools.reduce(jnp.maximum, [jnp.max(s, axis=1, keepdims=True) for s in scores])
            probs = [jnp.exp(s - top) for s in scores]
            denom = sum(jnp.sum(p, axis=1, keepdims=True) for p in probs)
            values = (me[2 * rows : 3 * rows], other[2 * rows : 3 * rows], halo[rows : 2 * rows])
            mixed = sum(
                jnp.dot(p.astype(jnp.bfloat16), v, preferred_element_type=jnp.float32)
                for p, v in zip(probs, values)
            )
            attended = jnp.where(mine, mixed / denom, attended)
        attended = attended.astype(jnp.bfloat16).astype(jnp.float32)
        return jnp.sum(attended.reshape(blocks, BLK, half), axis=1)

    here = block_sums(own_ref, r1_ref, r3_ref, odd, jnp.where(odd == 0, seq > 0, seq < last))
    there = block_sums(
        r1_ref, own_ref, r2_ref, 1 - odd, jnp.where(odd == 0, seq + 1 < last, seq > 1)
    )
    first = jnp.where(odd == 0, here, there)
    second = jnp.where(odd == 0, there, here)
    blank = jnp.zeros((SUB - 2 * blocks, half), jnp.float32)
    table = jnp.dot(jnp.concatenate([first, second, blank], axis=0), wc_ref[...], precision=HIGHEST)
    feature = fp_ref[...]
    none = jnp.zeros_like(feature)
    table = table[: 2 * blocks] + jnp.concatenate(
        [jnp.where(odd == 0, feature, none), jnp.where(odd == 0, none, feature)], axis=0
    )
    piece = jnp.concatenate([table[:, : E // 2], table[:, E // 2 :]], axis=0).astype(out_ref.dtype)
    out_ref[...] = jnp.broadcast_to(piece[None], out_ref.shape)


def tail_kernel(everyone_ref, mine_ref, last_ref, divisor_ref, derivative_ref, loss_ref):
    own_caps = derivative_ref.shape[0]
    devices, width, half = everyone_ref.shape
    caps = (mine_ref.shape[0] - BOUND_ROWS) // (E // LANES)
    sums = E // LANES * caps
    group = 2 * lax.axis_size("head")
    pairs = devices // group
    blocks = width // 2
    slot = lax.axis_index("seq") * lax.axis_size("head") + lax.axis_index("head")
    divisor = divisor_ref[0]

    total = mine_ref[...] + last_ref[...].astype(jnp.float32)
    raw = jnp.concatenate([total[c * caps : (c + 1) * caps] for c in range(E // LANES)], axis=1)

    def column(side):
        found = jnp.zeros((caps, LANES), jnp.float32)
        at = lax.broadcasted_iota(jnp.int32, (caps, LANES), 0) + side * caps
        lane = lax.broadcasted_iota(jnp.int32, (caps, LANES), 1)
        for r in range(-(-2 * caps // LANES)):
            line = total[sums + r : sums + r + 1]
            found = found + jnp.where(at == lane + r * LANES, line, 0.0)
        return jnp.sum(found, axis=1, keepdims=True)

    lower, upper = column(0), column(1)

    def unit(parts):
        mean = sum(jnp.sum(p * p, axis=-1, keepdims=True) for p in parts) * (1.0 / E)
        scale = lax.rsqrt(mean + 1e-06)
        parts = [(p * scale * E ** (-0.5)).astype(jnp.bfloat16) for p in parts]
        return parts[0] if len(parts) == 1 else jnp.concatenate(parts, axis=1)

    captions = unit([raw])
    sums = jnp.sum(
        everyone_ref[...].astype(jnp.float32).reshape(pairs, group, width, half), axis=1
    ).reshape(pairs * width, half)
    place = lax.broadcasted_iota(jnp.int32, (caps, pairs * width), 1)
    inner = place % width
    block = (place // width * blocks + inner % blocks).astype(jnp.float32)
    inside = (block >= lower) & (block < upper)
    pooled = [
        jnp.dot(
            jnp.where(inside & (inner // blocks == side), 1.0, 0.0), sums, precision=HIGHEST
        )
        for side in range(2)
    ]
    spans = unit(pooled)

    logits = transposed_dot(spans, captions) * divisor
    row_total = jnp.log(jnp.sum(jnp.exp(logits), axis=0, keepdims=True))
    tall = -(-own_caps // SUB) * SUB
    row = lax.broadcasted_iota(jnp.int32, (tall, caps), 0)
    marker = jnp.where(
        (row < own_caps) & (lax.broadcasted_iota(jnp.int32, (tall, caps), 1) == slot * own_caps + row),
        1.0,
        0.0,
    )
    own_spans = jnp.dot(
        marker.astype(jnp.bfloat16), spans, preferred_element_type=jnp.float32
    ).astype(jnp.bfloat16)
    own = transposed_dot(own_spans, captions) * divisor
    col_total = jnp.log(jnp.sum(jnp.exp(own), axis=1, keepdims=True))
    loss = 0.5 * (jnp.sum(marker * row_total, axis=1, keepdims=True) + col_total) - jnp.sum(
        marker * own, axis=1, keepdims=True
    )
    flip = lax.broadcasted_iota(jnp.int32, (tall, tall), 0) == lax.broadcasted_iota(
        jnp.int32, (tall, tall), 1
    )
    loss_ref[...] = jnp.sum(jnp.where(flip, loss, 0.0), axis=0, keepdims=True)[:, :own_caps]
    weights = (
        0.5 * jnp.exp(own - row_total) + 0.5 * jnp.exp(own - col_total) - marker
    ).astype(jnp.bfloat16)
    derivative = jnp.dot(weights, captions, preferred_element_type=jnp.float32) * divisor
    derivative_ref[...] = derivative[:own_caps]


def local(
    frames, norm_gain, w_qkv, w_out, w_proj, text_table, token_ids, span_bounds, contrast_divisor
):
    rows, width = frames.shape
    cols = w_qkv.shape[2]
    half = cols // 2
    seq_count, head_count = lax.axis_size("seq"), lax.axis_size("head")
    devices = seq_count * head_count
    own_caps = span_bounds.shape[0]
    blocks = rows // BLK
    shape = jax.ShapeDtypeStruct
    bf16, f32 = jnp.bfloat16, jnp.float32

    tall = E // LANES * token_ids.shape[0] + BOUND_ROWS
    given = (frames, norm_gain[None], w_qkv, token_ids.T, text_table, span_bounds)
    own, p1, p2, p3, mine, sent = call(
        first_kernel,
        [shape((n * rows, half), bf16) for n in (3, 3, 2, 2)]
        + [shape((tall, LANES), f32), shape((tall, LANES), bf16)],
        [HBM] * len(given),
        [
            pltpu.SMEM(a.shape, a.dtype) if a is span_bounds else pltpu.VMEM(a.shape, a.dtype)
            for a in given
        ]
        + [pltpu.VMEM(frames.shape, bf16), pltpu.SemaphoreType.DMA((8,))],
        (6 * rows * width * cols, 2 * w_qkv.size, 0),
    )(*[pltpu.with_memory_space_constraint(a, pltpu.HBM) for a in given])
    ends = seq_count - 1
    r1 = lax.ppermute(p1, "seq", [(s, s ^ 1) for s in range(seq_count)])
    r3 = lax.ppermute(
        p3,
        "seq",
        [(s, s + 1) for s in range(1, ends, 2)] + [(s, s - 1) for s in range(2, seq_count, 2)],
    )
    r2 = lax.ppermute(
        p2,
        "seq",
        [(s, s + 2) for s in range(1, ends - 1, 2)] + [(s, s - 2) for s in range(2, seq_count, 2)],
    )

    def swap(sent, seq_step, head_step):
        to = [
            (s ^ seq_step) * head_count + (h ^ head_step)
            for s in range(seq_count)
            for h in range(head_count)
        ]
        return lax.ppermute(sent, EVERY, list(enumerate(to)))

    def add(mine, *got):
        for g in got:
            mine = mine + g.astype(f32)
        return mine, mine.astype(bf16)

    got, r1 = lax.optimization_barrier((swap(sent, 0, 2), r1))
    mine, sent = add(mine, got)
    got = swap(sent, 1, 0)

    wc, fp = call(
        weights_kernel,
        [shape((half, E), f32), shape((blocks, E), f32)],
        [VMEM] * 3,
        cost=(10**10, 2 * (w_proj.size + w_out.size + frames.size), 0),
    )(frames, w_out, w_proj)

    piece = call(
        attend_kernel,
        shape((devices, 4 * blocks, E // 2), PIECE),
        [VMEM] * 6,
        cost=(10**10, 10 * rows * cols, 6 * rows * rows * cols // HDIM),
    )(own, r1, r2, r3, wc, fp)

    got, piece = lax.optimization_barrier((got, piece))
    mine, sent = add(mine, got)
    step = 2
    while step < seq_count:
        if 4 * step <= seq_count:
            mine, sent = add(mine, *[swap(sent, k * step, 0) for k in (1, 2, 3)])
            step *= 4
        else:
            mine, sent = add(mine, swap(sent, step, 0))
            step *= 2
    everyone = lax.all_to_all(piece, EVERY, 0, 0)
    got = swap(sent, 0, 1)

    derivative, loss = call(
        tail_kernel,
        [shape((own_caps, E), f32), shape((1, own_caps), f32)],
        [VMEM, VMEM, VMEM, SMEM],
        cost=(4 * E * token_ids.shape[0] ** 2, 2 * piece.size, 0),
    )(everyone, mine, got, contrast_divisor)
    return derivative, loss.reshape(own_caps)


def solution(mesh):
    placed = (
        P("seq", None),
        P(),
        P(None, None, "head"),
        P("head", None),
        P(),
        P(EVERY, None),
        P(),
        P(EVERY, None),
        P(),
    )
    return jax.shard_map(
        local,
        mesh=mesh,
        in_specs=placed,
        out_specs=(P(EVERY, None), P(EVERY)),
        check_vma=False,
    )
```

```python
import functools

import jax
import jax.numpy as jnp
from jax import lax
from jax.experimental import pallas as pl
from jax.experimental.pallas import tpu as pltpu
from jax.sharding import PartitionSpec as P

HDIM = 64
E = 512
BLK = 128
EVERY = ("seq", "head")
LANES = 128
SUB = 8
NEVER = -1e30
BOUND_ROWS = 16
PIECE = jnp.bfloat16
VMEM = pl.BlockSpec(memory_space=pltpu.VMEM)
SMEM = pl.BlockSpec(memory_space=pltpu.SMEM)
HBM = pl.BlockSpec(memory_space=pltpu.HBM)
HIGHEST = lax.Precision.HIGHEST


def call(body, outs, ins, scratch=(), cost=(0, 0, 0), mib=24):
    return pl.pallas_call(
        body,
        out_shape=outs,
        in_specs=ins,
        out_specs=jax.tree.map(lambda _: VMEM, outs),
        scratch_shapes=scratch,
        compiler_params=pltpu.CompilerParams(vmem_limit_bytes=mib << 20),
        cost_estimate=pl.CostEstimate(
            flops=cost[0], bytes_accessed=cost[1], transcendentals=cost[2]
        ),
    )


def transposed_dot(left, right):
    return lax.dot_general(
        left, right, (((1,), (1,)), ((), ())), preferred_element_type=jnp.float32
    )


def first_kernel(
    frames_hbm,
    gain_hbm,
    w_hbm,
    ids_hbm,
    table_hbm,
    bounds_hbm,
    own_ref,
    p1_ref,
    p2_ref,
    p3_ref,
    t32_ref,
    frames,
    gain,
    w,
    id_rows,
    table,
    bound,
    normed,
    sems,
):
    rows = frames.shape[0]
    half = own_ref.shape[1]
    parts = [(ids_hbm, id_rows), (frames_hbm, frames), (gain_hbm, gain)]
    parts += [(w_hbm.at[k], w.at[k]) for k in (1, 2, 0)]
    parts += [(table_hbm, table), (bounds_hbm, bound)]
    copies = [pltpu.make_async_copy(*part, sems.at[n]) for n, part in enumerate(parts)]
    for copy in copies:
        copy.start()
    odd = lax.axis_index("seq") % 2 == 1

    tokens, caps = id_rows.shape
    vocab = table.shape[0]
    own_caps = bound.shape[0]
    slot = lax.axis_index("seq") * lax.axis_size("head") + lax.axis_index("head")
    copies[0].wait()
    ids = (id_rows[...] - slot * vocab).T
    words = lax.broadcasted_iota(jnp.int32, (caps, vocab), 1)
    counts = jnp.zeros((caps, vocab), jnp.float32)
    for t in range(tokens):
        counts = counts + jnp.where(ids[:, t : t + 1] == words, 1.0, 0.0)
    counts = counts.astype(jnp.bfloat16)

    copies[1].wait()
    copies[2].wait()
    step = min(64, rows)
    for r in range(0, rows, step):
        part = frames[r : r + step].astype(jnp.float32)
        scale = lax.rsqrt(jnp.mean(part * part, axis=-1, keepdims=True) + 1e-05)
        normed[r : r + step] = (part * scale * gain[...]).astype(jnp.bfloat16)
    for n, k in enumerate((1, 2, 0)):
        copies[3 + n].wait()
        both = jnp.dot(normed[...], w[k], preferred_element_type=jnp.float32).astype(jnp.bfloat16)
        if k == 0:
            both = both * jnp.bfloat16(HDIM ** (-0.5))
        mine = jnp.where(odd, both[:, half:], both[:, :half])
        other = jnp.where(odd, both[:, :half], both[:, half:])
        own_ref[k * rows : (k + 1) * rows] = mine
        p1_ref[k * rows : (k + 1) * rows] = other
        if k > 0:
            p2_ref[(k - 1) * rows : k * rows] = mine
            p3_ref[(k - 1) * rows : k * rows] = other

    copies[6].wait()
    copies[7].wait()
    part = jnp.dot(counts, table[...], preferred_element_type=jnp.float32)
    row = lax.broadcasted_iota(jnp.int32, (BOUND_ROWS, LANES), 0)
    place = row * LANES + lax.broadcasted_iota(jnp.int32, (BOUND_ROWS, LANES), 1)
    bounds = jnp.zeros((BOUND_ROWS, LANES), jnp.float32)
    for c in range(own_caps):
        for side in range(2):
            block = (bound[c, side] // BLK).astype(jnp.float32)
            bounds = jnp.where(place == side * caps + slot * own_caps + c, block, bounds)
    sums = E // LANES * caps
    for c in range(E // LANES):
        chunk = part[:, c * LANES : (c + 1) * LANES]
        t32_ref[c * caps : (c + 1) * caps] = chunk
        p1_ref[3 * rows + c * caps : 3 * rows + (c + 1) * caps] = chunk.astype(jnp.bfloat16)
    t32_ref[sums:] = bounds
    p1_ref[3 * rows + sums :] = bounds.astype(jnp.bfloat16)


def weights_kernel(frames_ref, w_out_ref, w_proj_ref, wc_ref, fp_ref):
    half = wc_ref.shape[0]
    cols = w_out_ref.shape[0]
    blocks = fp_ref.shape[0]
    odd = lax.axis_index("seq") % 2
    start = pl.multiple_of(lax.axis_index("head") * cols, LANES)
    wc_ref[...] = jnp.dot(
        w_out_ref[pl.ds(pl.multiple_of(odd * half, half), half), :],
        w_proj_ref[...],
        preferred_element_type=jnp.float32,
    )
    features = frames_ref[:, pl.ds(start, cols)].astype(jnp.float32)
    sums = jnp.sum(features.reshape(blocks, BLK, cols), axis=1)
    padded = jnp.concatenate([sums, jnp.zeros((SUB - blocks, cols), jnp.float32)], axis=0)
    fp_ref[...] = jnp.dot(
        padded, w_proj_ref[pl.ds(start, cols), :].astype(jnp.float32), precision=HIGHEST
    )[:blocks]


def attend_kernel(own_ref, r1_ref, r2_ref, r3_ref, wc_ref, fp_ref, out_ref):
    rows = own_ref.shape[0] // 3
    half = own_ref.shape[1]
    blocks = rows // BLK
    seq, last = lax.axis_index("seq"), lax.axis_size("seq") - 1
    odd = seq % 2
    apart = lax.broadcasted_iota(jnp.int32, (rows, rows), 0) - lax.broadcasted_iota(
        jnp.int32, (rows, rows), 1
    )
    lane = lax.broadcasted_iota(jnp.int32, (rows, half), 1)

    def block_sums(me, other, halo, parity, exists):
        side = jnp.where(parity == 0, apart, -apart)
        near = side >= 0
        far = side <= jnp.where(exists, 0, -2 * rows)
        query = me[0:rows]
        attended = jnp.zeros((rows, half), jnp.float32)
        for head in range(half // HDIM):
            mine = lane // HDIM == head
            q = jnp.where(mine, query, jnp.zeros_like(query))
            scores = [
                transposed_dot(q, me[rows : 2 * rows]),
                jnp.where(near, transposed_dot(q, other[rows : 2 * rows]), NEVER),
                jnp.where(far, transposed_dot(q, halo[0:rows]), NEVER),
            ]
            top = functools.reduce(jnp.maximum, [jnp.max(s, axis=1, keepdims=True) for s in scores])
            probs = [jnp.exp(s - top) for s in scores]
            denom = sum(jnp.sum(p, axis=1, keepdims=True) for p in probs)
            values = (me[2 * rows : 3 * rows], other[2 * rows : 3 * rows], halo[rows : 2 * rows])
            mixed = sum(
                jnp.dot(p.astype(jnp.bfloat16), v, preferred_element_type=jnp.float32)
                for p, v in zip(probs, values)
            )
            attended = jnp.where(mine, mixed * (1.0 / denom), attended)
        attended = attended.astype(jnp.bfloat16).astype(jnp.float32)
        return jnp.sum(attended.reshape(blocks, BLK, half), axis=1)

    here = block_sums(own_ref, r1_ref, r3_ref, odd, jnp.where(odd == 0, seq > 0, seq < last))
    there = block_sums(
        r1_ref, own_ref, r2_ref, 1 - odd, jnp.where(odd == 0, seq + 1 < last, seq > 1)
    )
    first = jnp.where(odd == 0, here, there)
    second = jnp.where(odd == 0, there, here)
    blank = jnp.zeros((SUB - 2 * blocks, half), jnp.float32)
    table = jnp.dot(jnp.concatenate([first, second, blank], axis=0), wc_ref[...], precision=HIGHEST)
    feature = fp_ref[...]
    none = jnp.zeros_like(feature)
    table = table[: 2 * blocks] + jnp.concatenate(
        [jnp.where(odd == 0, feature, none), jnp.where(odd == 0, none, feature)], axis=0
    )
    piece = jnp.concatenate([table[:, : E // 2], table[:, E // 2 :]], axis=0).astype(out_ref.dtype)
    out_ref[...] = jnp.broadcast_to(piece[None], out_ref.shape)


def unit(parts):
    mean = sum(jnp.sum(p * p, axis=-1, keepdims=True) for p in parts) * (1.0 / E)
    scale = lax.rsqrt(mean + 1e-06)
    return jnp.concatenate(
        [(p * scale * E ** (-0.5)).astype(jnp.bfloat16) for p in parts], axis=1
    )


def caption_kernel(group, width, mine_ref, last_ref, captions_ref, masks_ref):
    caps = captions_ref.shape[0]
    sums = E // LANES * caps
    blocks = width // 2
    total = mine_ref[...] + last_ref[...].astype(jnp.float32)
    captions_ref[...] = unit([total[c * caps : (c + 1) * caps] for c in range(E // LANES)])

    def column(side):
        found = jnp.zeros((caps, LANES), jnp.float32)
        at = lax.broadcasted_iota(jnp.int32, (caps, LANES), 0) + side * caps
        lane = lax.broadcasted_iota(jnp.int32, (caps, LANES), 1)
        for r in range(-(-2 * caps // LANES)):
            line = total[sums + r : sums + r + 1]
            found = found + jnp.where(at == lane + r * LANES, line, 0.0)
        return jnp.sum(found, axis=1, keepdims=True)

    lower, upper = column(0), column(1)
    place = lax.broadcasted_iota(jnp.int32, (caps, masks_ref.shape[1]), 1)
    inner = place % width
    block = (place // (width * group) * blocks + inner % blocks).astype(jnp.float32)
    inside = jnp.where((block >= lower) & (block < upper), 1.0, 0.0)
    for side in range(2):
        masks_ref[side * caps : (side + 1) * caps] = jnp.where(
            inner // blocks == side, inside, 0.0
        ).astype(jnp.bfloat16)


def tail_kernel(everyone_ref, captions_ref, masks_ref, divisor_ref, derivative_ref, loss_ref):
    own_caps = derivative_ref.shape[0]
    devices, width, half = everyone_ref.shape
    caps = captions_ref.shape[0]
    slot = lax.axis_index("seq") * lax.axis_size("head") + lax.axis_index("head")
    divisor = divisor_ref[0]
    captions = captions_ref[...]
    pieces = everyone_ref[...].reshape(devices * width, half)
    pooled = jnp.dot(masks_ref[...], pieces, preferred_element_type=jnp.float32)
    spans = unit([pooled[:caps], pooled[caps:]])

    logits = transposed_dot(spans, captions) * divisor
    row_total = jnp.log(jnp.sum(jnp.exp(logits), axis=0, keepdims=True))
    tall = -(-own_caps // SUB) * SUB
    row = lax.broadcasted_iota(jnp.int32, (tall, caps), 0)
    marker = jnp.where(
        (row < own_caps) & (lax.broadcasted_iota(jnp.int32, (tall, caps), 1) == slot * own_caps + row),
        1.0,
        0.0,
    )
    own_spans = jnp.dot(
        marker.astype(jnp.bfloat16), spans, preferred_element_type=jnp.float32
    ).astype(jnp.bfloat16)
    own = transposed_dot(own_spans, captions) * divisor
    col_total = jnp.log(jnp.sum(jnp.exp(own), axis=1, keepdims=True))
    loss = 0.5 * (jnp.sum(marker * row_total, axis=1, keepdims=True) + col_total) - jnp.sum(
        marker * own, axis=1, keepdims=True
    )
    flip = lax.broadcasted_iota(jnp.int32, (tall, tall), 0) == lax.broadcasted_iota(
        jnp.int32, (tall, tall), 1
    )
    loss_ref[...] = jnp.sum(jnp.where(flip, loss, 0.0), axis=0, keepdims=True)[:, :own_caps]
    weights = (
        0.5 * jnp.exp(own - row_total) + 0.5 * jnp.exp(own - col_total) - marker
    ).astype(jnp.bfloat16)
    derivative = jnp.dot(weights, captions, preferred_element_type=jnp.float32) * divisor
    derivative_ref[...] = derivative[:own_caps]


def local(
    frames, norm_gain, w_qkv, w_out, w_proj, text_table, token_ids, span_bounds, contrast_divisor
):
    rows, width = frames.shape
    cols = w_qkv.shape[2]
    half = cols // 2
    seq_count, head_count = lax.axis_size("seq"), lax.axis_size("head")
    devices = seq_count * head_count
    own_caps = span_bounds.shape[0]
    blocks = rows // BLK
    shape = jax.ShapeDtypeStruct
    bf16, f32 = jnp.bfloat16, jnp.float32

    tall = E // LANES * token_ids.shape[0] + BOUND_ROWS
    given = (frames, norm_gain[None], w_qkv, token_ids.T, text_table, span_bounds)
    own, p1, p2, p3, mine = call(
        first_kernel,
        [shape((n, half), bf16) for n in (3 * rows, 3 * rows + tall, 2 * rows, 2 * rows)]
        + [shape((tall, LANES), f32)],
        [HBM] * len(given),
        [
            pltpu.SMEM(a.shape, a.dtype) if a is span_bounds else pltpu.VMEM(a.shape, a.dtype)
            for a in given
        ]
        + [pltpu.VMEM(frames.shape, bf16), pltpu.SemaphoreType.DMA((8,))],
        (6 * rows * width * cols, 2 * w_qkv.size, 0),
    )(*[pltpu.with_memory_space_constraint(a, pltpu.HBM) for a in given])
    ends = seq_count - 1
    r1 = lax.ppermute(p1, "seq", [(s, s ^ 1) for s in range(seq_count)])
    r3 = lax.ppermute(
        p3,
        "seq",
        [(s, s + 1) for s in range(1, ends, 2)] + [(s, s - 1) for s in range(2, seq_count, 2)],
    )
    r2 = lax.ppermute(
        p2,
        "seq",
        [(s, s + 2) for s in range(1, ends - 1, 2)] + [(s, s - 2) for s in range(2, seq_count, 2)],
    )

    def swap(sent, seq_step, head_step):
        to = [
            (s ^ seq_step) * head_count + (h ^ head_step)
            for s in range(seq_count)
            for h in range(head_count)
        ]
        return lax.ppermute(sent, EVERY, list(enumerate(to)))

    def add(mine, *got):
        for g in got:
            mine = mine + g.astype(f32)
        return mine, mine.astype(bf16)

    mine, sent = add(mine, r1[3 * rows :])
    got = swap(sent, 0, 2)

    wc, fp = call(
        weights_kernel,
        [shape((half, E), f32), shape((blocks, E), f32)],
        [VMEM] * 3,
        cost=(10**10, 2 * (w_proj.size + w_out.size + frames.size), 0),
    )(frames, w_out, w_proj)

    piece = call(
        attend_kernel,
        shape((devices, 4 * blocks, E // 2), PIECE),
        [VMEM] * 6,
        cost=(10**10, 10 * rows * cols, 6 * rows * rows * cols // HDIM),
    )(own, r1, r2, r3, wc, fp)

    got, piece = lax.optimization_barrier((got, piece))
    mine, sent = add(mine, got)
    step = 2
    while step < seq_count:
        if 4 * step <= seq_count:
            mine, sent = add(mine, *[swap(sent, k * step, 0) for k in (1, 2, 3)])
            step *= 4
        else:
            mine, sent = add(mine, swap(sent, step, 0))
            step *= 2
    everyone = lax.all_to_all(piece, EVERY, 0, 0)
    got = swap(sent, 0, 1)

    captions, masks = call(
        functools.partial(caption_kernel, 2 * head_count, 4 * blocks),
        [
            shape((token_ids.shape[0], E), bf16),
            shape((2 * token_ids.shape[0], devices * 4 * blocks), bf16),
        ],
        [VMEM] * 2,
    )(mine, got)
    derivative, loss = call(
        tail_kernel,
        [shape((own_caps, E), f32), shape((1, own_caps), f32)],
        [VMEM, VMEM, VMEM, SMEM],
        cost=(4 * E * token_ids.shape[0] ** 2, 2 * piece.size, 0),
    )(everyone, captions, masks, contrast_divisor)
    return derivative, loss.reshape(own_caps)


def solution(mesh):
    placed = (
        P("seq", None),
        P(),
        P(None, None, "head"),
        P("head", None),
        P(),
        P(EVERY, None),
        P(),
        P(EVERY, None),
        P(),
    )
    return jax.shard_map(
        local,
        mesh=mesh,
        in_specs=placed,
        out_specs=(P(EVERY, None), P(EVERY)),
        check_vma=False,
    )
```

```python
import functools

import jax
import jax.numpy as jnp
from jax import lax
from jax.experimental import pallas as pl
from jax.experimental.pallas import tpu as pltpu
from jax.sharding import PartitionSpec as P

HDIM = 64
E = 512
BLK = 128
EVERY = ("seq", "head")
LANES = 128
SUB = 8
NEVER = -1e30
BOUND_ROWS = 16
PIECE = jnp.bfloat16
VMEM = pl.BlockSpec(memory_space=pltpu.VMEM)
SMEM = pl.BlockSpec(memory_space=pltpu.SMEM)
HBM = pl.BlockSpec(memory_space=pltpu.HBM)
HIGHEST = lax.Precision.HIGHEST


def call(body, outs, ins, scratch=(), cost=(0, 0, 0), mib=24):
    return pl.pallas_call(
        body,
        out_shape=outs,
        in_specs=ins,
        out_specs=jax.tree.map(lambda _: VMEM, outs),
        scratch_shapes=scratch,
        compiler_params=pltpu.CompilerParams(vmem_limit_bytes=mib << 20),
        cost_estimate=pl.CostEstimate(
            flops=cost[0], bytes_accessed=cost[1], transcendentals=cost[2]
        ),
    )


def transposed_dot(left, right):
    return lax.dot_general(
        left, right, (((1,), (1,)), ((), ())), preferred_element_type=jnp.float32
    )


def first_kernel(
    frames_hbm,
    gain_hbm,
    w_hbm,
    ids_hbm,
    table_hbm,
    bounds_hbm,
    own_ref,
    p1_ref,
    p2_ref,
    p3_ref,
    t32_ref,
    frames,
    gain,
    w,
    id_rows,
    table,
    bound,
    normed,
    sems,
):
    rows = frames.shape[0]
    half = own_ref.shape[1]
    parts = [(ids_hbm, id_rows), (frames_hbm, frames), (gain_hbm, gain)]
    parts += [(w_hbm.at[k], w.at[k]) for k in (1, 2, 0)]
    parts += [(table_hbm, table), (bounds_hbm, bound)]
    copies = [pltpu.make_async_copy(*part, sems.at[n]) for n, part in enumerate(parts)]
    for copy in copies:
        copy.start()
    odd = lax.axis_index("seq") % 2 == 1

    tokens, caps = id_rows.shape
    vocab = table.shape[0]
    own_caps = bound.shape[0]
    slot = lax.axis_index("seq") * lax.axis_size("head") + lax.axis_index("head")
    copies[0].wait()
    ids = (id_rows[...] - slot * vocab).T
    words = lax.broadcasted_iota(jnp.int32, (caps, vocab), 1)
    counts = jnp.zeros((caps, vocab), jnp.float32)
    for t in range(tokens):
        counts = counts + jnp.where(ids[:, t : t + 1] == words, 1.0, 0.0)
    counts = counts.astype(jnp.bfloat16)

    copies[1].wait()
    copies[2].wait()
    step = min(64, rows)
    for r in range(0, rows, step):
        part = frames[r : r + step].astype(jnp.float32)
        scale = lax.rsqrt(jnp.mean(part * part, axis=-1, keepdims=True) + 1e-05)
        normed[r : r + step] = (part * scale * gain[...]).astype(jnp.bfloat16)
    for n, k in enumerate((1, 2, 0)):
        copies[3 + n].wait()
        both = jnp.dot(normed[...], w[k], preferred_element_type=jnp.float32).astype(jnp.bfloat16)
        if k == 0:
            both = both * jnp.bfloat16(HDIM ** (-0.5))
        mine = jnp.where(odd, both[:, half:], both[:, :half])
        other = jnp.where(odd, both[:, :half], both[:, half:])
        own_ref[k * rows : (k + 1) * rows] = mine
        p1_ref[k * rows : (k + 1) * rows] = other
        if k > 0:
            p2_ref[(k - 1) * rows : k * rows] = mine
            p3_ref[(k - 1) * rows : k * rows] = other

    copies[6].wait()
    copies[7].wait()
    part = jnp.dot(counts, table[...], preferred_element_type=jnp.float32)
    row = lax.broadcasted_iota(jnp.int32, (BOUND_ROWS, LANES), 0)
    place = row * LANES + lax.broadcasted_iota(jnp.int32, (BOUND_ROWS, LANES), 1)
    bounds = jnp.zeros((BOUND_ROWS, LANES), jnp.float32)
    for c in range(own_caps):
        for side in range(2):
            block = (bound[c, side] // BLK).astype(jnp.float32)
            bounds = jnp.where(place == side * caps + slot * own_caps + c, block, bounds)
    sums = E // LANES * caps
    for c in range(E // LANES):
        chunk = part[:, c * LANES : (c + 1) * LANES]
        t32_ref[c * caps : (c + 1) * caps] = chunk
        p1_ref[3 * rows + c * caps : 3 * rows + (c + 1) * caps] = chunk.astype(jnp.bfloat16)
    t32_ref[sums:] = bounds
    p1_ref[3 * rows + sums :] = bounds.astype(jnp.bfloat16)


def weights_kernel(frames_ref, w_out_ref, w_proj_ref, wc_ref, fp_ref):
    half = wc_ref.shape[0]
    cols = w_out_ref.shape[0]
    blocks = fp_ref.shape[0]
    odd = lax.axis_index("seq") % 2
    start = pl.multiple_of(lax.axis_index("head") * cols, LANES)
    wc_ref[...] = jnp.dot(
        w_out_ref[pl.ds(pl.multiple_of(odd * half, half), half), :],
        w_proj_ref[...],
        preferred_element_type=jnp.float32,
    )
    features = frames_ref[:, pl.ds(start, cols)].astype(jnp.float32)
    sums = jnp.sum(features.reshape(blocks, BLK, cols), axis=1)
    padded = jnp.concatenate([sums, jnp.zeros((SUB - blocks, cols), jnp.float32)], axis=0)
    fp_ref[...] = jnp.dot(
        padded, w_proj_ref[pl.ds(start, cols), :].astype(jnp.float32), precision=HIGHEST
    )[:blocks]


def attend_kernel(own_ref, r1_ref, r2_ref, r3_ref, wc_ref, fp_ref, out_ref):
    rows = own_ref.shape[0] // 3
    half = own_ref.shape[1]
    blocks = rows // BLK
    seq, last = lax.axis_index("seq"), lax.axis_size("seq") - 1
    odd = seq % 2
    apart = lax.broadcasted_iota(jnp.int32, (rows, rows), 0) - lax.broadcasted_iota(
        jnp.int32, (rows, rows), 1
    )
    lane = lax.broadcasted_iota(jnp.int32, (rows, half), 1)

    def block_sums(me, other, halo, parity, exists):
        side = jnp.where(parity == 0, apart, -apart)
        near = side >= 0
        far = side <= jnp.where(exists, 0, -2 * rows)
        query = me[0:rows]
        attended = jnp.zeros((rows, half), jnp.float32)
        for head in range(half // HDIM):
            mine = lane // HDIM == head
            q = jnp.where(mine, query, jnp.zeros_like(query))
            scores = [
                transposed_dot(q, me[rows : 2 * rows]),
                jnp.where(near, transposed_dot(q, other[rows : 2 * rows]), NEVER),
                jnp.where(far, transposed_dot(q, halo[0:rows]), NEVER),
            ]
            top = functools.reduce(jnp.maximum, [jnp.max(s, axis=1, keepdims=True) for s in scores])
            probs = [jnp.exp(s - top) for s in scores]
            denom = sum(jnp.sum(p, axis=1, keepdims=True) for p in probs)
            values = (me[2 * rows : 3 * rows], other[2 * rows : 3 * rows], halo[rows : 2 * rows])
            mixed = sum(
                jnp.dot(p.astype(jnp.bfloat16), v, preferred_element_type=jnp.float32)
                for p, v in zip(probs, values)
            )
            attended = jnp.where(mine, mixed * (1.0 / denom), attended)
        attended = attended.astype(jnp.bfloat16).astype(jnp.float32)
        return jnp.sum(attended.reshape(blocks, BLK, half), axis=1)

    here = block_sums(own_ref, r1_ref, r3_ref, odd, jnp.where(odd == 0, seq > 0, seq < last))
    there = block_sums(
        r1_ref, own_ref, r2_ref, 1 - odd, jnp.where(odd == 0, seq + 1 < last, seq > 1)
    )
    first = jnp.where(odd == 0, here, there)
    second = jnp.where(odd == 0, there, here)
    blank = jnp.zeros((SUB - 2 * blocks, half), jnp.float32)
    table = jnp.dot(jnp.concatenate([first, second, blank], axis=0), wc_ref[...], precision=HIGHEST)
    feature = fp_ref[...]
    none = jnp.zeros_like(feature)
    table = table[: 2 * blocks] + jnp.concatenate(
        [jnp.where(odd == 0, feature, none), jnp.where(odd == 0, none, feature)], axis=0
    )
    piece = jnp.concatenate([table[:, : E // 2], table[:, E // 2 :]], axis=0).astype(out_ref.dtype)
    out_ref[...] = jnp.broadcast_to(piece[None], out_ref.shape)


def unit(parts):
    mean = sum(jnp.sum(p * p, axis=-1, keepdims=True) for p in parts) * (1.0 / E)
    scale = lax.rsqrt(mean + 1e-06)
    return jnp.concatenate(
        [(p * scale * E ** (-0.5)).astype(jnp.bfloat16) for p in parts], axis=1
    )


def caption_kernel(group, width, mine_ref, *refs):
    *got_refs, captions_ref, masks_ref = refs
    caps = captions_ref.shape[0]
    sums = E // LANES * caps
    blocks = width // 2
    total = mine_ref[...] + sum(ref[...].astype(jnp.float32) for ref in got_refs)
    captions_ref[...] = unit([total[c * caps : (c + 1) * caps] for c in range(E // LANES)])

    def column(side):
        found = jnp.zeros((caps, LANES), jnp.float32)
        at = lax.broadcasted_iota(jnp.int32, (caps, LANES), 0) + side * caps
        lane = lax.broadcasted_iota(jnp.int32, (caps, LANES), 1)
        for r in range(-(-2 * caps // LANES)):
            line = total[sums + r : sums + r + 1]
            found = found + jnp.where(at == lane + r * LANES, line, 0.0)
        return jnp.sum(found, axis=1, keepdims=True)

    lower, upper = column(0), column(1)
    place = lax.broadcasted_iota(jnp.int32, (caps, masks_ref.shape[1]), 1)
    inner = place % width
    block = (place // (width * group) * blocks + inner % blocks).astype(jnp.float32)
    inside = jnp.where((block >= lower) & (block < upper), 1.0, 0.0)
    for side in range(2):
        masks_ref[side * caps : (side + 1) * caps] = jnp.where(
            inner // blocks == side, inside, 0.0
        ).astype(jnp.bfloat16)


def tail_kernel(everyone_ref, captions_ref, masks_ref, divisor_ref, derivative_ref, loss_ref):
    own_caps = derivative_ref.shape[0]
    devices, width, half = everyone_ref.shape
    caps = captions_ref.shape[0]
    slot = lax.axis_index("seq") * lax.axis_size("head") + lax.axis_index("head")
    divisor = divisor_ref[0]
    captions = captions_ref[...]
    pieces = everyone_ref[...].reshape(devices * width, half)
    pooled = jnp.dot(masks_ref[...], pieces, preferred_element_type=jnp.float32)
    spans = unit([pooled[:caps], pooled[caps:]])

    logits = transposed_dot(spans, captions) * divisor
    row_total = jnp.log(jnp.sum(jnp.exp(logits), axis=0, keepdims=True))
    tall = -(-own_caps // SUB) * SUB
    row = lax.broadcasted_iota(jnp.int32, (tall, caps), 0)
    marker = jnp.where(
        (row < own_caps) & (lax.broadcasted_iota(jnp.int32, (tall, caps), 1) == slot * own_caps + row),
        1.0,
        0.0,
    )
    own_spans = jnp.dot(
        marker.astype(jnp.bfloat16), spans, preferred_element_type=jnp.float32
    ).astype(jnp.bfloat16)
    own = transposed_dot(own_spans, captions) * divisor
    col_total = jnp.log(jnp.sum(jnp.exp(own), axis=1, keepdims=True))
    loss = 0.5 * (jnp.sum(marker * row_total, axis=1, keepdims=True) + col_total) - jnp.sum(
        marker * own, axis=1, keepdims=True
    )
    flip = lax.broadcasted_iota(jnp.int32, (tall, tall), 0) == lax.broadcasted_iota(
        jnp.int32, (tall, tall), 1
    )
    loss_ref[...] = jnp.sum(jnp.where(flip, loss, 0.0), axis=0, keepdims=True)[:, :own_caps]
    weights = (
        0.5 * jnp.exp(own - row_total) + 0.5 * jnp.exp(own - col_total) - marker
    ).astype(jnp.bfloat16)
    derivative = jnp.dot(weights, captions, preferred_element_type=jnp.float32) * divisor
    derivative_ref[...] = derivative[:own_caps]


def local(
    frames, norm_gain, w_qkv, w_out, w_proj, text_table, token_ids, span_bounds, contrast_divisor
):
    rows, width = frames.shape
    cols = w_qkv.shape[2]
    half = cols // 2
    seq_count, head_count = lax.axis_size("seq"), lax.axis_size("head")
    devices = seq_count * head_count
    own_caps = span_bounds.shape[0]
    blocks = rows // BLK
    shape = jax.ShapeDtypeStruct
    bf16, f32 = jnp.bfloat16, jnp.float32

    tall = E // LANES * token_ids.shape[0] + BOUND_ROWS
    given = (frames, norm_gain[None], w_qkv, token_ids.T, text_table, span_bounds)
    own, p1, p2, p3, mine = call(
        first_kernel,
        [shape((n, half), bf16) for n in (3 * rows, 3 * rows + tall, 2 * rows, 2 * rows)]
        + [shape((tall, LANES), f32)],
        [HBM] * len(given),
        [
            pltpu.SMEM(a.shape, a.dtype) if a is span_bounds else pltpu.VMEM(a.shape, a.dtype)
            for a in given
        ]
        + [pltpu.VMEM(frames.shape, bf16), pltpu.SemaphoreType.DMA((8,))],
        (6 * rows * width * cols, 2 * w_qkv.size, 0),
    )(*[pltpu.with_memory_space_constraint(a, pltpu.HBM) for a in given])
    ends = seq_count - 1
    r1 = lax.ppermute(p1, "seq", [(s, s ^ 1) for s in range(seq_count)])
    r3 = lax.ppermute(
        p3,
        "seq",
        [(s, s + 1) for s in range(1, ends, 2)] + [(s, s - 1) for s in range(2, seq_count, 2)],
    )
    r2 = lax.ppermute(
        p2,
        "seq",
        [(s, s + 2) for s in range(1, ends - 1, 2)] + [(s, s - 2) for s in range(2, seq_count, 2)],
    )

    def swap(sent, seq_step, head_step):
        to = [
            (s ^ seq_step) * head_count + (h ^ head_step)
            for s in range(seq_count)
            for h in range(head_count)
        ]
        return lax.ppermute(sent, EVERY, list(enumerate(to)))

    def add(mine, *got):
        for g in got:
            mine = mine + g.astype(f32)
        return mine, mine.astype(bf16)

    mine, sent = add(mine, r1[3 * rows :])
    got = swap(sent, 2, 0)

    wc, fp = call(
        weights_kernel,
        [shape((half, E), f32), shape((blocks, E), f32)],
        [VMEM] * 3,
        cost=(10**10, 2 * (w_proj.size + w_out.size + frames.size), 0),
    )(frames, w_out, w_proj)

    piece = call(
        attend_kernel,
        shape((devices, 4 * blocks, E // 2), PIECE),
        [VMEM] * 6,
        cost=(10**10, 10 * rows * cols, 6 * rows * rows * cols // HDIM),
    )(own, r1, r2, r3, wc, fp)

    got, piece = lax.optimization_barrier((got, piece))
    mine, sent = add(mine, got)
    step = 4
    while step < seq_count:
        mine, sent = add(mine, swap(sent, step, 0))
        step *= 2
    everyone = lax.all_to_all(piece, EVERY, 0, 0)
    gots = [swap(sent, 0, k) for k in range(1, head_count)]

    captions, masks = call(
        functools.partial(caption_kernel, 2 * head_count, 4 * blocks),
        [
            shape((token_ids.shape[0], E), bf16),
            shape((2 * token_ids.shape[0], devices * 4 * blocks), bf16),
        ],
        [VMEM] * head_count,
    )(mine, *gots)
    derivative, loss = call(
        tail_kernel,
        [shape((own_caps, E), f32), shape((1, own_caps), f32)],
        [VMEM, VMEM, VMEM, SMEM],
        cost=(4 * E * token_ids.shape[0] ** 2, 2 * piece.size, 0),
    )(everyone, captions, masks, contrast_divisor)
    return derivative, loss.reshape(own_caps)


def solution(mesh):
    placed = (
        P("seq", None),
        P(),
        P(None, None, "head"),
        P("head", None),
        P(),
        P(EVERY, None),
        P(),
        P(EVERY, None),
        P(),
    )
    return jax.shard_map(
        local,
        mesh=mesh,
        in_specs=placed,
        out_specs=(P(EVERY, None), P(EVERY)),
        check_vma=False,
    )
```

```python
import functools

import jax
import jax.numpy as jnp
from jax import lax
from jax.experimental import pallas as pl
from jax.experimental.pallas import tpu as pltpu
from jax.sharding import PartitionSpec as P

HDIM = 64
E = 512
BLK = 128
EVERY = ("seq", "head")
LANES = 128
SUB = 8
NEVER = -1e30
BOUND_ROWS = 16
PIECE = jnp.bfloat16
VMEM = pl.BlockSpec(memory_space=pltpu.VMEM)
SMEM = pl.BlockSpec(memory_space=pltpu.SMEM)
HBM = pl.BlockSpec(memory_space=pltpu.HBM)
HIGHEST = lax.Precision.HIGHEST


def call(body, outs, ins, scratch=(), cost=(0, 0, 0), mib=24):
    return pl.pallas_call(
        body,
        out_shape=outs,
        in_specs=ins,
        out_specs=jax.tree.map(lambda _: VMEM, outs),
        scratch_shapes=scratch,
        compiler_params=pltpu.CompilerParams(vmem_limit_bytes=mib << 20),
        cost_estimate=pl.CostEstimate(
            flops=cost[0], bytes_accessed=cost[1], transcendentals=cost[2]
        ),
    )


def transposed_dot(left, right):
    return lax.dot_general(
        left, right, (((1,), (1,)), ((), ())), preferred_element_type=jnp.float32
    )


def first_kernel(
    frames_hbm,
    gain_hbm,
    w_hbm,
    ids_hbm,
    table_hbm,
    bounds_hbm,
    own_ref,
    p1_ref,
    p2_ref,
    p3_ref,
    t32_ref,
    frames,
    gain,
    w,
    id_rows,
    table,
    bound,
    normed,
    sems,
):
    rows = frames.shape[0]
    half = own_ref.shape[1]
    parts = [(ids_hbm, id_rows), (frames_hbm, frames), (gain_hbm, gain)]
    parts += [(w_hbm.at[k], w.at[k]) for k in (1, 2, 0)]
    parts += [(table_hbm, table), (bounds_hbm, bound)]
    copies = [pltpu.make_async_copy(*part, sems.at[n]) for n, part in enumerate(parts)]
    for n in (0, 1, 2, 3, 4, 6, 5, 7):
        copies[n].start()
    odd = lax.axis_index("seq") % 2 == 1

    tokens, caps = id_rows.shape
    vocab = table.shape[0]
    own_caps = bound.shape[0]
    slot = lax.axis_index("seq") * lax.axis_size("head") + lax.axis_index("head")
    copies[0].wait()
    ids = (id_rows[...] - slot * vocab).T
    words = lax.broadcasted_iota(jnp.int32, (caps, vocab), 1)
    counts = jnp.zeros((caps, vocab), jnp.float32)
    for t in range(tokens):
        counts = counts + jnp.where(ids[:, t : t + 1] == words, 1.0, 0.0)
    counts = counts.astype(jnp.bfloat16)

    copies[1].wait()
    copies[2].wait()
    step = min(64, rows)
    for r in range(0, rows, step):
        part = frames[r : r + step].astype(jnp.float32)
        scale = lax.rsqrt(jnp.mean(part * part, axis=-1, keepdims=True) + 1e-05)
        normed[r : r + step] = (part * scale * gain[...]).astype(jnp.bfloat16)
    def project(n, k):
        copies[3 + n].wait()
        both = jnp.dot(normed[...], w[k], preferred_element_type=jnp.float32).astype(jnp.bfloat16)
        if k == 0:
            both = both * jnp.bfloat16(HDIM ** (-0.5))
        mine = jnp.where(odd, both[:, half:], both[:, :half])
        other = jnp.where(odd, both[:, :half], both[:, half:])
        own_ref[k * rows : (k + 1) * rows] = mine
        p1_ref[k * rows : (k + 1) * rows] = other
        if k > 0:
            p2_ref[(k - 1) * rows : k * rows] = mine
            p3_ref[(k - 1) * rows : k * rows] = other

    project(0, 1)
    project(1, 2)
    copies[6].wait()
    copies[7].wait()
    part = jnp.dot(counts, table[...], preferred_element_type=jnp.float32)
    row = lax.broadcasted_iota(jnp.int32, (BOUND_ROWS, LANES), 0)
    place = row * LANES + lax.broadcasted_iota(jnp.int32, (BOUND_ROWS, LANES), 1)
    bounds = jnp.zeros((BOUND_ROWS, LANES), jnp.float32)
    for c in range(own_caps):
        for side in range(2):
            block = (bound[c, side] // BLK).astype(jnp.float32)
            bounds = jnp.where(place == side * caps + slot * own_caps + c, block, bounds)
    sums = E // LANES * caps
    for c in range(E // LANES):
        chunk = part[:, c * LANES : (c + 1) * LANES]
        t32_ref[c * caps : (c + 1) * caps] = chunk
        p1_ref[3 * rows + c * caps : 3 * rows + (c + 1) * caps] = chunk.astype(jnp.bfloat16)
    t32_ref[sums:] = bounds
    p1_ref[3 * rows + sums :] = bounds.astype(jnp.bfloat16)
    project(2, 0)


def weights_kernel(frames_ref, w_out_ref, w_proj_ref, wc_ref, fp_ref):
    half = wc_ref.shape[0] // 2
    cols = w_out_ref.shape[0]
    blocks = fp_ref.shape[0]
    odd = lax.axis_index("seq") % 2
    start = pl.multiple_of(lax.axis_index("head") * cols, LANES)
    product = jnp.dot(
        w_out_ref[pl.ds(pl.multiple_of(odd * half, half), half), :],
        w_proj_ref[...],
        preferred_element_type=jnp.float32,
    )
    high = product.astype(jnp.bfloat16)
    wc_ref[:half] = high
    wc_ref[half:] = (product - high.astype(jnp.float32)).astype(jnp.bfloat16)
    features = frames_ref[:, pl.ds(start, cols)].astype(jnp.float32)
    sums = jnp.sum(features.reshape(blocks, BLK, cols), axis=1)
    padded = jnp.concatenate([sums, jnp.zeros((SUB - blocks, cols), jnp.float32)], axis=0)
    fp_ref[...] = jnp.dot(
        padded, w_proj_ref[pl.ds(start, cols), :].astype(jnp.float32), precision=HIGHEST
    )[:blocks]


def attend_kernel(own_ref, r1_ref, r2_ref, r3_ref, wc_ref, fp_ref, out_ref):
    rows = own_ref.shape[0] // 3
    half = own_ref.shape[1]
    blocks = rows // BLK
    seq, last = lax.axis_index("seq"), lax.axis_size("seq") - 1
    odd = seq % 2
    apart = lax.broadcasted_iota(jnp.int32, (rows, rows), 0) - lax.broadcasted_iota(
        jnp.int32, (rows, rows), 1
    )
    lane = lax.broadcasted_iota(jnp.int32, (rows, half), 1)

    def block_sums(me, other, halo, parity, exists):
        side = jnp.where(parity == 0, apart, -apart)
        near = side >= 0
        far = side <= jnp.where(exists, 0, -2 * rows)
        query = me[0:rows]
        attended = jnp.zeros((rows, half), jnp.float32)
        for head in range(half // HDIM):
            mine = lane // HDIM == head
            q = jnp.where(mine, query, jnp.zeros_like(query))
            scores = [
                transposed_dot(q, me[rows : 2 * rows]),
                jnp.where(near, transposed_dot(q, other[rows : 2 * rows]), NEVER),
                jnp.where(far, transposed_dot(q, halo[0:rows]), NEVER),
            ]
            top = functools.reduce(jnp.maximum, [jnp.max(s, axis=1, keepdims=True) for s in scores])
            probs = [jnp.exp(s - top) for s in scores]
            denom = sum(jnp.sum(p, axis=1, keepdims=True) for p in probs)
            values = (me[2 * rows : 3 * rows], other[2 * rows : 3 * rows], halo[rows : 2 * rows])
            mixed = sum(
                jnp.dot(p.astype(jnp.bfloat16), v, preferred_element_type=jnp.float32)
                for p, v in zip(probs, values)
            )
            attended = jnp.where(mine, mixed * (1.0 / denom), attended)
        attended = attended.astype(jnp.bfloat16).astype(jnp.float32)
        return jnp.sum(attended.reshape(blocks, BLK, half), axis=1)

    here = block_sums(own_ref, r1_ref, r3_ref, odd, jnp.where(odd == 0, seq > 0, seq < last))
    there = block_sums(
        r1_ref, own_ref, r2_ref, 1 - odd, jnp.where(odd == 0, seq + 1 < last, seq > 1)
    )
    first = jnp.where(odd == 0, here, there)
    second = jnp.where(odd == 0, there, here)
    blank = jnp.zeros((SUB - 2 * blocks, half), jnp.float32)
    sums = jnp.concatenate([first, second, blank], axis=0)
    high = sums.astype(jnp.bfloat16)
    low = (sums - high.astype(jnp.float32)).astype(jnp.bfloat16)
    both = jnp.concatenate([high, low], axis=0)
    table = jnp.dot(both, wc_ref[:half], preferred_element_type=jnp.float32)
    table = table[:SUB] + table[SUB:] + jnp.dot(
        high, wc_ref[half:], preferred_element_type=jnp.float32
    )
    feature = fp_ref[...]
    none = jnp.zeros_like(feature)
    table = table[: 2 * blocks] + jnp.concatenate(
        [jnp.where(odd == 0, feature, none), jnp.where(odd == 0, none, feature)], axis=0
    )
    piece = jnp.concatenate([table[:, : E // 2], table[:, E // 2 :]], axis=0).astype(out_ref.dtype)
    out_ref[...] = jnp.broadcast_to(piece[None], out_ref.shape)


def unit(parts):
    mean = sum(jnp.sum(p * p, axis=-1, keepdims=True) for p in parts) * (1.0 / E)
    scale = lax.rsqrt(mean + 1e-06)
    return jnp.concatenate(
        [(p * scale * E ** (-0.5)).astype(jnp.bfloat16) for p in parts], axis=1
    )


def caption_kernel(group, width, mine_ref, *refs):
    *got_refs, captions_ref, masks_ref = refs
    caps = captions_ref.shape[0]
    sums = E // LANES * caps
    blocks = width // 2
    total = mine_ref[...] + sum(ref[...].astype(jnp.float32) for ref in got_refs)
    captions_ref[...] = unit([total[c * caps : (c + 1) * caps] for c in range(E // LANES)])

    def column(side):
        found = jnp.zeros((caps, LANES), jnp.float32)
        at = lax.broadcasted_iota(jnp.int32, (caps, LANES), 0) + side * caps
        lane = lax.broadcasted_iota(jnp.int32, (caps, LANES), 1)
        for r in range(-(-2 * caps // LANES)):
            line = total[sums + r : sums + r + 1]
            found = found + jnp.where(at == lane + r * LANES, line, 0.0)
        return jnp.sum(found, axis=1, keepdims=True)

    lower, upper = column(0), column(1)
    place = lax.broadcasted_iota(jnp.int32, (caps, masks_ref.shape[1]), 1)
    inner = place % width
    block = (place // (width * group) * blocks + inner % blocks).astype(jnp.float32)
    inside = jnp.where((block >= lower) & (block < upper), 1.0, 0.0)
    for side in range(2):
        masks_ref[side * caps : (side + 1) * caps] = jnp.where(
            inner // blocks == side, inside, 0.0
        ).astype(jnp.bfloat16)


def tail_kernel(everyone_ref, captions_ref, masks_ref, divisor_ref, derivative_ref, loss_ref):
    own_caps = derivative_ref.shape[0]
    devices, width, half = everyone_ref.shape
    caps = captions_ref.shape[0]
    slot = lax.axis_index("seq") * lax.axis_size("head") + lax.axis_index("head")
    divisor = divisor_ref[0]
    captions = captions_ref[...]
    pieces = everyone_ref[...].reshape(devices * width, half)
    pooled = jnp.dot(masks_ref[...], pieces, preferred_element_type=jnp.float32)
    spans = unit([pooled[:caps], pooled[caps:]])

    logits = transposed_dot(spans, captions) * divisor
    row_total = jnp.log(jnp.sum(jnp.exp(logits), axis=0, keepdims=True))
    tall = -(-own_caps // SUB) * SUB
    row = lax.broadcasted_iota(jnp.int32, (tall, caps), 0)
    marker = jnp.where(
        (row < own_caps) & (lax.broadcasted_iota(jnp.int32, (tall, caps), 1) == slot * own_caps + row),
        1.0,
        0.0,
    )
    own_spans = jnp.dot(
        marker.astype(jnp.bfloat16), spans, preferred_element_type=jnp.float32
    ).astype(jnp.bfloat16)
    own = transposed_dot(own_spans, captions) * divisor
    col_total = jnp.log(jnp.sum(jnp.exp(own), axis=1, keepdims=True))
    loss = 0.5 * (jnp.sum(marker * row_total, axis=1, keepdims=True) + col_total) - jnp.sum(
        marker * own, axis=1, keepdims=True
    )
    flip = lax.broadcasted_iota(jnp.int32, (tall, tall), 0) == lax.broadcasted_iota(
        jnp.int32, (tall, tall), 1
    )
    loss_ref[...] = jnp.sum(jnp.where(flip, loss, 0.0), axis=0, keepdims=True)[:, :own_caps]
    weights = (
        0.5 * jnp.exp(own - row_total) + 0.5 * jnp.exp(own - col_total) - marker
    ).astype(jnp.bfloat16)
    derivative = jnp.dot(weights, captions, preferred_element_type=jnp.float32) * divisor
    derivative_ref[...] = derivative[:own_caps]


def local(
    frames, norm_gain, w_qkv, w_out, w_proj, text_table, token_ids, span_bounds, contrast_divisor
):
    rows, width = frames.shape
    cols = w_qkv.shape[2]
    half = cols // 2
    seq_count, head_count = lax.axis_size("seq"), lax.axis_size("head")
    devices = seq_count * head_count
    own_caps = span_bounds.shape[0]
    blocks = rows // BLK
    shape = jax.ShapeDtypeStruct
    bf16, f32 = jnp.bfloat16, jnp.float32

    tall = E // LANES * token_ids.shape[0] + BOUND_ROWS
    given = (frames, norm_gain[None], w_qkv, token_ids.T, text_table, span_bounds)
    own, p1, p2, p3, mine = call(
        first_kernel,
        [shape((n, half), bf16) for n in (3 * rows, 3 * rows + tall, 2 * rows, 2 * rows)]
        + [shape((tall, LANES), f32)],
        [HBM] * len(given),
        [
            pltpu.SMEM(a.shape, a.dtype) if a is span_bounds else pltpu.VMEM(a.shape, a.dtype)
            for a in given
        ]
        + [pltpu.VMEM(frames.shape, bf16), pltpu.SemaphoreType.DMA((8,))],
        (6 * rows * width * cols, 2 * w_qkv.size, 0),
    )(*[pltpu.with_memory_space_constraint(a, pltpu.HBM) for a in given])
    ends = seq_count - 1
    r1 = lax.ppermute(p1, "seq", [(s, s ^ 1) for s in range(seq_count)])
    r3 = lax.ppermute(
        p3,
        "seq",
        [(s, s + 1) for s in range(1, ends, 2)] + [(s, s - 1) for s in range(2, seq_count, 2)],
    )
    r2 = lax.ppermute(
        p2,
        "seq",
        [(s, s + 2) for s in range(1, ends - 1, 2)] + [(s, s - 2) for s in range(2, seq_count, 2)],
    )

    def swap(sent, seq_step, head_step):
        to = [
            (s ^ seq_step) * head_count + (h ^ head_step)
            for s in range(seq_count)
            for h in range(head_count)
        ]
        return lax.ppermute(sent, EVERY, list(enumerate(to)))

    def add(mine, *got):
        for g in got:
            mine = mine + g.astype(f32)
        return mine, mine.astype(bf16)

    mine, sent = add(mine, r1[3 * rows :])
    mine, sent = add(mine, swap(sent, 0, 1))
    got = swap(sent, 2, 0)

    wc, fp = call(
        weights_kernel,
        [shape((2 * half, E), bf16), shape((blocks, E), f32)],
        [VMEM] * 3,
        cost=(10**10, 2 * (w_proj.size + w_out.size + frames.size), 0),
    )(frames, w_out, w_proj)

    piece = call(
        attend_kernel,
        shape((devices, 4 * blocks, E // 2), PIECE),
        [VMEM] * 6,
        cost=(10**10, 10 * rows * cols, 6 * rows * rows * cols // HDIM),
    )(own, r1, r2, r3, wc, fp)

    got, piece = lax.optimization_barrier((got, piece))
    mine, sent = add(mine, got)
    step = 4
    while step < seq_count:
        mine, sent = add(mine, swap(sent, step, 0))
        step *= 2
    everyone = lax.all_to_all(piece, EVERY, 0, 0)
    gots = [swap(sent, 0, k) for k in range(2, head_count, 2)]

    captions, masks = call(
        functools.partial(caption_kernel, 2 * head_count, 4 * blocks),
        [
            shape((token_ids.shape[0], E), bf16),
            shape((2 * token_ids.shape[0], devices * 4 * blocks), bf16),
        ],
        [VMEM] * (1 + len(gots)),
    )(mine, *gots)
    derivative, loss = call(
        tail_kernel,
        [shape((own_caps, E), f32), shape((1, own_caps), f32)],
        [VMEM, VMEM, VMEM, SMEM],
        cost=(4 * E * token_ids.shape[0] ** 2, 2 * piece.size, 0),
    )(everyone, captions, masks, contrast_divisor)
    return derivative, loss.reshape(own_caps)


def solution(mesh):
    placed = (
        P("seq", None),
        P(),
        P(None, None, "head"),
        P("head", None),
        P(),
        P(EVERY, None),
        P(),
        P(EVERY, None),
        P(),
    )
    return jax.shard_map(
        local,
        mesh=mesh,
        in_specs=placed,
        out_specs=(P(EVERY, None), P(EVERY)),
        check_vma=False,
    )
```

```python
import functools

import jax
import jax.numpy as jnp
from jax import lax
from jax.experimental import pallas as pl
from jax.experimental.pallas import tpu as pltpu
from jax.sharding import PartitionSpec as P

HDIM = 64
E = 512
BLK = 128
EVERY = ("seq", "head")
LANES = 128
SUB = 8
NEVER = -1e30
BOUND_ROWS = 16
PIECE = jnp.bfloat16
VMEM = pl.BlockSpec(memory_space=pltpu.VMEM)
SMEM = pl.BlockSpec(memory_space=pltpu.SMEM)
HBM = pl.BlockSpec(memory_space=pltpu.HBM)
HIGHEST = lax.Precision.HIGHEST


def call(body, outs, ins, scratch=(), cost=(0, 0, 0), mib=24):
    return pl.pallas_call(
        body,
        out_shape=outs,
        in_specs=ins,
        out_specs=jax.tree.map(lambda _: VMEM, outs),
        scratch_shapes=scratch,
        compiler_params=pltpu.CompilerParams(vmem_limit_bytes=mib << 20),
        cost_estimate=pl.CostEstimate(
            flops=cost[0], bytes_accessed=cost[1], transcendentals=cost[2]
        ),
    )


def transposed_dot(left, right):
    return lax.dot_general(
        left, right, (((1,), (1,)), ((), ())), preferred_element_type=jnp.float32
    )


def first_kernel(
    frames_hbm,
    gain_hbm,
    w_hbm,
    ids_hbm,
    table_hbm,
    bounds_hbm,
    own_ref,
    p1_ref,
    p2_ref,
    p3_ref,
    t32_ref,
    frames,
    gain,
    w,
    id_rows,
    table,
    bound,
    normed,
    sems,
):
    rows = frames.shape[0]
    half = own_ref.shape[1]
    parts = [(ids_hbm, id_rows), (frames_hbm, frames), (gain_hbm, gain)]
    parts += [(w_hbm.at[k], w.at[k]) for k in (1, 2, 0)]
    parts += [(table_hbm, table), (bounds_hbm, bound)]
    copies = [pltpu.make_async_copy(*part, sems.at[n]) for n, part in enumerate(parts)]
    for n in (0, 1, 2, 3, 4, 6, 5, 7):
        copies[n].start()
    odd = lax.axis_index("seq") % 2 == 1

    tokens, caps = id_rows.shape
    vocab = table.shape[0]
    own_caps = bound.shape[0]
    slot = lax.axis_index("seq") * lax.axis_size("head") + lax.axis_index("head")
    copies[0].wait()
    ids = (id_rows[...] - slot * vocab).T
    words = lax.broadcasted_iota(jnp.int32, (caps, vocab), 1)
    counts = jnp.zeros((caps, vocab), jnp.float32)
    for t in range(tokens):
        counts = counts + jnp.where(ids[:, t : t + 1] == words, 1.0, 0.0)
    counts = counts.astype(jnp.bfloat16)

    copies[1].wait()
    copies[2].wait()
    step = min(64, rows)
    for r in range(0, rows, step):
        part = frames[r : r + step].astype(jnp.float32)
        scale = lax.rsqrt(jnp.mean(part * part, axis=-1, keepdims=True) + 1e-05)
        normed[r : r + step] = (part * scale * gain[...]).astype(jnp.bfloat16)
    def project(n, k):
        copies[3 + n].wait()
        both = jnp.dot(normed[...], w[k], preferred_element_type=jnp.float32).astype(jnp.bfloat16)
        if k == 0:
            both = both * jnp.bfloat16(HDIM ** (-0.5))
        mine = jnp.where(odd, both[:, half:], both[:, :half])
        other = jnp.where(odd, both[:, :half], both[:, half:])
        own_ref[k * rows : (k + 1) * rows] = mine
        p1_ref[k * rows : (k + 1) * rows] = other
        if k > 0:
            p2_ref[(k - 1) * rows : k * rows] = mine
            p3_ref[(k - 1) * rows : k * rows] = other

    project(0, 1)
    project(1, 2)
    copies[6].wait()
    copies[7].wait()
    part = jnp.dot(counts, table[...], preferred_element_type=jnp.float32)
    row = lax.broadcasted_iota(jnp.int32, (BOUND_ROWS, LANES), 0)
    place = row * LANES + lax.broadcasted_iota(jnp.int32, (BOUND_ROWS, LANES), 1)
    bounds = jnp.zeros((BOUND_ROWS, LANES), jnp.float32)
    for c in range(own_caps):
        for side in range(2):
            block = (bound[c, side] // BLK).astype(jnp.float32)
            bounds = jnp.where(place == side * caps + slot * own_caps + c, block, bounds)
    sums = E // LANES * caps
    for c in range(E // LANES):
        chunk = part[:, c * LANES : (c + 1) * LANES]
        t32_ref[c * caps : (c + 1) * caps] = chunk
        p1_ref[3 * rows + c * caps : 3 * rows + (c + 1) * caps] = chunk.astype(jnp.bfloat16)
    t32_ref[sums:] = bounds
    p1_ref[3 * rows + sums :] = bounds.astype(jnp.bfloat16)
    project(2, 0)


def weights_kernel(frames_ref, w_out_ref, w_proj_ref, wc_ref, fp_ref):
    half = wc_ref.shape[0] // 2
    cols = w_out_ref.shape[0]
    blocks = fp_ref.shape[0]
    odd = lax.axis_index("seq") % 2
    start = pl.multiple_of(lax.axis_index("head") * cols, LANES)
    product = jnp.dot(
        w_out_ref[pl.ds(pl.multiple_of(odd * half, half), half), :],
        w_proj_ref[...],
        preferred_element_type=jnp.float32,
    )
    high = product.astype(jnp.bfloat16)
    wc_ref[:half] = high
    wc_ref[half:] = (product - high.astype(jnp.float32)).astype(jnp.bfloat16)
    features = frames_ref[:, pl.ds(start, cols)].astype(jnp.float32)
    sums = jnp.sum(features.reshape(blocks, BLK, cols), axis=1)
    padded = jnp.concatenate([sums, jnp.zeros((SUB - blocks, cols), jnp.float32)], axis=0)
    fp_ref[...] = jnp.dot(
        padded, w_proj_ref[pl.ds(start, cols), :].astype(jnp.float32), precision=HIGHEST
    )[:blocks]


def attend_kernel(own_ref, r1_ref, r2_ref, r3_ref, wc_ref, fp_ref, out_ref):
    rows = own_ref.shape[0] // 3
    half = own_ref.shape[1]
    blocks = rows // BLK
    seq, last = lax.axis_index("seq"), lax.axis_size("seq") - 1
    odd = seq % 2
    apart = lax.broadcasted_iota(jnp.int32, (rows, rows), 0) - lax.broadcasted_iota(
        jnp.int32, (rows, rows), 1
    )
    lane = lax.broadcasted_iota(jnp.int32, (rows, half), 1)

    def block_sums(me, other, halo, parity, exists):
        side = jnp.where(parity == 0, apart, -apart)
        near = side >= 0
        far = side <= jnp.where(exists, 0, -2 * rows)
        query = me[0:rows]
        attended = jnp.zeros((rows, half), jnp.float32)
        for head in range(half // HDIM):
            mine = lane // HDIM == head
            q = jnp.where(mine, query, jnp.zeros_like(query))
            scores = [
                transposed_dot(q, me[rows : 2 * rows]),
                jnp.where(near, transposed_dot(q, other[rows : 2 * rows]), NEVER),
                jnp.where(far, transposed_dot(q, halo[0:rows]), NEVER),
            ]
            top = functools.reduce(jnp.maximum, [jnp.max(s, axis=1, keepdims=True) for s in scores])
            probs = [jnp.exp(s - top) for s in scores]
            denom = sum(jnp.sum(p, axis=1, keepdims=True) for p in probs)
            values = (me[2 * rows : 3 * rows], other[2 * rows : 3 * rows], halo[rows : 2 * rows])
            mixed = sum(
                jnp.dot(p.astype(jnp.bfloat16), v, preferred_element_type=jnp.float32)
                for p, v in zip(probs, values)
            )
            attended = jnp.where(mine, mixed * (1.0 / denom), attended)
        attended = attended.astype(jnp.bfloat16).astype(jnp.float32)
        return jnp.sum(attended.reshape(blocks, BLK, half), axis=1)

    here = block_sums(own_ref, r1_ref, r3_ref, odd, jnp.where(odd == 0, seq > 0, seq < last))
    there = block_sums(
        r1_ref, own_ref, r2_ref, 1 - odd, jnp.where(odd == 0, seq + 1 < last, seq > 1)
    )
    first = jnp.where(odd == 0, here, there)
    second = jnp.where(odd == 0, there, here)
    blank = jnp.zeros((SUB - 2 * blocks, half), jnp.float32)
    sums = jnp.concatenate([first, second, blank], axis=0)
    high = sums.astype(jnp.bfloat16)
    low = (sums - high.astype(jnp.float32)).astype(jnp.bfloat16)
    both = jnp.concatenate([high, low], axis=0)
    table = jnp.dot(both, wc_ref[:half], preferred_element_type=jnp.float32)
    table = table[:SUB] + table[SUB:] + jnp.dot(
        high, wc_ref[half:], preferred_element_type=jnp.float32
    )
    feature = fp_ref[...]
    none = jnp.zeros_like(feature)
    table = table[: 2 * blocks] + jnp.concatenate(
        [jnp.where(odd == 0, feature, none), jnp.where(odd == 0, none, feature)], axis=0
    )
    piece = jnp.concatenate([table[:, : E // 2], table[:, E // 2 :]], axis=0).astype(out_ref.dtype)
    out_ref[...] = jnp.broadcast_to(piece[None], out_ref.shape)


def unit(parts):
    mean = sum(jnp.sum(p * p, axis=-1, keepdims=True) for p in parts) * (1.0 / E)
    scale = lax.rsqrt(mean + 1e-06)
    return jnp.concatenate(
        [(p * scale * E ** (-0.5)).astype(jnp.bfloat16) for p in parts], axis=1
    )


def caption_kernel(group, width, mine_ref, *refs):
    *got_refs, captions_ref, masks_ref = refs
    caps = captions_ref.shape[0]
    sums = E // LANES * caps
    blocks = width // 2
    total = mine_ref[...] + sum(ref[...].astype(jnp.float32) for ref in got_refs)
    captions_ref[...] = unit([total[c * caps : (c + 1) * caps] for c in range(E // LANES)])

    def column(side):
        found = jnp.zeros((caps, LANES), jnp.float32)
        at = lax.broadcasted_iota(jnp.int32, (caps, LANES), 0) + side * caps
        lane = lax.broadcasted_iota(jnp.int32, (caps, LANES), 1)
        for r in range(-(-2 * caps // LANES)):
            line = total[sums + r : sums + r + 1]
            found = found + jnp.where(at == lane + r * LANES, line, 0.0)
        return jnp.sum(found, axis=1, keepdims=True)

    lower, upper = column(0), column(1)
    place = lax.broadcasted_iota(jnp.int32, (caps, masks_ref.shape[1]), 1)
    inner = place % width
    pair = masks_ref.shape[1] // (width * group) - 1 - place // (width * group)
    block = (pair * blocks + inner % blocks).astype(jnp.float32)
    inside = jnp.where((block >= lower) & (block < upper), 1.0, 0.0)
    for side in range(2):
        masks_ref[side * caps : (side + 1) * caps] = jnp.where(
            inner // blocks == side, inside, 0.0
        ).astype(jnp.bfloat16)


def tail_kernel(everyone_ref, captions_ref, masks_ref, divisor_ref, derivative_ref, loss_ref):
    own_caps = derivative_ref.shape[0]
    devices, width, half = everyone_ref.shape
    caps = captions_ref.shape[0]
    slot = lax.axis_index("seq") * lax.axis_size("head") + lax.axis_index("head")
    divisor = divisor_ref[0]
    captions = captions_ref[...]
    pieces = everyone_ref[...].reshape(devices * width, half)
    pooled = jnp.dot(masks_ref[...], pieces, preferred_element_type=jnp.float32)
    spans = unit([pooled[:caps], pooled[caps:]])

    logits = transposed_dot(spans, captions) * divisor
    row_total = jnp.log(jnp.sum(jnp.exp(logits), axis=0, keepdims=True))
    tall = -(-own_caps // SUB) * SUB
    row = lax.broadcasted_iota(jnp.int32, (tall, caps), 0)
    marker = jnp.where(
        (row < own_caps) & (lax.broadcasted_iota(jnp.int32, (tall, caps), 1) == slot * own_caps + row),
        1.0,
        0.0,
    )
    own_spans = jnp.dot(
        marker.astype(jnp.bfloat16), spans, preferred_element_type=jnp.float32
    ).astype(jnp.bfloat16)
    own = transposed_dot(own_spans, captions) * divisor
    col_total = jnp.log(jnp.sum(jnp.exp(own), axis=1, keepdims=True))
    loss = 0.5 * (jnp.sum(marker * row_total, axis=1, keepdims=True) + col_total) - jnp.sum(
        marker * own, axis=1, keepdims=True
    )
    flip = lax.broadcasted_iota(jnp.int32, (tall, tall), 0) == lax.broadcasted_iota(
        jnp.int32, (tall, tall), 1
    )
    loss_ref[...] = jnp.sum(jnp.where(flip, loss, 0.0), axis=0, keepdims=True)[:, :own_caps]
    weights = (
        0.5 * jnp.exp(own - row_total) + 0.5 * jnp.exp(own - col_total) - marker
    ).astype(jnp.bfloat16)
    derivative = jnp.dot(weights, captions, preferred_element_type=jnp.float32) * divisor
    derivative_ref[...] = derivative[:own_caps]


def local(
    frames, norm_gain, w_qkv, w_out, w_proj, text_table, token_ids, span_bounds, contrast_divisor
):
    rows, width = frames.shape
    cols = w_qkv.shape[2]
    half = cols // 2
    seq_count, head_count = lax.axis_size("seq"), lax.axis_size("head")
    devices = seq_count * head_count
    own_caps = span_bounds.shape[0]
    blocks = rows // BLK
    shape = jax.ShapeDtypeStruct
    bf16, f32 = jnp.bfloat16, jnp.float32

    tall = E // LANES * token_ids.shape[0] + BOUND_ROWS
    given = (frames, norm_gain[None], w_qkv, token_ids.T, text_table, span_bounds)
    own, p1, p2, p3, mine = call(
        first_kernel,
        [shape((n, half), bf16) for n in (3 * rows, 3 * rows + tall, 2 * rows, 2 * rows)]
        + [shape((tall, LANES), f32)],
        [HBM] * len(given),
        [
            pltpu.SMEM(a.shape, a.dtype) if a is span_bounds else pltpu.VMEM(a.shape, a.dtype)
            for a in given
        ]
        + [pltpu.VMEM(frames.shape, bf16), pltpu.SemaphoreType.DMA((8,))],
        (6 * rows * width * cols, 2 * w_qkv.size, 0),
    )(*[pltpu.with_memory_space_constraint(a, pltpu.HBM) for a in given])
    ends = seq_count - 1
    r1 = lax.ppermute(p1, "seq", [(s, s ^ 1) for s in range(seq_count)])
    r3 = lax.ppermute(
        p3,
        "seq",
        [(s, s + 1) for s in range(1, ends, 2)] + [(s, s - 1) for s in range(2, seq_count, 2)],
    )
    r2 = lax.ppermute(
        p2,
        "seq",
        [(s, s + 2) for s in range(1, ends - 1, 2)] + [(s, s - 2) for s in range(2, seq_count, 2)],
    )

    def swap(sent, seq_step, head_step):
        to = [
            (s ^ seq_step) * head_count + (h ^ head_step)
            for s in range(seq_count)
            for h in range(head_count)
        ]
        return lax.ppermute(sent, EVERY, list(enumerate(to)))

    def add(mine, *got):
        for g in got:
            mine = mine + g.astype(f32)
        return mine, mine.astype(bf16)

    mine, sent = add(mine, r1[3 * rows :])
    mine, sent = add(mine, swap(sent, 0, 1))
    got = swap(sent, 2, 0)

    wc, fp = call(
        weights_kernel,
        [shape((2 * half, E), bf16), shape((blocks, E), f32)],
        [VMEM] * 3,
        cost=(10**10, 2 * (w_proj.size + w_out.size + frames.size), 0),
    )(frames, w_out, w_proj)

    piece = call(
        attend_kernel,
        shape((devices, 4 * blocks, E // 2), PIECE),
        [VMEM] * 6,
        cost=(10**10, 10 * rows * cols, 6 * rows * rows * cols // HDIM),
    )(own, r1, r2, r3, wc, fp)

    got, piece = lax.optimization_barrier((got, piece))
    mine, sent = add(mine, got)
    step = 4
    while step < seq_count:
        mine, sent = add(mine, swap(sent, step, 0))
        step *= 2
    backward = list(range(devices))[::-1]
    everyone = lax.all_to_all(piece, EVERY, 0, 0, axis_index_groups=[backward])
    gots = [swap(sent, 0, k) for k in range(2, head_count, 2)]

    captions, masks = call(
        functools.partial(caption_kernel, 2 * head_count, 4 * blocks),
        [
            shape((token_ids.shape[0], E), bf16),
            shape((2 * token_ids.shape[0], devices * 4 * blocks), bf16),
        ],
        [VMEM] * (1 + len(gots)),
    )(mine, *gots)
    derivative, loss = call(
        tail_kernel,
        [shape((own_caps, E), f32), shape((1, own_caps), f32)],
        [VMEM, VMEM, VMEM, SMEM],
        cost=(4 * E * token_ids.shape[0] ** 2, 2 * piece.size, 0),
    )(everyone, captions, masks, contrast_divisor)
    return derivative, loss.reshape(own_caps)


def solution(mesh):
    placed = (
        P("seq", None),
        P(),
        P(None, None, "head"),
        P("head", None),
        P(),
        P(EVERY, None),
        P(),
        P(EVERY, None),
        P(),
    )
    return jax.shard_map(
        local,
        mesh=mesh,
        in_specs=placed,
        out_specs=(P(EVERY, None), P(EVERY)),
        check_vma=False,
    )
```

```python
import functools

import jax
import jax.numpy as jnp
from jax import lax
from jax.experimental import pallas as pl
from jax.experimental.pallas import tpu as pltpu
from jax.sharding import PartitionSpec as P

HDIM = 64
E = 512
BLK = 128
EVERY = ("seq", "head")
LANES = 128
SUB = 8
NEVER = -1e30
BOUND_ROWS = 16
PIECE = jnp.bfloat16
VMEM = pl.BlockSpec(memory_space=pltpu.VMEM)
SMEM = pl.BlockSpec(memory_space=pltpu.SMEM)
HBM = pl.BlockSpec(memory_space=pltpu.HBM)
HIGHEST = lax.Precision.HIGHEST


def call(body, outs, ins, scratch=(), cost=(0, 0, 0), mib=24):
    return pl.pallas_call(
        body,
        out_shape=outs,
        in_specs=ins,
        out_specs=jax.tree.map(lambda _: VMEM, outs),
        scratch_shapes=scratch,
        compiler_params=pltpu.CompilerParams(vmem_limit_bytes=mib << 20),
        cost_estimate=pl.CostEstimate(
            flops=cost[0], bytes_accessed=cost[1], transcendentals=cost[2]
        ),
    )


def transposed_dot(left, right):
    return lax.dot_general(
        left, right, (((1,), (1,)), ((), ())), preferred_element_type=jnp.float32
    )


def first_kernel(
    frames_hbm,
    gain_hbm,
    w_hbm,
    ids_hbm,
    table_hbm,
    bounds_hbm,
    own_ref,
    p1_ref,
    p2_ref,
    p3_ref,
    t32_ref,
    frames,
    gain,
    w,
    id_rows,
    table,
    bound,
    normed,
    sems,
):
    rows = frames.shape[0]
    half = own_ref.shape[1]
    parts = [(ids_hbm, id_rows), (frames_hbm, frames), (gain_hbm, gain)]
    parts += [(w_hbm.at[k], w.at[k]) for k in (1, 2, 0)]
    parts += [(table_hbm, table), (bounds_hbm, bound)]
    copies = [pltpu.make_async_copy(*part, sems.at[n]) for n, part in enumerate(parts)]
    for n in (0, 1, 2, 3, 4, 6, 5, 7):
        copies[n].start()
    odd = lax.axis_index("seq") % 2 == 1

    tokens, caps = id_rows.shape
    vocab = table.shape[0]
    own_caps = bound.shape[0]
    slot = lax.axis_index("seq") * lax.axis_size("head") + lax.axis_index("head")
    copies[0].wait()
    ids = (id_rows[...] - slot * vocab).T
    words = lax.broadcasted_iota(jnp.int32, (caps, vocab), 1)
    counts = jnp.zeros((caps, vocab), jnp.float32)
    for t in range(tokens):
        counts = counts + jnp.where(ids[:, t : t + 1] == words, 1.0, 0.0)
    counts = counts.astype(jnp.bfloat16)

    copies[1].wait()
    copies[2].wait()
    step = min(64, rows)
    for r in range(0, rows, step):
        part = frames[r : r + step].astype(jnp.float32)
        scale = lax.rsqrt(jnp.mean(part * part, axis=-1, keepdims=True) + 1e-05)
        normed[r : r + step] = (part * scale * gain[...]).astype(jnp.bfloat16)
    def project(n, k):
        copies[3 + n].wait()
        both = jnp.dot(normed[...], w[k], preferred_element_type=jnp.float32).astype(jnp.bfloat16)
        if k == 0:
            both = both * jnp.bfloat16(HDIM ** (-0.5))
        mine = jnp.where(odd, both[:, half:], both[:, :half])
        other = jnp.where(odd, both[:, :half], both[:, half:])
        own_ref[k * rows : (k + 1) * rows] = mine
        p1_ref[k * rows : (k + 1) * rows] = other
        if k > 0:
            p2_ref[(k - 1) * rows : k * rows] = mine
            p3_ref[(k - 1) * rows : k * rows] = other

    project(0, 1)
    project(1, 2)
    copies[6].wait()
    copies[7].wait()
    part = jnp.dot(counts, table[...], preferred_element_type=jnp.float32)
    row = lax.broadcasted_iota(jnp.int32, (BOUND_ROWS, LANES), 0)
    place = row * LANES + lax.broadcasted_iota(jnp.int32, (BOUND_ROWS, LANES), 1)
    bounds = jnp.zeros((BOUND_ROWS, LANES), jnp.float32)
    for c in range(own_caps):
        for side in range(2):
            block = (bound[c, side] // BLK).astype(jnp.float32)
            bounds = jnp.where(place == side * caps + slot * own_caps + c, block, bounds)
    sums = E // LANES * caps
    for c in range(E // LANES):
        chunk = part[:, c * LANES : (c + 1) * LANES]
        t32_ref[c * caps : (c + 1) * caps] = chunk
        p1_ref[3 * rows + c * caps : 3 * rows + (c + 1) * caps] = chunk.astype(jnp.bfloat16)
    t32_ref[sums:] = bounds
    p1_ref[3 * rows + sums :] = bounds.astype(jnp.bfloat16)
    project(2, 0)


def weights_kernel(frames_ref, w_out_ref, w_proj_ref, wc_ref, fp_ref):
    half = wc_ref.shape[0] // 2
    cols = w_out_ref.shape[0]
    blocks = fp_ref.shape[0]
    odd = lax.axis_index("seq") % 2
    start = pl.multiple_of(lax.axis_index("head") * cols, LANES)
    product = jnp.dot(
        w_out_ref[pl.ds(pl.multiple_of(odd * half, half), half), :],
        w_proj_ref[...],
        preferred_element_type=jnp.float32,
    )
    high = product.astype(jnp.bfloat16)
    wc_ref[:half] = high
    wc_ref[half:] = (product - high.astype(jnp.float32)).astype(jnp.bfloat16)
    features = frames_ref[:, pl.ds(start, cols)].astype(jnp.float32)
    sums = jnp.sum(features.reshape(blocks, BLK, cols), axis=1)
    padded = jnp.concatenate([sums, jnp.zeros((SUB - blocks, cols), jnp.float32)], axis=0)
    fp_ref[...] = jnp.dot(
        padded, w_proj_ref[pl.ds(start, cols), :].astype(jnp.float32), precision=HIGHEST
    )[:blocks]


def attend_kernel(own_ref, r1_ref, r2_ref, r3_ref, wc_ref, fp_ref, out_ref):
    rows = own_ref.shape[0] // 3
    half = own_ref.shape[1]
    blocks = rows // BLK
    seq, last = lax.axis_index("seq"), lax.axis_size("seq") - 1
    odd = seq % 2
    heads = half // HDIM
    apart = lax.broadcasted_iota(jnp.int32, (rows, rows), 0) - lax.broadcasted_iota(
        jnp.int32, (rows, rows), 1
    )
    apart = jnp.concatenate([apart] * heads, axis=0)
    lane = lax.broadcasted_iota(jnp.int32, (rows, half), 1)

    def block_sums(me, other, halo, parity, exists):
        side = jnp.where(parity == 0, apart, -apart)
        near = side >= 0
        far = side <= jnp.where(exists, 0, -2 * rows)
        query = me[0:rows]
        blank = jnp.zeros_like(query)
        q = jnp.concatenate(
            [jnp.where(lane // HDIM == head, query, blank) for head in range(heads)], axis=0
        )
        scores = [
            transposed_dot(q, me[rows : 2 * rows]),
            jnp.where(near, transposed_dot(q, other[rows : 2 * rows]), NEVER),
            jnp.where(far, transposed_dot(q, halo[0:rows]), NEVER),
        ]
        top = jnp.max(functools.reduce(jnp.maximum, scores), axis=1, keepdims=True)
        probs = [jnp.exp(s - top) for s in scores]
        denom = jnp.sum(sum(probs), axis=1, keepdims=True)
        values = (me[2 * rows : 3 * rows], other[2 * rows : 3 * rows], halo[rows : 2 * rows])
        mixed = jnp.dot(
            jnp.concatenate([p.astype(jnp.bfloat16) for p in probs], axis=1),
            jnp.concatenate(values, axis=0),
            preferred_element_type=jnp.float32,
        )
        mixed = mixed * (1.0 / denom)
        attended = mixed[:rows]
        for head in range(1, heads):
            attended = jnp.where(
                lane // HDIM == head, mixed[head * rows : (head + 1) * rows], attended
            )
        attended = attended.astype(jnp.bfloat16).astype(jnp.float32)
        return jnp.sum(attended.reshape(blocks, BLK, half), axis=1)

    here = block_sums(own_ref, r1_ref, r3_ref, odd, jnp.where(odd == 0, seq > 0, seq < last))
    there = block_sums(
        r1_ref, own_ref, r2_ref, 1 - odd, jnp.where(odd == 0, seq + 1 < last, seq > 1)
    )
    first = jnp.where(odd == 0, here, there)
    second = jnp.where(odd == 0, there, here)
    blank = jnp.zeros((SUB - 2 * blocks, half), jnp.float32)
    sums = jnp.concatenate([first, second, blank], axis=0)
    high = sums.astype(jnp.bfloat16)
    low = (sums - high.astype(jnp.float32)).astype(jnp.bfloat16)
    both = jnp.concatenate([high, low], axis=0)
    table = jnp.dot(both, wc_ref[:half], preferred_element_type=jnp.float32)
    table = table[:SUB] + table[SUB:] + jnp.dot(
        high, wc_ref[half:], preferred_element_type=jnp.float32
    )
    feature = fp_ref[...]
    none = jnp.zeros_like(feature)
    table = table[: 2 * blocks] + jnp.concatenate(
        [jnp.where(odd == 0, feature, none), jnp.where(odd == 0, none, feature)], axis=0
    )
    piece = jnp.concatenate([table[:, : E // 2], table[:, E // 2 :]], axis=0).astype(out_ref.dtype)
    out_ref[...] = jnp.broadcast_to(piece[None], out_ref.shape)


def unit(parts):
    mean = sum(jnp.sum(p * p, axis=-1, keepdims=True) for p in parts) * (1.0 / E)
    scale = lax.rsqrt(mean + 1e-06)
    return jnp.concatenate(
        [(p * scale * E ** (-0.5)).astype(jnp.bfloat16) for p in parts], axis=1
    )


def caption_kernel(group, width, mine_ref, *refs):
    *got_refs, captions_ref, masks_ref = refs
    caps = captions_ref.shape[0]
    sums = E // LANES * caps
    blocks = width // 2
    total = mine_ref[...] + sum(ref[...].astype(jnp.float32) for ref in got_refs)
    captions_ref[...] = unit([total[c * caps : (c + 1) * caps] for c in range(E // LANES)])

    def column(side):
        found = jnp.zeros((caps, LANES), jnp.float32)
        at = lax.broadcasted_iota(jnp.int32, (caps, LANES), 0) + side * caps
        lane = lax.broadcasted_iota(jnp.int32, (caps, LANES), 1)
        for r in range(-(-2 * caps // LANES)):
            line = total[sums + r : sums + r + 1]
            found = found + jnp.where(at == lane + r * LANES, line, 0.0)
        return jnp.sum(found, axis=1, keepdims=True)

    lower, upper = column(0), column(1)
    place = lax.broadcasted_iota(jnp.int32, (caps, masks_ref.shape[1]), 1)
    inner = place % width
    pair = masks_ref.shape[1] // (width * group) - 1 - place // (width * group)
    block = (pair * blocks + inner % blocks).astype(jnp.float32)
    inside = jnp.where((block >= lower) & (block < upper), 1.0, 0.0)
    for side in range(2):
        masks_ref[side * caps : (side + 1) * caps] = jnp.where(
            inner // blocks == side, inside, 0.0
        ).astype(jnp.bfloat16)


def tail_kernel(everyone_ref, captions_ref, masks_ref, divisor_ref, derivative_ref, loss_ref):
    own_caps = derivative_ref.shape[0]
    devices, width, half = everyone_ref.shape
    caps = captions_ref.shape[0]
    slot = lax.axis_index("seq") * lax.axis_size("head") + lax.axis_index("head")
    divisor = divisor_ref[0]
    captions = captions_ref[...]
    pieces = everyone_ref[...].reshape(devices * width, half)
    pooled = jnp.dot(masks_ref[...], pieces, preferred_element_type=jnp.float32)
    spans = unit([pooled[:caps], pooled[caps:]])

    logits = transposed_dot(spans, captions) * divisor
    row_total = jnp.log(jnp.sum(jnp.exp(logits), axis=0, keepdims=True))
    tall = -(-own_caps // SUB) * SUB
    row = lax.broadcasted_iota(jnp.int32, (tall, caps), 0)
    marker = jnp.where(
        (row < own_caps) & (lax.broadcasted_iota(jnp.int32, (tall, caps), 1) == slot * own_caps + row),
        1.0,
        0.0,
    )
    own_spans = jnp.dot(
        marker.astype(jnp.bfloat16), spans, preferred_element_type=jnp.float32
    ).astype(jnp.bfloat16)
    own = transposed_dot(own_spans, captions) * divisor
    col_total = jnp.log(jnp.sum(jnp.exp(own), axis=1, keepdims=True))
    loss = 0.5 * (jnp.sum(marker * row_total, axis=1, keepdims=True) + col_total) - jnp.sum(
        marker * own, axis=1, keepdims=True
    )
    flip = lax.broadcasted_iota(jnp.int32, (tall, tall), 0) == lax.broadcasted_iota(
        jnp.int32, (tall, tall), 1
    )
    loss_ref[...] = jnp.sum(jnp.where(flip, loss, 0.0), axis=0, keepdims=True)[:, :own_caps]
    weights = (
        0.5 * jnp.exp(own - row_total) + 0.5 * jnp.exp(own - col_total) - marker
    ).astype(jnp.bfloat16)
    derivative = jnp.dot(weights, captions, preferred_element_type=jnp.float32) * divisor
    derivative_ref[...] = derivative[:own_caps]


def local(
    frames, norm_gain, w_qkv, w_out, w_proj, text_table, token_ids, span_bounds, contrast_divisor
):
    rows, width = frames.shape
    cols = w_qkv.shape[2]
    half = cols // 2
    seq_count, head_count = lax.axis_size("seq"), lax.axis_size("head")
    devices = seq_count * head_count
    own_caps = span_bounds.shape[0]
    blocks = rows // BLK
    shape = jax.ShapeDtypeStruct
    bf16, f32 = jnp.bfloat16, jnp.float32

    tall = E // LANES * token_ids.shape[0] + BOUND_ROWS
    given = (frames, norm_gain[None], w_qkv, token_ids.T, text_table, span_bounds)
    own, p1, p2, p3, mine = call(
        first_kernel,
        [shape((n, half), bf16) for n in (3 * rows, 3 * rows + tall, 2 * rows, 2 * rows)]
        + [shape((tall, LANES), f32)],
        [HBM] * len(given),
        [
            pltpu.SMEM(a.shape, a.dtype) if a is span_bounds else pltpu.VMEM(a.shape, a.dtype)
            for a in given
        ]
        + [pltpu.VMEM(frames.shape, bf16), pltpu.SemaphoreType.DMA((8,))],
        (6 * rows * width * cols, 2 * w_qkv.size, 0),
    )(*[pltpu.with_memory_space_constraint(a, pltpu.HBM) for a in given])
    ends = seq_count - 1
    r1 = lax.ppermute(p1, "seq", [(s, s ^ 1) for s in range(seq_count)])
    r3 = lax.ppermute(
        p3,
        "seq",
        [(s, s + 1) for s in range(1, ends, 2)] + [(s, s - 1) for s in range(2, seq_count, 2)],
    )
    r2 = lax.ppermute(
        p2,
        "seq",
        [(s, s + 2) for s in range(1, ends - 1, 2)] + [(s, s - 2) for s in range(2, seq_count, 2)],
    )

    def swap(sent, seq_step, head_step):
        to = [
            (s ^ seq_step) * head_count + (h ^ head_step)
            for s in range(seq_count)
            for h in range(head_count)
        ]
        return lax.ppermute(sent, EVERY, list(enumerate(to)))

    def add(mine, *got):
        for g in got:
            mine = mine + g.astype(f32)
        return mine, mine.astype(bf16)

    mine, sent = add(mine, r1[3 * rows :])
    mine, sent = add(mine, swap(sent, 0, 1))
    got = swap(sent, 2, 0)

    wc, fp = call(
        weights_kernel,
        [shape((2 * half, E), bf16), shape((blocks, E), f32)],
        [VMEM] * 3,
        cost=(10**10, 2 * (w_proj.size + w_out.size + frames.size), 0),
    )(frames, w_out, w_proj)

    piece = call(
        attend_kernel,
        shape((devices, 4 * blocks, E // 2), PIECE),
        [VMEM] * 6,
        cost=(10**10, 10 * rows * cols, 6 * rows * rows * cols // HDIM),
    )(own, r1, r2, r3, wc, fp)

    got, piece = lax.optimization_barrier((got, piece))
    mine, sent = add(mine, got)
    step = 4
    while step < seq_count:
        mine, sent = add(mine, swap(sent, step, 0))
        step *= 2
    backward = list(range(devices))[::-1]
    everyone = lax.all_to_all(piece, EVERY, 0, 0, axis_index_groups=[backward])
    gots = [swap(sent, 0, k) for k in range(2, head_count, 2)]

    captions, masks = call(
        functools.partial(caption_kernel, 2 * head_count, 4 * blocks),
        [
            shape((token_ids.shape[0], E), bf16),
            shape((2 * token_ids.shape[0], devices * 4 * blocks), bf16),
        ],
        [VMEM] * (1 + len(gots)),
    )(mine, *gots)
    derivative, loss = call(
        tail_kernel,
        [shape((own_caps, E), f32), shape((1, own_caps), f32)],
        [VMEM, VMEM, VMEM, SMEM],
        cost=(4 * E * token_ids.shape[0] ** 2, 2 * piece.size, 0),
    )(everyone, captions, masks, contrast_divisor)
    return derivative, loss.reshape(own_caps)


def solution(mesh):
    placed = (
        P("seq", None),
        P(),
        P(None, None, "head"),
        P("head", None),
        P(),
        P(EVERY, None),
        P(),
        P(EVERY, None),
        P(),
    )
    return jax.shard_map(
        local,
        mesh=mesh,
        in_specs=placed,
        out_specs=(P(EVERY, None), P(EVERY)),
        check_vma=False,
    )
```

```python
import functools

import jax
import jax.numpy as jnp
from jax import lax
from jax.experimental import pallas as pl
from jax.experimental.pallas import tpu as pltpu
from jax.sharding import PartitionSpec as P

HDIM = 64
E = 512
BLK = 128
EVERY = ("seq", "head")
LANES = 128
SUB = 8
NEVER = -1e30
BOUND_ROWS = 16
PIECE = jnp.bfloat16
VMEM = pl.BlockSpec(memory_space=pltpu.VMEM)
SMEM = pl.BlockSpec(memory_space=pltpu.SMEM)
HBM = pl.BlockSpec(memory_space=pltpu.HBM)
HIGHEST = lax.Precision.HIGHEST


def call(body, outs, ins, scratch=(), cost=(0, 0, 0), mib=24):
    return pl.pallas_call(
        body,
        out_shape=outs,
        in_specs=ins,
        out_specs=jax.tree.map(lambda _: VMEM, outs),
        scratch_shapes=scratch,
        compiler_params=pltpu.CompilerParams(vmem_limit_bytes=mib << 20),
        cost_estimate=pl.CostEstimate(
            flops=cost[0], bytes_accessed=cost[1], transcendentals=cost[2]
        ),
    )


def transposed_dot(left, right):
    return lax.dot_general(
        left, right, (((1,), (1,)), ((), ())), preferred_element_type=jnp.float32
    )


def first_kernel(
    frames_hbm,
    gain_hbm,
    w_hbm,
    ids_hbm,
    table_hbm,
    bounds_hbm,
    own_ref,
    p1_ref,
    p2_ref,
    p3_ref,
    t32_ref,
    frames,
    gain,
    w,
    id_rows,
    table,
    bound,
    normed,
    sems,
):
    rows = frames.shape[0]
    half = own_ref.shape[1]
    parts = [(ids_hbm, id_rows), (frames_hbm, frames), (gain_hbm, gain)]
    parts += [(w_hbm.at[k], w.at[k]) for k in (1, 2, 0)]
    parts += [(table_hbm, table), (bounds_hbm, bound)]
    copies = [pltpu.make_async_copy(*part, sems.at[n]) for n, part in enumerate(parts)]
    for n in (0, 1, 2, 3, 4, 6, 5, 7):
        copies[n].start()
    odd = lax.axis_index("seq") % 2 == 1

    tokens, caps = id_rows.shape
    vocab = table.shape[0]
    own_caps = bound.shape[0]
    slot = lax.axis_index("seq") * lax.axis_size("head") + lax.axis_index("head")
    copies[0].wait()
    ids = id_rows[...] - slot * vocab
    ids = jnp.where((ids >= 0) & (ids < vocab), ids, -1).T
    words = lax.broadcasted_iota(jnp.int32, (caps, vocab), 1).astype(jnp.int16)
    counts = jnp.zeros((caps, vocab), jnp.bfloat16)
    one, none = jnp.ones_like(counts), jnp.zeros_like(counts)
    for t in range(tokens):
        column = jnp.broadcast_to(ids[:, t : t + 1], (caps, vocab)).astype(jnp.int16)
        counts = counts + jnp.where(column == words, one, none)

    copies[1].wait()
    copies[2].wait()
    step = min(64, rows)
    for r in range(0, rows, step):
        part = frames[r : r + step].astype(jnp.float32)
        scale = lax.rsqrt(jnp.mean(part * part, axis=-1, keepdims=True) + 1e-05)
        normed[r : r + step] = (part * scale * gain[...]).astype(jnp.bfloat16)
    def project(n, k):
        copies[3 + n].wait()
        both = jnp.dot(normed[...], w[k], preferred_element_type=jnp.float32).astype(jnp.bfloat16)
        if k == 0:
            both = both * jnp.bfloat16(HDIM ** (-0.5))
        mine = jnp.where(odd, both[:, half:], both[:, :half])
        other = jnp.where(odd, both[:, :half], both[:, half:])
        own_ref[k * rows : (k + 1) * rows] = mine
        p1_ref[k * rows : (k + 1) * rows] = other
        if k > 0:
            p2_ref[(k - 1) * rows : k * rows] = mine
            p3_ref[(k - 1) * rows : k * rows] = other

    project(0, 1)
    project(1, 2)
    copies[6].wait()
    copies[7].wait()
    part = jnp.dot(counts, table[...], preferred_element_type=jnp.float32)
    row = lax.broadcasted_iota(jnp.int32, (BOUND_ROWS, LANES), 0)
    place = row * LANES + lax.broadcasted_iota(jnp.int32, (BOUND_ROWS, LANES), 1)
    bounds = jnp.zeros((BOUND_ROWS, LANES), jnp.float32)
    for c in range(own_caps):
        for side in range(2):
            block = (bound[c, side] // BLK).astype(jnp.float32)
            bounds = jnp.where(place == side * caps + slot * own_caps + c, block, bounds)
    sums = E // LANES * caps
    for c in range(E // LANES):
        chunk = part[:, c * LANES : (c + 1) * LANES]
        t32_ref[c * caps : (c + 1) * caps] = chunk
        p1_ref[3 * rows + c * caps : 3 * rows + (c + 1) * caps] = chunk.astype(jnp.bfloat16)
    t32_ref[sums:] = bounds
    p1_ref[3 * rows + sums :] = bounds.astype(jnp.bfloat16)
    project(2, 0)


def weights_kernel(frames_ref, w_out_ref, w_proj_ref, wc_ref, fp_ref):
    half = wc_ref.shape[0] // 2
    cols = w_out_ref.shape[0]
    blocks = fp_ref.shape[0]
    odd = lax.axis_index("seq") % 2
    start = pl.multiple_of(lax.axis_index("head") * cols, LANES)
    product = jnp.dot(
        w_out_ref[pl.ds(pl.multiple_of(odd * half, half), half), :],
        w_proj_ref[...],
        preferred_element_type=jnp.float32,
    )
    high = product.astype(jnp.bfloat16)
    wc_ref[:half] = high
    wc_ref[half:] = (product - high.astype(jnp.float32)).astype(jnp.bfloat16)
    features = frames_ref[:, pl.ds(start, cols)].astype(jnp.float32)
    sums = jnp.sum(features.reshape(blocks, BLK, cols), axis=1)
    padded = jnp.concatenate([sums, jnp.zeros((SUB - blocks, cols), jnp.float32)], axis=0)
    fp_ref[...] = jnp.dot(
        padded, w_proj_ref[pl.ds(start, cols), :].astype(jnp.float32), precision=HIGHEST
    )[:blocks]


def attend_kernel(own_ref, r1_ref, r2_ref, r3_ref, wc_ref, fp_ref, out_ref):
    rows = own_ref.shape[0] // 3
    half = own_ref.shape[1]
    blocks = rows // BLK
    seq, last = lax.axis_index("seq"), lax.axis_size("seq") - 1
    odd = seq % 2
    heads = half // HDIM
    apart = lax.broadcasted_iota(jnp.int32, (rows, rows), 0) - lax.broadcasted_iota(
        jnp.int32, (rows, rows), 1
    )
    apart = jnp.concatenate([apart] * heads, axis=0)
    lane = lax.broadcasted_iota(jnp.int32, (rows, half), 1)

    def block_sums(me, other, halo, parity, exists):
        side = jnp.where(parity == 0, apart, -apart)
        near = side >= 0
        far = side <= jnp.where(exists, 0, -2 * rows)
        query = me[0:rows]
        blank = jnp.zeros_like(query)
        q = jnp.concatenate(
            [jnp.where(lane // HDIM == head, query, blank) for head in range(heads)], axis=0
        )
        scores = [
            transposed_dot(q, me[rows : 2 * rows]),
            jnp.where(near, transposed_dot(q, other[rows : 2 * rows]), NEVER),
            jnp.where(far, transposed_dot(q, halo[0:rows]), NEVER),
        ]
        top = jnp.max(functools.reduce(jnp.maximum, scores), axis=1, keepdims=True)
        probs = [jnp.exp(s - top) for s in scores]
        denom = jnp.sum(sum(probs), axis=1, keepdims=True)
        values = (me[2 * rows : 3 * rows], other[2 * rows : 3 * rows], halo[rows : 2 * rows])
        mixed = jnp.dot(
            jnp.concatenate([p.astype(jnp.bfloat16) for p in probs], axis=1),
            jnp.concatenate(values, axis=0),
            preferred_element_type=jnp.float32,
        )
        mixed = mixed * (1.0 / denom)
        attended = mixed[:rows]
        for head in range(1, heads):
            attended = jnp.where(
                lane // HDIM == head, mixed[head * rows : (head + 1) * rows], attended
            )
        attended = attended.astype(jnp.bfloat16).astype(jnp.float32)
        return jnp.sum(attended.reshape(blocks, BLK, half), axis=1)

    here = block_sums(own_ref, r1_ref, r3_ref, odd, jnp.where(odd == 0, seq > 0, seq < last))
    there = block_sums(
        r1_ref, own_ref, r2_ref, 1 - odd, jnp.where(odd == 0, seq + 1 < last, seq > 1)
    )
    first = jnp.where(odd == 0, here, there)
    second = jnp.where(odd == 0, there, here)
    blank = jnp.zeros((SUB - 2 * blocks, half), jnp.float32)
    sums = jnp.concatenate([first, second, blank], axis=0)
    high = sums.astype(jnp.bfloat16)
    low = (sums - high.astype(jnp.float32)).astype(jnp.bfloat16)
    both = jnp.concatenate([high, low], axis=0)
    table = jnp.dot(both, wc_ref[:half], preferred_element_type=jnp.float32)
    table = table[:SUB] + table[SUB:] + jnp.dot(
        high, wc_ref[half:], preferred_element_type=jnp.float32
    )
    feature = fp_ref[...]
    none = jnp.zeros_like(feature)
    table = table[: 2 * blocks] + jnp.concatenate(
        [jnp.where(odd == 0, feature, none), jnp.where(odd == 0, none, feature)], axis=0
    )
    piece = jnp.concatenate([table[:, : E // 2], table[:, E // 2 :]], axis=0).astype(out_ref.dtype)
    out_ref[...] = jnp.broadcast_to(piece[None], out_ref.shape)


def unit(parts):
    mean = sum(jnp.sum(p * p, axis=-1, keepdims=True) for p in parts) * (1.0 / E)
    scale = lax.rsqrt(mean + 1e-06)
    return jnp.concatenate(
        [(p * scale * E ** (-0.5)).astype(jnp.bfloat16) for p in parts], axis=1
    )


def caption_kernel(group, width, mine_ref, *refs):
    *got_refs, captions_ref, masks_ref = refs
    caps = captions_ref.shape[0]
    sums = E // LANES * caps
    blocks = width // 2
    total = mine_ref[...] + sum(ref[...].astype(jnp.float32) for ref in got_refs)
    captions_ref[...] = unit([total[c * caps : (c + 1) * caps] for c in range(E // LANES)])

    def column(side):
        found = jnp.zeros((caps, LANES), jnp.float32)
        at = lax.broadcasted_iota(jnp.int32, (caps, LANES), 0) + side * caps
        lane = lax.broadcasted_iota(jnp.int32, (caps, LANES), 1)
        for r in range(-(-2 * caps // LANES)):
            line = total[sums + r : sums + r + 1]
            found = found + jnp.where(at == lane + r * LANES, line, 0.0)
        return jnp.sum(found, axis=1, keepdims=True)

    lower, upper = column(0), column(1)
    place = lax.broadcasted_iota(jnp.int32, (caps, masks_ref.shape[1]), 1)
    inner = place % width
    pair = masks_ref.shape[1] // (width * group) - 1 - place // (width * group)
    block = (pair * blocks + inner % blocks).astype(jnp.float32)
    inside = jnp.where((block >= lower) & (block < upper), 1.0, 0.0)
    for side in range(2):
        masks_ref[side * caps : (side + 1) * caps] = jnp.where(
            inner // blocks == side, inside, 0.0
        ).astype(jnp.bfloat16)


def tail_kernel(everyone_ref, captions_ref, masks_ref, divisor_ref, derivative_ref, loss_ref):
    own_caps = derivative_ref.shape[0]
    devices, width, half = everyone_ref.shape
    caps = captions_ref.shape[0]
    slot = lax.axis_index("seq") * lax.axis_size("head") + lax.axis_index("head")
    divisor = divisor_ref[0]
    captions = captions_ref[...]
    pieces = everyone_ref[...].reshape(devices * width, half)
    pooled = jnp.dot(masks_ref[...], pieces, preferred_element_type=jnp.float32)
    spans = unit([pooled[:caps], pooled[caps:]])

    logits = transposed_dot(spans, captions) * divisor
    row_total = jnp.log(jnp.sum(jnp.exp(logits), axis=0, keepdims=True))
    tall = -(-own_caps // SUB) * SUB
    row = lax.broadcasted_iota(jnp.int32, (tall, caps), 0)
    marker = jnp.where(
        (row < own_caps) & (lax.broadcasted_iota(jnp.int32, (tall, caps), 1) == slot * own_caps + row),
        1.0,
        0.0,
    )
    own_spans = jnp.dot(
        marker.astype(jnp.bfloat16), spans, preferred_element_type=jnp.float32
    ).astype(jnp.bfloat16)
    own = transposed_dot(own_spans, captions) * divisor
    col_total = jnp.log(jnp.sum(jnp.exp(own), axis=1, keepdims=True))
    loss = 0.5 * (jnp.sum(marker * row_total, axis=1, keepdims=True) + col_total) - jnp.sum(
        marker * own, axis=1, keepdims=True
    )
    flip = lax.broadcasted_iota(jnp.int32, (tall, tall), 0) == lax.broadcasted_iota(
        jnp.int32, (tall, tall), 1
    )
    loss_ref[...] = jnp.sum(jnp.where(flip, loss, 0.0), axis=0, keepdims=True)[:, :own_caps]
    weights = (
        0.5 * jnp.exp(own - row_total) + 0.5 * jnp.exp(own - col_total) - marker
    ).astype(jnp.bfloat16)
    derivative = jnp.dot(weights, captions, preferred_element_type=jnp.float32) * divisor
    derivative_ref[...] = derivative[:own_caps]


def local(
    frames, norm_gain, w_qkv, w_out, w_proj, text_table, token_ids, span_bounds, contrast_divisor
):
    rows, width = frames.shape
    cols = w_qkv.shape[2]
    half = cols // 2
    seq_count, head_count = lax.axis_size("seq"), lax.axis_size("head")
    devices = seq_count * head_count
    own_caps = span_bounds.shape[0]
    blocks = rows // BLK
    shape = jax.ShapeDtypeStruct
    bf16, f32 = jnp.bfloat16, jnp.float32

    tall = E // LANES * token_ids.shape[0] + BOUND_ROWS
    given = (frames, norm_gain[None], w_qkv, token_ids.T, text_table, span_bounds)
    own, p1, p2, p3, mine = call(
        first_kernel,
        [shape((n, half), bf16) for n in (3 * rows, 3 * rows + tall, 2 * rows, 2 * rows)]
        + [shape((tall, LANES), f32)],
        [HBM] * len(given),
        [
            pltpu.SMEM(a.shape, a.dtype) if a is span_bounds else pltpu.VMEM(a.shape, a.dtype)
            for a in given
        ]
        + [pltpu.VMEM(frames.shape, bf16), pltpu.SemaphoreType.DMA((8,))],
        (6 * rows * width * cols, 2 * w_qkv.size, 0),
    )(*[pltpu.with_memory_space_constraint(a, pltpu.HBM) for a in given])
    ends = seq_count - 1
    r1 = lax.ppermute(p1, "seq", [(s, s ^ 1) for s in range(seq_count)])
    r3 = lax.ppermute(
        p3,
        "seq",
        [(s, s + 1) for s in range(1, ends, 2)] + [(s, s - 1) for s in range(2, seq_count, 2)],
    )
    r2 = lax.ppermute(
        p2,
        "seq",
        [(s, s + 2) for s in range(1, ends - 1, 2)] + [(s, s - 2) for s in range(2, seq_count, 2)],
    )

    def swap(sent, seq_step, head_step):
        to = [
            (s ^ seq_step) * head_count + (h ^ head_step)
            for s in range(seq_count)
            for h in range(head_count)
        ]
        return lax.ppermute(sent, EVERY, list(enumerate(to)))

    def add(mine, *got):
        for g in got:
            mine = mine + g.astype(f32)
        return mine, mine.astype(bf16)

    mine, sent = add(mine, r1[3 * rows :])
    mine, sent = add(mine, swap(sent, 0, 1))
    got = swap(sent, 2, 0)

    wc, fp = call(
        weights_kernel,
        [shape((2 * half, E), bf16), shape((blocks, E), f32)],
        [VMEM] * 3,
        cost=(10**10, 2 * (w_proj.size + w_out.size + frames.size), 0),
    )(frames, w_out, w_proj)

    piece = call(
        attend_kernel,
        shape((devices, 4 * blocks, E // 2), PIECE),
        [VMEM] * 6,
        cost=(10**10, 10 * rows * cols, 6 * rows * rows * cols // HDIM),
    )(own, r1, r2, r3, wc, fp)

    got, piece = lax.optimization_barrier((got, piece))
    mine, sent = add(mine, got)
    step = 4
    while step < seq_count:
        mine, sent = add(mine, swap(sent, step, 0))
        step *= 2
    backward = list(range(devices))[::-1]
    everyone = lax.all_to_all(piece, EVERY, 0, 0, axis_index_groups=[backward])
    gots = [swap(sent, 0, k) for k in range(2, head_count, 2)]

    captions, masks = call(
        functools.partial(caption_kernel, 2 * head_count, 4 * blocks),
        [
            shape((token_ids.shape[0], E), bf16),
            shape((2 * token_ids.shape[0], devices * 4 * blocks), bf16),
        ],
        [VMEM] * (1 + len(gots)),
    )(mine, *gots)
    derivative, loss = call(
        tail_kernel,
        [shape((own_caps, E), f32), shape((1, own_caps), f32)],
        [VMEM, VMEM, VMEM, SMEM],
        cost=(4 * E * token_ids.shape[0] ** 2, 2 * piece.size, 0),
    )(everyone, captions, masks, contrast_divisor)
    return derivative, loss.reshape(own_caps)


def solution(mesh):
    placed = (
        P("seq", None),
        P(),
        P(None, None, "head"),
        P("head", None),
        P(),
        P(EVERY, None),
        P(),
        P(EVERY, None),
        P(),
    )
    return jax.shard_map(
        local,
        mesh=mesh,
        in_specs=placed,
        out_specs=(P(EVERY, None), P(EVERY)),
        check_vma=False,
    )
```

```python
import functools

import jax
import jax.numpy as jnp
from jax import lax
from jax.experimental import pallas as pl
from jax.experimental.pallas import tpu as pltpu
from jax.sharding import PartitionSpec as P

HDIM = 64
E = 512
BLK = 128
EVERY = ("seq", "head")
LANES = 128
SUB = 8
NEVER = -1e30
BOUND_ROWS = 16
PIECE = jnp.bfloat16
VMEM = pl.BlockSpec(memory_space=pltpu.VMEM)
SMEM = pl.BlockSpec(memory_space=pltpu.SMEM)
HBM = pl.BlockSpec(memory_space=pltpu.HBM)
HIGHEST = lax.Precision.HIGHEST


def call(body, outs, ins, scratch=(), cost=(0, 0, 0), mib=24):
    return pl.pallas_call(
        body,
        out_shape=outs,
        in_specs=ins,
        out_specs=jax.tree.map(lambda _: VMEM, outs),
        scratch_shapes=scratch,
        compiler_params=pltpu.CompilerParams(vmem_limit_bytes=mib << 20),
        cost_estimate=pl.CostEstimate(
            flops=cost[0], bytes_accessed=cost[1], transcendentals=cost[2]
        ),
    )


def transposed_dot(left, right):
    return lax.dot_general(
        left, right, (((1,), (1,)), ((), ())), preferred_element_type=jnp.float32
    )


def first_kernel(
    frames_hbm,
    gain_hbm,
    w_hbm,
    ids_hbm,
    table_hbm,
    bounds_hbm,
    own_ref,
    p1_ref,
    p2_ref,
    p3_ref,
    t32_ref,
    frames,
    gain,
    w,
    id_rows,
    table,
    bound,
    normed,
    sems,
):
    rows = frames.shape[0]
    half = own_ref.shape[1]
    parts = [(ids_hbm, id_rows), (frames_hbm, frames), (gain_hbm, gain)]
    parts += [(w_hbm.at[k], w.at[k]) for k in (1, 2, 0)]
    parts += [(table_hbm, table), (bounds_hbm, bound)]
    copies = [pltpu.make_async_copy(*part, sems.at[n]) for n, part in enumerate(parts)]
    for n in (0, 1, 2, 3, 4, 6, 5, 7):
        copies[n].start()
    odd = lax.axis_index("seq") % 2 == 1

    tokens, caps = id_rows.shape
    vocab = table.shape[0]
    own_caps = bound.shape[0]
    slot = lax.axis_index("seq") * lax.axis_size("head") + lax.axis_index("head")
    copies[0].wait()
    ids = id_rows[...] - slot * vocab
    ids = jnp.where((ids >= 0) & (ids < vocab), ids, -1).T
    words = lax.broadcasted_iota(jnp.int32, (caps, vocab), 1).astype(jnp.int16)
    counts = jnp.zeros((caps, vocab), jnp.bfloat16)
    one, none = jnp.ones_like(counts), jnp.zeros_like(counts)
    for t in range(tokens):
        column = jnp.broadcast_to(ids[:, t : t + 1], (caps, vocab)).astype(jnp.int16)
        counts = counts + jnp.where(column == words, one, none)

    copies[1].wait()
    copies[2].wait()
    step = min(64, rows)
    for r in range(0, rows, step):
        part = frames[r : r + step].astype(jnp.float32)
        scale = lax.rsqrt(jnp.mean(part * part, axis=-1, keepdims=True) + 1e-05)
        normed[r : r + step] = (part * scale * gain[...]).astype(jnp.bfloat16)
    def project(n, k):
        copies[3 + n].wait()
        both = jnp.dot(normed[...], w[k], preferred_element_type=jnp.float32).astype(jnp.bfloat16)
        if k == 0:
            both = both * jnp.bfloat16(HDIM ** (-0.5))
        mine = jnp.where(odd, both[:, half:], both[:, :half])
        other = jnp.where(odd, both[:, :half], both[:, half:])
        own_ref[k * rows : (k + 1) * rows] = mine
        p1_ref[k * rows : (k + 1) * rows] = other
        if k > 0:
            p2_ref[(k - 1) * rows : k * rows] = mine
            p3_ref[(k - 1) * rows : k * rows] = other

    project(0, 1)
    project(1, 2)
    copies[6].wait()
    copies[7].wait()
    part = jnp.dot(counts, table[...], preferred_element_type=jnp.float32)
    row = lax.broadcasted_iota(jnp.int32, (BOUND_ROWS, LANES), 0)
    place = row * LANES + lax.broadcasted_iota(jnp.int32, (BOUND_ROWS, LANES), 1)
    bounds = jnp.zeros((BOUND_ROWS, LANES), jnp.float32)
    for c in range(own_caps):
        for side in range(2):
            block = (bound[c, side] // BLK).astype(jnp.float32)
            bounds = jnp.where(place == side * caps + slot * own_caps + c, block, bounds)
    sums = E // LANES * caps
    for c in range(E // LANES):
        chunk = part[:, c * LANES : (c + 1) * LANES]
        t32_ref[c * caps : (c + 1) * caps] = chunk
        p1_ref[3 * rows + c * caps : 3 * rows + (c + 1) * caps] = chunk.astype(jnp.bfloat16)
    t32_ref[sums:] = bounds
    p1_ref[3 * rows + sums :] = bounds.astype(jnp.bfloat16)
    project(2, 0)


def weights_kernel(frames_ref, w_out_ref, w_proj_ref, wc_ref, fp_ref):
    half = wc_ref.shape[0] // 2
    cols = w_out_ref.shape[0]
    blocks = fp_ref.shape[0]
    odd = lax.axis_index("seq") % 2
    start = pl.multiple_of(lax.axis_index("head") * cols, LANES)
    product = jnp.dot(
        w_out_ref[pl.ds(pl.multiple_of(odd * half, half), half), :],
        w_proj_ref[...],
        preferred_element_type=jnp.float32,
    )
    high = product.astype(jnp.bfloat16)
    wc_ref[:half] = high
    wc_ref[half:] = (product - high.astype(jnp.float32)).astype(jnp.bfloat16)
    features = frames_ref[:, pl.ds(start, cols)].astype(jnp.float32)
    sums = jnp.sum(features.reshape(blocks, BLK, cols), axis=1)
    padded = jnp.concatenate([sums, jnp.zeros((SUB - blocks, cols), jnp.float32)], axis=0)
    fp_ref[...] = jnp.dot(
        padded, w_proj_ref[pl.ds(start, cols), :].astype(jnp.float32), precision=HIGHEST
    )[:blocks]


def attend_kernel(own_ref, r1_ref, r2_ref, r3_ref, wc_ref, fp_ref, out_ref):
    rows = own_ref.shape[0] // 3
    half = own_ref.shape[1]
    blocks = rows // BLK
    seq, last = lax.axis_index("seq"), lax.axis_size("seq") - 1
    odd = seq % 2
    heads = half // HDIM
    apart = lax.broadcasted_iota(jnp.int32, (rows, rows), 0) - lax.broadcasted_iota(
        jnp.int32, (rows, rows), 1
    )
    lane = lax.broadcasted_iota(jnp.int32, (rows, half), 1)

    def block_sums(me, other, halo, parity, exists):
        side = jnp.concatenate([jnp.where(parity == 0, apart, -apart)] * heads, axis=0)
        near = side >= 0
        far = side <= jnp.where(exists, 0, -2 * rows)
        query = me[0:rows]
        blank = jnp.zeros_like(query)
        q = jnp.concatenate(
            [jnp.where(lane // HDIM == head, query, blank) for head in range(heads)], axis=0
        )
        scores = [
            transposed_dot(q, me[rows : 2 * rows]),
            jnp.where(near, transposed_dot(q, other[rows : 2 * rows]), NEVER),
            jnp.where(far, transposed_dot(q, halo[0:rows]), NEVER),
        ]
        top = jnp.max(functools.reduce(jnp.maximum, scores), axis=1, keepdims=True)
        probs = [jnp.exp(s - top) for s in scores]
        denom = jnp.sum(sum(probs), axis=1, keepdims=True)
        values = (me[2 * rows : 3 * rows], other[2 * rows : 3 * rows], halo[rows : 2 * rows])
        mixed = jnp.dot(
            jnp.concatenate([p.astype(jnp.bfloat16) for p in probs], axis=1),
            jnp.concatenate(values, axis=0),
            preferred_element_type=jnp.float32,
        )
        mixed = mixed * (1.0 / denom)
        attended = mixed[:rows]
        for head in range(1, heads):
            attended = jnp.where(
                lane // HDIM == head, mixed[head * rows : (head + 1) * rows], attended
            )
        attended = attended.astype(jnp.bfloat16).astype(jnp.float32)
        return jnp.sum(attended.reshape(blocks, BLK, half), axis=1)

    here = block_sums(own_ref, r1_ref, r3_ref, odd, jnp.where(odd == 0, seq > 0, seq < last))
    there = block_sums(
        r1_ref, own_ref, r2_ref, 1 - odd, jnp.where(odd == 0, seq + 1 < last, seq > 1)
    )
    first = jnp.where(odd == 0, here, there)
    second = jnp.where(odd == 0, there, here)
    blank = jnp.zeros((SUB - 2 * blocks, half), jnp.float32)
    sums = jnp.concatenate([first, second, blank], axis=0)
    high = sums.astype(jnp.bfloat16)
    low = (sums - high.astype(jnp.float32)).astype(jnp.bfloat16)
    both = jnp.concatenate([high, low], axis=0)
    table = jnp.dot(both, wc_ref[:half], preferred_element_type=jnp.float32)
    table = table[:SUB] + table[SUB:] + jnp.dot(
        high, wc_ref[half:], preferred_element_type=jnp.float32
    )
    feature = fp_ref[...]
    none = jnp.zeros_like(feature)
    table = table[: 2 * blocks] + jnp.concatenate(
        [jnp.where(odd == 0, feature, none), jnp.where(odd == 0, none, feature)], axis=0
    )
    piece = jnp.concatenate([table[:, : E // 2], table[:, E // 2 :]], axis=0).astype(out_ref.dtype)
    out_ref[...] = jnp.broadcast_to(piece[None], out_ref.shape)


def unit(parts):
    mean = sum(jnp.sum(p * p, axis=-1, keepdims=True) for p in parts) * (1.0 / E)
    scale = lax.rsqrt(mean + 1e-06)
    return jnp.concatenate(
        [(p * scale * E ** (-0.5)).astype(jnp.bfloat16) for p in parts], axis=1
    )


def caption_kernel(group, width, mine_ref, *refs):
    *got_refs, captions_ref, masks_ref = refs
    caps = captions_ref.shape[0]
    sums = E // LANES * caps
    blocks = width // 2
    total = mine_ref[...] + sum(ref[...].astype(jnp.float32) for ref in got_refs)
    captions_ref[...] = unit([total[c * caps : (c + 1) * caps] for c in range(E // LANES)])

    def column(side):
        found = jnp.zeros((caps, LANES), jnp.float32)
        at = lax.broadcasted_iota(jnp.int32, (caps, LANES), 0) + side * caps
        lane = lax.broadcasted_iota(jnp.int32, (caps, LANES), 1)
        for r in range(-(-2 * caps // LANES)):
            line = total[sums + r : sums + r + 1]
            found = found + jnp.where(at == lane + r * LANES, line, 0.0)
        return jnp.sum(found, axis=1, keepdims=True)

    lower, upper = column(0), column(1)
    place = lax.broadcasted_iota(jnp.int32, (caps, masks_ref.shape[1]), 1)
    inner = place % width
    pair = masks_ref.shape[1] // (width * group) - 1 - place // (width * group)
    block = (pair * blocks + inner % blocks).astype(jnp.float32)
    inside = jnp.where((block >= lower) & (block < upper), 1.0, 0.0)
    for side in range(2):
        masks_ref[side * caps : (side + 1) * caps] = jnp.where(
            inner // blocks == side, inside, 0.0
        ).astype(jnp.bfloat16)


def tail_kernel(everyone_ref, captions_ref, masks_ref, divisor_ref, derivative_ref, loss_ref):
    own_caps = derivative_ref.shape[0]
    devices, width, half = everyone_ref.shape
    caps = captions_ref.shape[0]
    slot = lax.axis_index("seq") * lax.axis_size("head") + lax.axis_index("head")
    divisor = divisor_ref[0]
    captions = captions_ref[...]
    pieces = everyone_ref[...].reshape(devices * width, half)
    pooled = jnp.dot(masks_ref[...], pieces, preferred_element_type=jnp.float32)
    spans = unit([pooled[:caps], pooled[caps:]])

    logits = transposed_dot(spans, captions) * divisor
    row_total = jnp.log(jnp.sum(jnp.exp(logits), axis=0, keepdims=True))
    tall = -(-own_caps // SUB) * SUB
    row = lax.broadcasted_iota(jnp.int32, (tall, caps), 0)
    marker = jnp.where(
        (row < own_caps) & (lax.broadcasted_iota(jnp.int32, (tall, caps), 1) == slot * own_caps + row),
        1.0,
        0.0,
    )
    own_spans = jnp.dot(
        marker.astype(jnp.bfloat16), spans, preferred_element_type=jnp.float32
    ).astype(jnp.bfloat16)
    own = transposed_dot(own_spans, captions) * divisor
    col_total = jnp.log(jnp.sum(jnp.exp(own), axis=1, keepdims=True))
    loss = 0.5 * (jnp.sum(marker * row_total, axis=1, keepdims=True) + col_total) - jnp.sum(
        marker * own, axis=1, keepdims=True
    )
    flip = lax.broadcasted_iota(jnp.int32, (tall, tall), 0) == lax.broadcasted_iota(
        jnp.int32, (tall, tall), 1
    )
    loss_ref[...] = jnp.sum(jnp.where(flip, loss, 0.0), axis=0, keepdims=True)[:, :own_caps]
    weights = (
        0.5 * jnp.exp(own - row_total) + 0.5 * jnp.exp(own - col_total) - marker
    ).astype(jnp.bfloat16)
    derivative = jnp.dot(weights, captions, preferred_element_type=jnp.float32) * divisor
    derivative_ref[...] = derivative[:own_caps]


def local(
    frames, norm_gain, w_qkv, w_out, w_proj, text_table, token_ids, span_bounds, contrast_divisor
):
    rows, width = frames.shape
    cols = w_qkv.shape[2]
    half = cols // 2
    seq_count, head_count = lax.axis_size("seq"), lax.axis_size("head")
    devices = seq_count * head_count
    own_caps = span_bounds.shape[0]
    blocks = rows // BLK
    shape = jax.ShapeDtypeStruct
    bf16, f32 = jnp.bfloat16, jnp.float32

    tall = E // LANES * token_ids.shape[0] + BOUND_ROWS
    given = (frames, norm_gain[None], w_qkv, token_ids.T, text_table, span_bounds)
    own, p1, p2, p3, mine = call(
        first_kernel,
        [shape((n, half), bf16) for n in (3 * rows, 3 * rows + tall, 2 * rows, 2 * rows)]
        + [shape((tall, LANES), f32)],
        [HBM] * len(given),
        [
            pltpu.SMEM(a.shape, a.dtype) if a is span_bounds else pltpu.VMEM(a.shape, a.dtype)
            for a in given
        ]
        + [pltpu.VMEM(frames.shape, bf16), pltpu.SemaphoreType.DMA((8,))],
        (6 * rows * width * cols, 2 * w_qkv.size, 0),
    )(*[pltpu.with_memory_space_constraint(a, pltpu.HBM) for a in given])
    ends = seq_count - 1
    r1 = lax.ppermute(p1, "seq", [(s, s ^ 1) for s in range(seq_count)])
    r3 = lax.ppermute(
        p3,
        "seq",
        [(s, s + 1) for s in range(1, ends, 2)] + [(s, s - 1) for s in range(2, seq_count, 2)],
    )
    r2 = lax.ppermute(
        p2,
        "seq",
        [(s, s + 2) for s in range(1, ends - 1, 2)] + [(s, s - 2) for s in range(2, seq_count, 2)],
    )

    def swap(sent, seq_step, head_step):
        to = [
            (s ^ seq_step) * head_count + (h ^ head_step)
            for s in range(seq_count)
            for h in range(head_count)
        ]
        return lax.ppermute(sent, EVERY, list(enumerate(to)))

    def add(mine, *got):
        for g in got:
            mine = mine + g.astype(f32)
        return mine, mine.astype(bf16)

    mine, sent = add(mine, r1[3 * rows :])
    mine, sent = add(mine, swap(sent, 0, 1))
    got = swap(sent, 2, 0)

    wc, fp = call(
        weights_kernel,
        [shape((2 * half, E), bf16), shape((blocks, E), f32)],
        [VMEM] * 3,
        cost=(10**10, 2 * (w_proj.size + w_out.size + frames.size), 0),
    )(frames, w_out, w_proj)

    piece = call(
        attend_kernel,
        shape((devices, 4 * blocks, E // 2), PIECE),
        [VMEM] * 6,
        cost=(10**10, 10 * rows * cols, 6 * rows * rows * cols // HDIM),
    )(own, r1, r2, r3, wc, fp)

    got, piece = lax.optimization_barrier((got, piece))
    mine, sent = add(mine, got)
    step = 4
    while step < seq_count:
        mine, sent = add(mine, swap(sent, step, 0))
        step *= 2
    backward = list(range(devices))[::-1]
    everyone = lax.all_to_all(piece, EVERY, 0, 0, axis_index_groups=[backward])
    gots = [swap(sent, 0, k) for k in range(2, head_count, 2)]

    captions, masks = call(
        functools.partial(caption_kernel, 2 * head_count, 4 * blocks),
        [
            shape((token_ids.shape[0], E), bf16),
            shape((2 * token_ids.shape[0], devices * 4 * blocks), bf16),
        ],
        [VMEM] * (1 + len(gots)),
    )(mine, *gots)
    derivative, loss = call(
        tail_kernel,
        [shape((own_caps, E), f32), shape((1, own_caps), f32)],
        [VMEM, VMEM, VMEM, SMEM],
        cost=(4 * E * token_ids.shape[0] ** 2, 2 * piece.size, 0),
    )(everyone, captions, masks, contrast_divisor)
    return derivative, loss.reshape(own_caps)


def solution(mesh):
    placed = (
        P("seq", None),
        P(),
        P(None, None, "head"),
        P("head", None),
        P(),
        P(EVERY, None),
        P(),
        P(EVERY, None),
        P(),
    )
    return jax.shard_map(
        local,
        mesh=mesh,
        in_specs=placed,
        out_specs=(P(EVERY, None), P(EVERY)),
        check_vma=False,
    )
```
